128 devices in a mesh: seq: 32 (over y, x, core), head: 4 (over z).
Axes of the slice: x: 4, y: 4, z: 4, core: 2. Of those that a mesh axis runs over, the one named last changes fastest.
Arguments:
- tokens: bfloat16 [4096, 1536], P('seq'), may hold values from -6 to 6
- cotangent: bfloat16 [4096, 1536], P('seq'), may hold values from -6 to 6
- norm_first: float32 [1536], replicated, may hold values from 0.5 to 1.5
- in_inner: bfloat16 [1536, 3072], P(None, 'head'), may hold values from -0.15625 to 0.15625
- in_gate: bfloat16 [1536, 3072], P(None, 'head'), may hold values from -0.15625 to 0.15625
- conv_weight: float32 [4, 3072], P(None, 'head'), may hold values from -3 to 3
- conv_bias: float32 [3072], P('head'), may hold values from -0.5 to 0.5
- projector: bfloat16 [3072, 128], P('head'), may hold values from -0.109375 to 0.109375
- projector_gains: float32 [128], replicated, may hold values from 0.5 to 1.5
- step_weight: bfloat16 [96, 3072], P(None, 'head'), may hold values from -0.625 to 0.625
- step_bias: float32 [3072], P('head'), may hold values from -1.5 to 0
- log_rates: float32 [3072, 16], P('head'), may hold values from -16 to -2, as said below
- skip_gain: float32 [3072], P('head'), may hold values from 17 to 66
- out_weight: bfloat16 [3072, 1536], P('head'), may hold values from -0.0048828125 to 0.0048828125
- norm_second: float32 [1536], replicated, may hold values from 0.5 to 1.5
- gate_weight: bfloat16 [1536, 4096], P(None, 'head'), may hold values from -0.15625 to 0.15625
- up_weight: bfloat16 [1536, 4096], P(None, 'head'), may hold values from -0.15625 to 0.15625
- down_weight: bfloat16 [4096, 1536], P('head'), may hold values from -0.09375 to 0.09375
Outputs:
- output: bfloat16 [4096, 1536], P('seq')
- grad_tokens: bfloat16 [4096, 1536], P('seq')
- grad_norm_first: float32 [1536], P('seq')
- grad_in_inner: float32 [1536, 3072], P('seq', 'head')
- grad_in_gate: float32 [1536, 3072], P('seq', 'head')
- grad_conv_weight: float32 [4, 3072], P(None, ('head', 'seq'))
- grad_conv_bias: float32 [3072], P(('head', 'seq'))
- grad_projector: float32 [3072, 128], P('head', 'seq')
- grad_projector_gains: float32 [128], P('seq')
- grad_step_weight: float32 [96, 3072], P(None, ('head', 'seq'))
- grad_step_bias: float32 [3072], P(('head', 'seq'))
- grad_log_rates: float32 [3072, 16], P(('head', 'seq'))
- grad_skip_gain: float32 [3072], P(('head', 'seq'))
- grad_out_weight: float32 [3072, 1536], P('head', 'seq')
- grad_norm_second: float32 [1536], P('seq')
- grad_gate_weight: float32 [1536, 4096], P('seq', 'head')
- grad_up_weight: float32 [1536, 4096], P('seq', 'head')
- grad_down_weight: float32 [4096, 1536], P('head', 'seq')
The draws below stay inside these ranges and needn't reach their ends.
Inputs may be any that keep to these rules, and one draw needn't show every extreme that they name: `log_rates`: logarithms of per-step decay rates.
All inputs are finite; a program needn't handle non-finite values.
Results may differ from the reference program's by a relative error of at most 0.0239.
Values may be sent and summed in bfloat16 or wider, within the bound.
A program may use at most 256 MiB of HBM per device.

```python
import math
import jax
import jax.numpy as jnp
from jax import lax

D = 1536
DI = 3072
STATE = 16
CONV = 4
RANK = 96
FF = 4096
SEQS = 2
LEN_DEV = 128
LEN = 4096
SEQ_LEN = 2048
N_SEQ = 32


def draw_log_rates(key, part):
    key = jax.random.fold_in(key, 7)
    pick_key, level_key = jax.random.split(key)
    fraction = 0.5
    chooser = jax.random.uniform(pick_key, (DI, STATE), jnp.float32)
    levels = jax.random.uniform(level_key, (DI, STATE), jnp.float32)
    slow_low = math.log(0.1 / SEQ_LEN)
    slow_high = math.log(1.5 / SEQ_LEN)
    fast_low = math.log(0.02)
    fast_high = math.log(0.06)
    slow_rates = slow_low + levels * (slow_high - slow_low)
    fast_rates = fast_low + levels * (fast_high - fast_low)
    return jnp.where(chooser < fraction, slow_rates, fast_rates).astype(jnp.float32)


def steps_of(stream_key, dims, cuts, least, high):
    level, own = 1.0, jax.random.fold_in(stream_key, 6)
    for axis_at, shards_of in cuts:
        draws = jnp.exp(jax.random.uniform(jax.random.fold_in(own, axis_at), (shards_of,), jnp.float32, least / len(cuts), high / len(cuts)))
        level = level * jnp.repeat(draws, dims[axis_at] // shards_of).reshape([-1 if axis == axis_at else 1 for axis in range(len(dims))])
    return level


def bell_draw(stream_key, dims, width, bound, cuts=(), held_as=jnp.bfloat16):
    entries = width * jax.random.normal(stream_key, dims, jnp.float32)
    if cuts:
        entries = entries * steps_of(stream_key, dims, cuts, -0.22, 0.18)
    return jnp.clip(entries, -bound, bound).astype(held_as)


def setup_inputs(seed: int = 0) -> dict:
    streams_of = jax.random.split(jax.random.key(seed), 19)
    tokens = bell_draw(streams_of[0], (LEN, D), 1.0, 6.0, ((0, 32),))
    cotangent = bell_draw(streams_of[1], (LEN, D), 1.0, 6.0, ((0, 32),))
    norm_first = jnp.clip(1.0 + 0.1 * jax.random.normal(streams_of[2], (D,), jnp.float32), 0.5, 1.5)
    in_inner = bell_draw(streams_of[3], (D, DI), D ** -0.5, 0.15625, ((1, 4),))
    in_gate = bell_draw(streams_of[4], (D, DI), D ** -0.5, 0.15625, ((1, 4),))
    conv_weight = bell_draw(streams_of[5], (CONV, DI), CONV ** -0.5, 3.0, ((1, 4),), jnp.float32)
    conv_bias = jnp.clip(jax.random.uniform(streams_of[6], (DI,), jnp.float32, -0.5, 0.5) * steps_of(streams_of[6], (DI,), ((0, 4),), -0.4, 0.0), -0.5, 0.5)
    projector = bell_draw(streams_of[7], (DI, RANK + 2 * STATE), DI ** -0.5, 0.109375, ((0, 4),))
    projector_gains = jnp.clip(1.0 + 0.1 * jax.random.normal(streams_of[8], (RANK + 2 * STATE,), jnp.float32), 0.5, 1.5)
    step_weight = bell_draw(streams_of[9], (RANK, DI), RANK ** -0.5, 0.625, ((1, 4),))
    step_bias = jnp.clip(-1.5 + 1.5 * jax.random.uniform(streams_of[10], (DI,), jnp.float32) ** steps_of(streams_of[10], (DI,), ((0, 4),), -0.2, 0.2), -1.5, 0.0)
    log_rates = draw_log_rates(jax.random.fold_in(streams_of[18], 71), 0)
    skip_gain = jnp.clip(17.0 + 49.0 * jax.random.uniform(streams_of[12], (DI,), jnp.float32) ** steps_of(streams_of[12], (DI,), ((0, 4),), -0.2, 0.2), 17.0, 66.0)
    out_weight = bell_draw(streams_of[13], (DI, D), (DI * SEQ_LEN // 4) ** -0.5, 0.0048828125, ((0, 4),))
    norm_second = jnp.clip(1.0 + 0.1 * jax.random.normal(streams_of[14], (D,), jnp.float32), 0.5, 1.5)
    gate_weight = bell_draw(streams_of[15], (D, FF), D ** -0.5, 0.15625, ((1, 4),))
    up_weight = bell_draw(streams_of[16], (D, FF), D ** -0.5, 0.15625, ((1, 4),))
    down_weight = bell_draw(streams_of[17], (FF, D), FF ** -0.5, 0.09375, ((0, 4),))
    return dict(tokens=tokens, cotangent=cotangent, norm_first=norm_first, in_inner=in_inner, in_gate=in_gate, conv_weight=conv_weight, conv_bias=conv_bias, projector=projector, projector_gains=projector_gains, step_weight=step_weight, step_bias=step_bias, log_rates=log_rates, skip_gain=skip_gain, out_weight=out_weight, norm_second=norm_second, gate_weight=gate_weight, up_weight=up_weight, down_weight=down_weight)


@jax.custom_vjp
def low(v):
    return lax.optimization_barrier(v.astype(jnp.bfloat16)).astype(jnp.float32)

@jax.custom_vjp
def low_back(v):
    return v

def low_keep(v):
    return (low(v), None)

def low_pass(kept, grad):
    return (grad,)

def back_keep(v):
    return (v, None)

def back_low(kept, grad):
    return (low(grad),)
low.defvjp(low_keep, low_pass)
low_back.defvjp(back_keep, back_low)
eps_norm = 1e-05

def product(left, right):
    return jnp.dot(left, right, precision=lax.Precision.HIGHEST, preferred_element_type=jnp.float32)

def rms_scale(values, gain):
    return values * lax.rsqrt(lax.optimization_barrier(jnp.mean(values * values, axis=-1, keepdims=True)) + eps_norm) * gain

def chain_join(earlier, later):
    return (earlier[0] * later[0], later[0] * earlier[1] + later[1])

def forward(resid, norm_first, in_inner, in_gate, conv_weight, conv_bias, projector, projector_gains, step_weight, step_bias, log_rates, skip_gain, out_weight, norm_second, gate_weight, up_weight, down_weight):
    normed = low(rms_scale(resid, norm_first))
    inner_pre = low(low_back(product(normed, in_inner)))
    gate_in = low_back(product(normed, in_gate))
    per_sequence = inner_pre.reshape(SEQS, SEQ_LEN, DI)
    padded = jnp.concatenate([jnp.zeros((SEQS, CONV - 1, DI), jnp.float32), per_sequence], axis=1)
    conv_sum = conv_bias[None, None, :] + conv_weight[0] * padded[:, 0:SEQ_LEN]
    for offset in range(1, CONV):
        conv_sum = conv_sum + conv_weight[offset] * padded[:, offset:offset + SEQ_LEN]
    inner_act = low(jax.nn.silu(conv_sum.reshape(LEN, DI)))
    projected = low_back(product(inner_act, projector))
    step_norm = low(rms_scale(projected[:, :RANK], projector_gains[:RANK]))
    entry_norm = rms_scale(projected[:, RANK:RANK + STATE], projector_gains[RANK:RANK + STATE])
    read_norm = rms_scale(projected[:, RANK + STATE:], projector_gains[RANK + STATE:])
    step_raw = low_back(product(step_norm, step_weight))
    step_size = jax.nn.softplus(step_raw + step_bias)
    neg_rate = -jnp.exp(log_rates)
    group = N_SEQ // SEQS

    def block_step(running, pieces):
        block_index, sizes_here, inner_here, entry_here, read_here = pieces
        running = jnp.where(block_index % group == 0, jnp.zeros_like(running), running)
        decays = jnp.exp(sizes_here[:, :, None] * neg_rate[None])
        inject = (sizes_here * inner_here)[:, :, None] * entry_here[:, None, :]
        cumulative, local_sums = lax.associative_scan(chain_join, (decays, inject), axis=0)
        states = local_sums + cumulative * running[None]
        return (states[-1], lax.optimization_barrier(jnp.sum(states * read_here[:, None, :], axis=2)))
    shaped = (jnp.arange(N_SEQ, dtype=jnp.int32), step_size.reshape(N_SEQ, LEN_DEV, DI), inner_act.reshape(N_SEQ, LEN_DEV, DI), entry_norm.reshape(N_SEQ, LEN_DEV, STATE), read_norm.reshape(N_SEQ, LEN_DEV, STATE))
    _, block_outs = lax.scan(jax.checkpoint(block_step), jnp.zeros((DI, STATE), jnp.float32), shaped)
    scan_out = block_outs.reshape(LEN, DI) + skip_gain * inner_act
    mixed = low(scan_out * jax.nn.silu(gate_in))
    mixer_out = low_back(product(mixed, out_weight))
    middle = resid + mixer_out
    normed_two = low(rms_scale(middle, norm_second))
    gate_pre = low_back(product(normed_two, gate_weight))
    up_pre = low_back(product(normed_two, up_weight))
    activation = low(jax.nn.silu(gate_pre) * up_pre)
    return middle + product(activation, down_weight)

def reference(tokens, cotangent, norm_first, in_inner, in_gate, conv_weight, conv_bias, projector, projector_gains, step_weight, step_bias, log_rates, skip_gain, out_weight, norm_second, gate_weight, up_weight, down_weight):
    floats = [tensor.astype(jnp.float32) for tensor in (tokens, norm_first, in_inner, in_gate, conv_weight, conv_bias, projector, projector_gains, step_weight, step_bias, log_rates, skip_gain, out_weight, norm_second, gate_weight, up_weight, down_weight)]
    result, pullback = jax.vjp(forward, *floats)
    grads = pullback(cotangent.astype(jnp.float32))
    return (result.astype(jnp.bfloat16), grads[0].astype(jnp.bfloat16), grads[1], grads[2], grads[3], grads[4], grads[5], grads[6], grads[7], grads[8], grads[9], grads[10], grads[11], grads[12], grads[13], grads[14], grads[15], grads[16])
```

```python
import types

import jax
import jax.numpy as jnp
from jax import lax
from jax.experimental import pallas as pl
from jax.experimental.pallas import tpu as pltpu
from jax.sharding import PartitionSpec as P

F32 = jnp.float32
BF16 = jnp.bfloat16
T, D, C, F, N, R = 128, 1536, 768, 1024, 16, 96
GROUP = 16
EPS = 1e-5
LOG2E = 1.4426950408889634
HIGH = lax.Precision.HIGHEST
MESH = pl.DeviceIdType.MESH
SMALL = 56
W = 384


def dot(a, b, precision=None):
    return jnp.dot(a, b, precision=precision, preferred_element_type=F32)


def dot_nt(a, b, precision=None):
    return lax.dot_general(a, b, (((1,), (1,)), ((), ())), precision=precision, preferred_element_type=F32)


def tiles(total, width):
    return [slice(i, i + width) for i in range(0, total, width)]


def wide(v):
    return jnp.concatenate([v] * (W // 128), axis=1)


def rcopy(src, dst, sems, i, device):
    return pltpu.make_async_remote_copy(
        src_ref=src, dst_ref=dst, send_sem=sems.at[(0, *i)], recv_sem=sems.at[(1, *i)], device_id=device, device_id_type=MESH
    )


def start(copies):
    for c in copies:
        c.start()
    return copies


def finish(copies):
    for c in copies:
        c.wait()


class Ring:
    def __init__(self, part, land, sems, me, at):
        right, left, far = lax.rem(me + 1, 4), lax.rem(me + 3, 4), lax.rem(me + 2, 4)
        self.part, self.land, self.me, self.right, self.left = part, land, me, right, left

        def send(i, d, h, to):
            return rcopy(part(d, h), land(i, h), sems, (i,), at(to))

        self.first = [send(0, far, 0, right), send(1, far, 1, left)]
        self.direct = [send(2, right, 1, right), send(3, left, 0, left)]
        self.second = [send(4, right, 0, right), send(5, left, 1, left)]

    def begin(self):
        start(self.first)
        start(self.direct)

    def pass_on(self):
        for i, (d, h) in enumerate(((self.right, 0), (self.left, 1))):
            self.first[i].wait()
            own = self.part(d, h)
            own[...] = (own[...].astype(F32) + self.land(i, h)[...].astype(F32)).astype(own.dtype)
            self.second[i].start()

    def total(self, h):
        a, b = (4, 3) if h == 0 else (5, 2)
        return self.part(self.me, h)[...].astype(F32) + (self.land(a, h)[...].astype(F32) + self.land(b, h)[...].astype(F32))

    def arrive(self):
        finish(self.direct)
        finish(self.second)


class Unit:
    def __init__(self, grid, land_one, land_two, sems_one, sems_two, x, y, at, x_first, split):
        self.grid = grid

        def chunk(d, h):
            half = slice(2 * h, 2 * h + 2)
            return grid.at[half, d] if x_first else grid.at[d, half]

        def piece(d, h):
            return split(grid.at[d, x] if x_first else grid.at[y, d], h)

        along_x, along_y = (x, lambda d: at(d, y)), (y, lambda d: at(x, d))
        one, two = (along_x, along_y) if x_first else (along_y, along_x)
        self.one = Ring(chunk, lambda i, h: land_one.at[i], sems_one, *one)
        self.two = Ring(piece, lambda i, h: split(land_two.at[i], h), sems_two, *two)

    def a0(self):
        self.one.begin()

    def a1(self):
        self.one.pass_on()

    def a2(self):
        one = self.one
        one.arrive()
        for h in range(2):
            own = one.part(one.me, h)
            own[...] = one.total(h).astype(own.dtype)
        self.two.begin()

    def b1(self):
        self.two.pass_on()

    def b2(self, store):
        self.two.arrive()
        for h in range(2):
            store(h, self.two.total(h))


def kernel(*refs):
    r = types.SimpleNamespace(**dict(zip([*INS, *OUTS, *SCRATCH], refs, strict=True)))
    s = lax.axis_index("seq")
    z = lax.axis_index("head")
    p = lax.rem(s, GROUP)
    base = s - p
    core = lax.rem(s, 2)
    x = lax.rem(s // 2, 4)
    y = s // 8

    def zdev(k):
        return (s, lax.rem(z + k, 4))

    def gdev(k):
        return (base + lax.rem(p + k, GROUP), z)

    def chip(cx, cy):
        return (cy * 8 + cx * 2 + core, z)

    sibling = (s + 1 - 2 * core, z)
    barrier = pltpu.get_barrier_semaphore()
    for k in range(1, 4):
        pl.semaphore_signal(barrier, 1, device_id=zdev(k), device_id_type=MESH)

    def greet(k, c):
        pl.semaphore_signal(barrier, 1, device_id=gdev(k), device_id_type=MESH)
        return c

    lax.fori_loop(1, GROUP, greet, 0)
    pl.semaphore_signal(barrier, 1, device_id=(s + 8 * (3 - 2 * y), z), device_id_type=MESH)

    def load(i, src, dst):
        c = pltpu.make_async_copy(src, dst, r.load_sem.at[i])
        c.start()
        return c

    ld_tok = load(0, r.in_tok, r.tok)
    ld_in = load(1, r.in_w_in, r.w_in)
    ld_gate = load(2, r.in_w_gate, r.w_gate)
    ld_cot = load(3, r.in_cot, r.cot)
    ld_fd = load(4, r.in_w_fd, r.w_fd)
    ld_proj = load(5, r.in_w_proj, r.w_proj)
    r.w_step[...] = jnp.zeros((T, C), BF16)
    ld_step = load(6, r.in_w_step, r.w_step.at[0:R])
    ld_out = load(7, r.in_w_out, r.w_out)
    ld_fg = load(8, r.in_w_fg, r.w_fg)
    ld_fu = load(9, r.in_w_fu, r.w_fu)

    vec = r.in_vec
    eye = (lax.broadcasted_iota(jnp.int32, (N, N), 0) == lax.broadcasted_iota(jnp.int32, (N, N), 1)).astype(F32)
    nr = -jnp.exp(dot_nt(eye, r.in_rates[...], HIGH))
    r.nr[...] = nr
    nr2 = nr * LOG2E
    r.nr2[...] = nr2
    r.cs_src[...] = jnp.zeros((N, 16, 128), F32)
    r.rc_src[...] = jnp.zeros((N, 8, 128), F32)
    r.nr3[...] = jnp.zeros((N, 8, 128), F32)
    for j in range(6):
        r.nr3[:, j, :] = nr2[:, 128 * j : 128 * j + 128]

    ld_tok.wait()
    g1 = r.in_norms[0:1, :]
    for rows in tiles(T, 32):
        v = r.tok[rows, :].astype(F32)
        rs = lax.rsqrt(jnp.mean(v * v, axis=-1, keepdims=True) + EPS)
        r.rinv[rows, :] = jnp.broadcast_to(rs, (32, 128))
        r.normed[rows, :] = (v * rs * g1).astype(BF16)
    ld_in.wait()
    nrm = r.normed[...]
    for c in tiles(C, 256):
        r.ext[8 : 8 + T, c] = dot(nrm, r.w_in[:, c]).astype(BF16).astype(F32)
    pl.semaphore_wait(barrier, 3 + 15 + 1)
    halo = start([rcopy(r.ext.at[T : T + 8], r.halo, r.halo_sem, (0,), gdev(1))])
    ld_gate.wait()
    for c in tiles(C, 256):
        r.gate_in[:, c] = dot(nrm, r.w_gate[:, c])
    finish(halo)
    r.ext[0:8, :] = jnp.where(p == 0, 0.0, r.halo[...])
    for c in tiles(C, 128):
        tot = vec[4:5, c] + vec[0:1, c] * r.ext[5 : 5 + T, c]
        for k in range(1, 4):
            tot = tot + vec[k : k + 1, c] * r.ext[5 + k : 5 + k + T, c]
        r.conv_sum[:, c] = tot
        r.inner[:, c] = (tot * jax.nn.sigmoid(tot)).astype(BF16)

    def zsum(buf, sems):
        copies = start([rcopy(buf.at[z], buf.at[z], sems, (k,), zdev(k)) for k in range(1, 4)])

        def result():
            finish(copies)
            return (buf[0] + buf[1]) + (buf[2] + buf[3])

        return result

    ld_proj.wait()
    r.pz[z] = dot(r.inner[...], r.w_proj[...])
    projected = zsum(r.pz, r.pz_sem)

    ld_cot.wait()
    ld_fd.wait()
    cot = r.cot[...]
    for c in tiles(F, 256):
        r.gact[:, c] = dot_nt(cot, r.w_fd[c, :])

    def turned(value, at, lhs, i):
        at[...] = value.T.reshape(16, 2, 48, T)
        lhs[:, :, 0:T] = at[:, core]
        return start([rcopy(at.at[:, 1 - core], lhs.at[:, :, T : 2 * T], r.turn_sem, (i,), sibling)])

    def both(b, i):
        return start([rcopy(b.at[0:T], b.at[T : 2 * T], r.both_sem, (i,), sibling)])

    tn_cot = turned(cot, r.at_cot, r.l_cot, 0)
    tn_nrm = turned(nrm, r.at_nrm, r.l_nrm, 1)

    proj = projected()
    r.proj[...] = proj
    lane = lax.broadcasted_iota(jnp.int32, (1, 128), 1)
    m1 = (lane < R).astype(F32)
    m3 = (lane >= R + N).astype(F32)
    m2 = 1.0 - m1 - m3

    def by_part(v):
        return (
            m1 * (jnp.sum(v * m1, -1, keepdims=True) / R)
            + m2 * (jnp.sum(v * m2, -1, keepdims=True) / N)
            + m3 * (jnp.sum(v * m3, -1, keepdims=True) / N)
        )

    rr = lax.rsqrt(by_part(proj * proj) + EPS)
    r.proj_r[...] = rr
    pn = proj * rr * r.in_gains[...]
    r.pn[...] = pn
    step_in = (pn * m1).astype(BF16)
    r.step_in[...] = step_in
    ld_step.wait()
    for c in tiles(C, 256):
        raw = dot(step_in, r.w_step[:, c]) + vec[5:6, c]
        r.raw[:, c] = raw
        st = jnp.maximum(raw, 0.0) + jnp.log1p(jnp.exp(-jnp.abs(raw)))
        r.step[:, c] = st
        r.u[:, c] = st * r.inner[:, c].astype(F32)
    rown = lax.broadcasted_iota(jnp.int32, (N, 128), 0)
    lanes = lax.broadcasted_iota(jnp.int32, (N, 128), 1)
    selb = (lanes == rown + R).astype(F32)
    selc = (lanes == rown + R + N).astype(F32)

    def spread(b, carry):
        rows = r.pn[pl.ds(b * 8, 8), :]
        for i in range(8):
            one = jnp.broadcast_to(rows[i : i + 1, :], (N, 128))
            r.Bb[b * 8 + i] = jnp.broadcast_to(jnp.sum(one * selb, -1, keepdims=True), (N, 128))
            r.Cb[b * 8 + i] = jnp.broadcast_to(jnp.sum(one * selc, -1, keepdims=True), (N, 128))
        return carry

    lax.fori_loop(0, T // 8, spread, 0)

    for c in tiles(C, W):
        a2 = r.nr2[:, c]

        def first(b, h):
            st = r.step[pl.ds(b * 8, 8), c]
            uu = r.u[pl.ds(b * 8, 8), c]
            for i in range(8):
                h = jnp.exp2(a2 * st[i : i + 1, :]) * h + uu[i : i + 1, :] * wide(r.Bb[b * 8 + i])
            return h

        h = lax.fori_loop(0, T // 8, first, jnp.zeros((N, W), F32))
        tot = jnp.sum(r.step[:, c], axis=0, keepdims=True)
        for j, cj in enumerate(tiles(W, 128)):
            r.cs_src[:, c.start // 128 + j, :] = h[:, cj]
            r.cs_src[:, 8 + c.start // 128 + j, :] = jnp.broadcast_to(tot[:, cj], (N, 128))

    def each(fn):
        def body(k, carry):
            fn(k)
            return carry

        lax.fori_loop(1, GROUP, body, 0)

    def swap(src, dst, sems):
        def one(k):
            q = lax.rem(p + k, GROUP)
            return rcopy(src.at[q], dst.at[p], sems, (k,), (base + q, z))

        each(lambda k: one(k).start())
        dst[p] = src[p]
        return lambda: each(lambda k: one(k).wait())

    swapped = swap(r.cs_src, r.cs_recv, r.cs_sem)
    finish(tn_cot)
    finish(tn_nrm)
    swapped()
    mine = r.nr3[p]

    def carry_one(j, state):
        r.so[j] = state
        return jnp.exp2(mine * r.cs_recv[j, 8:16, :]) * state + r.cs_recv[j, 0:8, :]

    lax.fori_loop(0, GROUP, carry_one, jnp.zeros((8, 128), F32))
    swap(r.so, r.si, r.so_sem)()
    for j in range(6):
        r.H[0, :, 128 * j : 128 * j + 128] = r.si[:, j, :]

    for c in tiles(C, W):
        a2 = r.nr2[:, c]

        def second(b, h):
            st = r.step[pl.ds(b * 8, 8), c]
            uu = r.u[pl.ds(b * 8, 8), c]
            rows = []
            for i in range(8):
                h = jnp.exp2(a2 * st[i : i + 1, :]) * h + uu[i : i + 1, :] * wide(r.Bb[b * 8 + i])
                r.H[b * 8 + i + 1, :, c] = h
                rows.append(jnp.sum(h * wide(r.Cb[b * 8 + i]), axis=0, keepdims=True))
            r.scan_out[pl.ds(b * 8, 8), c] = jnp.concatenate(rows, axis=0)
            return h

        lax.fori_loop(0, T // 8, second, r.H[0, :, c])

    for c in tiles(C, 128):
        so = r.scan_out[:, c] + vec[6:7, c] * r.inner[:, c].astype(F32)
        r.scan_out[:, c] = so
        gi = r.gate_in[:, c]
        r.b_out[0:T, c] = (so * (gi * jax.nn.sigmoid(gi))).astype(BF16)
    by_out = both(r.b_out, 0)

    def zscatter(src, dst, sems, j):
        c = slice(512 * j, 512 * j + 512)
        return start([rcopy(src.at[lax.rem(z + k, 4), :, c], dst.at[k - 1, :, c], sems, (j, k), zdev(k)) for k in range(1, 4)])

    def zsummed(src, dst, copies):
        finish(copies)
        return (src[z].astype(F32) + dst[0].astype(F32)) + (dst[1].astype(F32) + dst[2].astype(F32))

    def zgather(buf, sems):
        return start([rcopy(buf.at[z], buf.at[z], sems, (k,), zdev(k)) for k in range(1, 4)])

    def fours(v):
        return v.astype(BF16).reshape(4, 32, v.shape[-1])

    ld_out.wait()
    mixed = r.b_out[0:T, :]
    sent = []
    for j, c in enumerate(tiles(D, 512)):
        r.rs1_src[:, :, c] = fours(dot(mixed, r.w_out[:, c]))
        sent += zscatter(r.rs1_src, r.rs1_dst, r.rs1_sem, j)
    own = pl.ds(pl.multiple_of(z * 32, 32), 32)
    middle = r.tok[own, :].astype(F32) + zsummed(r.rs1_src, r.rs1_dst, sent)
    r.middle[...] = middle
    r2 = lax.rsqrt(jnp.mean(middle * middle, axis=-1, keepdims=True) + EPS)
    g2 = r.in_norms[1:2, :]
    r.n2[z] = (middle * r2 * g2).astype(BF16)
    finish(zgather(r.n2, r.n2_sem))

    n2 = r.n2[...].reshape(T, D)
    ld_fg.wait()
    ld_fu.wait()
    for c in tiles(F, 256):
        g = dot(n2, r.w_fg[:, c])
        u = dot(n2, r.w_fu[:, c])
        ga = r.gact[:, c]
        sg = jax.nn.sigmoid(g)
        sl = g * sg
        r.b_act[0:T, c] = (sl * u).astype(BF16)
        r.b_gg[0:T, c] = (ga * u * (sg * (1.0 + g * (1.0 - sg)))).astype(BF16)
        r.b_gu[0:T, c] = (ga * sl).astype(BF16)
    by_act = both(r.b_act, 1)
    by_gg = both(r.b_gg, 2)
    by_gu = both(r.b_gu, 3)
    gg = r.b_gg[0:T, :]
    gu = r.b_gu[0:T, :]
    sent = []
    for j, c in enumerate(tiles(D, 512)):
        r.rs2_src[:, :, c] = fours(dot_nt(gg, r.w_fg[c, :]) + dot_nt(gu, r.w_fu[c, :]))
        sent += zscatter(r.rs2_src, r.rs2_dst, r.rs2_sem, j)
    tn_n2 = turned(n2, r.at_cot, r.l_n2, 2)

    def unit(grid, land_one, land_two, i, x_first, n):
        cut = (n // 2 + 127) // 128 * 128

        def split(ref, h):
            return ref.at[:, cut:n] if h else ref.at[:, 0:cut]

        return Unit(grid, land_one, land_two, r.one_sem.at[:, i], r.two_sem.at[:, i], x, y, chip, x_first, split)

    def product_of(grid, lhs, b, lo, n):
        left = lhs[...].reshape(D // 2, 2 * T)
        for c in tiles(n, 256 if n % 256 == 0 else 128):
            cols = slice(lo + c.start, lo + c.stop)
            grid[:, :, :, c] = dot(left, b[:, cols]).astype(BF16).reshape(4, 4, 48, c.stop - c.start)

    def out_to(ref, lo, n):
        cut = (n // 2 + 127) // 128 * 128

        def store(h, v):
            ref[:, (lo + cut if h else lo) : (lo + n if h else lo + cut)] = v

        return store

    u_fd = unit(r.gr_fd, r.x_fd, r.y_fd, 0, True, F)
    u_fg = unit(r.gr_fg, r.x_fg, r.y_fg, 1, False, F)
    u_fu = [unit(r.gr_fu.at[i], r.x_fu.at[i], r.y_fu.at[i], 2 + i, i == 0, 512) for i in range(2)]
    u_out = unit(r.gr_out, r.x_out, r.y_out, 4, True, C)
    u_gate = unit(r.gr_gate, r.x_gate, r.y_gate, 5, False, C)
    u_in = [unit(r.gr_in.at[i], r.x_in.at[i], r.y_in.at[i], 6 + i, i == 0, 384) for i in range(2)]

    finish(by_act)
    product_of(r.gr_fd, r.l_cot, r.b_act, 0, F)
    u_fd.a0()
    act = r.b_act[0:T, :]
    for c in tiles(D, 512):
        r.rs1_src[:, :, c] = fours(dot(act, r.w_fd[:, c]))

    gy = zsummed(r.rs2_src, r.rs2_dst, sent)
    v = r.middle[...]
    r2 = lax.rsqrt(jnp.mean(v * v, axis=-1, keepdims=True) + EPS)
    vr = v * r2
    gn = gy * g2
    gm = r.cot[own, :].astype(F32) + r2 * (gn - vr * jnp.mean(vr * gn, axis=-1, keepdims=True))
    r.gmid[...] = gm
    r.gmo[z] = gm.astype(BF16)
    got = zgather(r.gmo, r.gmo_sem)
    r.dn[1:2, :] = jnp.sum(vr * gy, axis=0, keepdims=True)
    sent3 = []
    for j in range(3):
        sent3 += zscatter(r.rs1_src, r.rs3_dst, r.rs3_sem, j)
    finish(tn_n2)
    finish(by_gg)
    product_of(r.gr_fg, r.l_n2, r.b_gg, 0, F)
    u_fg.a0()
    finish(got)

    gmo = r.gmo[...].reshape(T, D)
    for c in tiles(C, 256):
        gmx = dot_nt(gmo, r.w_out[c, :])
        gi = r.gate_in[:, c]
        sg = jax.nn.sigmoid(gi)
        r.gso[:, c] = gmx * (gi * sg)
        r.b_gate[0:T, c] = (gmx * r.scan_out[:, c] * (sg * (1.0 + gi * (1.0 - sg)))).astype(BF16)
    by_gate = both(r.b_gate, 4)
    tn_gmo = turned(gmo, r.at_nrm, r.l_gmo, 3)

    def rev_first(c):
        a2 = r.nr2[:, c]

        def body(k, cr):
            b = T // 8 - 1 - k
            st = r.step[pl.ds(b * 8, 8), c]
            gs = r.gso[pl.ds(b * 8, 8), c]
            for i in range(7, -1, -1):
                cr = jnp.exp2(a2 * st[i : i + 1, :]) * (gs[i : i + 1, :] * wide(r.Cb[b * 8 + i]) + cr)
            return cr

        cr = lax.fori_loop(0, T // 8, body, jnp.zeros((N, W), F32))
        for j, cj in enumerate(tiles(W, 128)):
            r.rc_src[:, c.start // 128 + j, :] = cr[:, cj]

    for c in tiles(C, W):
        rev_first(c)
    swapped = swap(r.rc_src, r.rc_recv, r.rc_sem)
    u_fd.a1()
    u_fg.a1()
    finish(by_gu)
    for i in range(2):
        product_of(r.gr_fu.at[i], r.l_n2, r.b_gu, 512 * i, 512)
        u_fu[i].a0()
    swapped()

    def carry_back(k, state):
        j = GROUP - 1 - k
        r.so[j] = state
        return jnp.exp2(mine * r.cs_recv[j, 8:16, :]) * state + r.rc_recv[j]

    lax.fori_loop(0, GROUP, carry_back, jnp.zeros((8, 128), F32))
    swapped = swap(r.so, r.si, r.ro_sem)
    r.n2[z] = (r.middle[...] + zsummed(r.rs1_src, r.rs3_dst, sent3)).astype(BF16)
    sent_out = zgather(r.n2, r.outg_sem)
    u_fd.a2()
    u_fg.a2()
    swapped()
    for j in range(6):
        r.gstate[:, 128 * j : 128 * j + 128] = r.si[:, j, :]

    def rev_second(c):
        a2 = r.nr2[:, c]
        a = r.nr[:, c]

        def body(k, state):
            cr, gl = state
            b = T // 8 - 1 - k
            st = r.step[pl.ds(b * 8, 8), c]
            gs = r.gso[pl.ds(b * 8, 8), c]
            uu = r.u[pl.ds(b * 8, 8), c]
            s1, s2 = [None] * 8, [None] * 8
            for i in range(7, -1, -1):
                t = b * 8 + i
                si, gi, ui = st[i : i + 1, :], gs[i : i + 1, :], uu[i : i + 1, :]
                g = gi * wide(r.Cb[t]) + cr
                s1[i] = jnp.sum(g * wide(r.Bb[t]), axis=0, keepdims=True)
                pr = gi * r.H[t + 1, :, c]
                pe = g * ui
                pr = (pr[:, 0:128] + pr[:, 128:256]) + pr[:, 256:384]
                pe = (pe[:, 0:128] + pe[:, 128:256]) + pe[:, 256:384]
                if c.start:
                    pr = pr + r.PR[t]
                    pe = pe + r.PE[t]
                r.PR[t] = pr
                r.PE[t] = pe
                cr = jnp.exp2(a2 * si) * g
                q = cr * r.H[t, :, c]
                s2[i] = jnp.sum(q * a, axis=0, keepdims=True)
                gl = gl + q * si
            r.gate_in[pl.ds(b * 8, 8), c] = jnp.concatenate(s1, axis=0)
            r.scan_out[pl.ds(b * 8, 8), c] = jnp.concatenate(s2, axis=0)
            return cr, gl

        _, gl = lax.fori_loop(0, T // 8, body, (r.gstate[:, c], jnp.zeros((N, W), F32)))
        r.rows[R : R + N, c] = gl * a

    for c in tiles(C, W):
        rev_second(c)
        (u_fu[0] if c.start == 0 else u_fu[1]).a1()

    def gather_rows(b, carry):
        rows = []
        for i in range(8):
            t = b * 8 + i
            e = jnp.sum(r.PE[t], -1, keepdims=True) * selb + jnp.sum(r.PR[t], -1, keepdims=True) * selc
            rows.append(jnp.sum(e, axis=0, keepdims=True))
        r.er[pl.ds(b * 8, 8), :] = jnp.concatenate(rows, axis=0)
        return carry

    lax.fori_loop(0, T // 8, gather_rows, 0)
    for c in tiles(C, 256):
        inner = r.inner[:, c].astype(F32)
        s1 = r.gate_in[:, c]
        raw_g = (r.scan_out[:, c] + s1 * inner) * jax.nn.sigmoid(r.raw[:, c])
        r.gsr[:, c] = raw_g.astype(BF16)
        r.rows[R + N + 5 : R + N + 6, c] = jnp.sum(raw_g, axis=0, keepdims=True)
        gso = r.gso[:, c]
        r.rows[R + N + 6 : R + N + 7, c] = jnp.sum(gso * inner, axis=0, keepdims=True)
        r.gate_in[:, c] = gso * vec[6:7, c] + s1 * r.step[:, c]
    r.pz[z] = dot_nt(r.gsr[...], r.w_step[...]) + r.er[...]
    summed = zsum(r.pz, r.pz2_sem)
    finish(tn_gmo)
    finish(by_out)
    product_of(r.gr_out, r.l_gmo, r.b_out, 0, C)
    u_out.a0()
    gy = summed()
    vr = r.proj[...] * r.proj_r[...]
    gn = gy * r.in_gains[...]
    gpj = (r.proj_r[...] * (gn - vr * by_part(vr * gn))).astype(BF16)
    r.dg[...] = jnp.broadcast_to(jnp.sum(vr * gy, axis=0, keepdims=True), (8, 128))
    for c in tiles(C, 256):
        gi = r.gate_in[:, c] + dot_nt(gpj, r.w_proj[c, :])
        cs = r.conv_sum[:, c]
        sg = jax.nn.sigmoid(cs)
        r.gcs[0:T, c] = gi * (sg * (1.0 + cs * (1.0 - sg)))
    halo = start([rcopy(r.gcs.at[0:8], r.halo2, r.halo_sem, (1,), gdev(15))])
    finish(by_gate)
    product_of(r.gr_gate, r.l_nrm, r.b_gate, 0, C)
    u_gate.a0()
    finish(halo)
    r.gcs[T : T + 8, :] = jnp.where(p == GROUP - 1, 0.0, r.halo2[...])
    for c in tiles(C, 128):
        tot = vec[3:4, c] * r.gcs[0:T, c]
        for k in range(3):
            tot = tot + vec[k : k + 1, c] * r.gcs[3 - k : 3 - k + T, c]
        r.b_in[0:T, c] = tot.astype(BF16)
    by_in = both(r.b_in, 5)
    gip = r.b_in[0:T, :]
    ggi = r.b_gate[0:T, :]
    sent = []
    for j, c in enumerate(tiles(D, 512)):
        gnp = dot_nt(gip, r.w_in[c, :]) + dot_nt(ggi, r.w_gate[c, :])
        r.rs2_src[:, :, c] = fours(gnp)
        sent += zscatter(r.rs2_src, r.rs1_dst, r.rs4_sem, j)
        r.dn[0:1, c] = jnp.sum(r.tok[:, c].astype(F32) * (r.rinv[:, 0:1] * gnp), axis=0, keepdims=True)
    finish(by_in)
    for i in range(2):
        product_of(r.gr_in.at[i], r.l_nrm, r.b_in, 384 * i, 384)
        u_in[i].a0()
    def owner(shape):
        i = lax.broadcasted_iota(jnp.int32, shape, 0)
        return 2 * (i & 15) + (i >> 4)

    k1 = lax.broadcasted_iota(jnp.int32, (32, D), 1) - 48 * owner((32, D))
    at48 = ((k1 >= 0) & (k1 < 48)).astype(F32)
    kk = lax.broadcasted_iota(jnp.int32, (D, 128), 0)
    spot = lax.broadcasted_iota(jnp.int32, (D, 128), 1) - (kk - 48 * ((kk * 683) >> 15))
    k4 = lax.broadcasted_iota(jnp.int32, (32, 128), 1) - 4 * owner((32, 128))
    at4 = ((k4 >= 0) & (k4 < 4)).astype(F32)
    k5 = lax.broadcasted_iota(jnp.int32, (128, 128), 0)
    spot4 = (lax.broadcasted_iota(jnp.int32, (128, 128), 1) - (k5 & 3) == 96).astype(F32)
    r.nz[z] = (
        dot(at48 * r.dn[0:1, :], (spot == 0).astype(F32), HIGH)
        + dot(at48 * r.dn[1:2, :], (spot == 48).astype(F32), HIGH)
        + dot(at4 * (r.dg[0:1, :] * 0.25), spot4, HIGH)
    )
    gains = zsum(r.nz, r.nz_sem)
    for c in tiles(C, 128):
        gc = r.gcs[0:T, c]
        for k in range(4):
            r.rows[R + N + k : R + N + k + 1, c] = jnp.sum(gc * r.ext[5 + k : 5 + k + T, c], axis=0, keepdims=True)
        r.rows[R + N + 4 : R + N + 5, c] = jnp.sum(gc, axis=0, keepdims=True)
    r.rows[0:R, :] = jnp.zeros((R, C), F32)
    r.rows[R + N + 7 : T, :] = jnp.zeros((T - R - N - 7, C), F32)
    chan = (dot(r.gsr[...].T, r.step_in[...]) + r.rows[...].T).reshape(16, 2, 24, 128)
    ll = lax.broadcasted_iota(jnp.int32, (128, 128), 0)
    order = (lax.broadcasted_iota(jnp.int32, (128, 128), 1) == 4 * (2 * (ll & 15) + ((ll >> 4) & 1)) + (ll >> 5)).astype(BF16)
    pt = dot(dot_nt(order, gpj).astype(BF16), r.inner[...])
    gained = gains()
    for h in range(2):
        r.small[:, h, 24:48, :] = chan[:, h]
        r.small[:, h, 48:56, :] = jnp.zeros((16, 8, 128), F32)
        r.small[:, h, 48, :] = gained[16 * h : 16 * h + 16, :]
        for i in range(4):
            for j in range(6):
                r.small[:, h, i * 6 + j, :] = pt[32 * i + 16 * h : 32 * i + 16 * h + 16, 128 * j : 128 * j + 128]
    pair = start([rcopy(r.small.at[:, 1 - core], r.small_recv, r.small_sem, (0,), sibling)])
    for i in range(2):
        u_in[i].a1()
    finish(pair)
    r.gr_small[...] = (r.small[:, core] + r.small_recv[...]).reshape(4, 4, SMALL, 128)

    def rows_split(ref, h):
        return ref.at[32:SMALL, :] if h else ref.at[0:32, :]

    u_small = Unit(r.gr_small, r.x_small, r.y_small, r.one_sem.at[:, 8], r.two_sem.at[:, 8], x, y, chip, True, rows_split)
    u_small.a0()
    gn1 = zsummed(r.rs2_src, r.rs1_dst, sent)
    v = r.tok[own, :].astype(F32)
    rs = lax.rsqrt(jnp.mean(v * v, axis=-1, keepdims=True) + EPS)
    vr = v * rs
    gn = gn1 * g1
    r.gmo[z] = (r.gmid[...] + rs * (gn - vr * jnp.mean(vr * gn, axis=-1, keepdims=True))).astype(BF16)
    sent_tok = zgather(r.gmo, r.gtok_sem)
    u_small.a1()
    u_in[0].a2()
    u_in[1].a2()
    u_small.a2()
    u_fu[0].a2()
    u_fu[1].a2()
    u_out.a1()
    u_gate.a1()
    u_out.a2()
    u_gate.a2()
    for u in (u_fd, u_fg, *u_fu, u_out, u_gate, *u_in, u_small):
        u.b1()
    u_fd.b2(out_to(r.out_big, 0, F))
    u_fg.b2(out_to(r.out_big, F, F))
    for i in range(2):
        u_fu[i].b2(out_to(r.out_big, 2 * F + 512 * i, 512))
    u_out.b2(out_to(r.out_big, 3 * F, C))
    u_gate.b2(out_to(r.out_big, 3 * F + C, C))
    for i in range(2):
        u_in[i].b2(out_to(r.out_big, 3 * F + 2 * C + 384 * i, 384))

    def small_store(h, v):
        r.out_small[(32 if h else 0) : (SMALL if h else 32), :] = v

    u_small.b2(small_store)
    finish(sent_out)
    y_out = pltpu.make_async_copy(r.n2, r.out_y, r.load_sem.at[0])
    y_out.start()
    finish(sent_tok)
    gt_out = pltpu.make_async_copy(r.gmo, r.out_gt, r.load_sem.at[1])
    gt_out.start()
    y_out.wait()
    gt_out.wait()


def V(*shape, dtype=BF16):
    return pltpu.VMEM(shape, dtype)


def V32(*shape):
    return pltpu.VMEM(shape, F32)


def S(*shape):
    return pltpu.SemaphoreType.DMA(shape)


BIG = 3 * F + 3 * C
HBM, VMEM = pl.ANY, pltpu.VMEM
INS = dict(
    in_tok=HBM, in_cot=HBM, in_w_in=HBM, in_w_gate=HBM, in_w_proj=HBM, in_w_step=HBM, in_w_out=HBM, in_w_fg=HBM, in_w_fu=HBM,
    in_w_fd=HBM, in_vec=VMEM, in_norms=VMEM, in_gains=VMEM, in_rates=VMEM,
)
OUTS = dict(out_y=((4, 32, D), BF16), out_gt=((4, 32, D), BF16), out_big=((48, BIG), F32), out_small=((SMALL, 128), F32))
SCRATCH = dict(
    tok=V(T, D), cot=V(T, D), w_in=V(D, C), w_gate=V(D, C), w_proj=V(C, 128), w_step=V(T, C), w_out=V(C, D), w_fg=V(D, F), w_fu=V(D, F),
    w_fd=V(F, D), load_sem=pltpu.SemaphoreType.DMA((10,)),
    nr=V32(N, C), nr2=V32(N, C), nr3=V32(N, 8, 128), rinv=V32(T, 128), normed=V(T, D), ext=V32(T + 8, C), halo=V32(8, C),
    halo_sem=S(2, 2), gate_in=V32(T, C), conv_sum=V32(T, C), inner=V(T, C),
    pz=V32(4, T, 128), pz_sem=S(2, 4), proj=V32(T, 128), proj_r=V32(T, 128), pn=V32(T, 128), step_in=V(T, 128),
    raw=V32(T, C), step=V32(T, C), u=V32(T, C), Bb=V32(T, N, 128), Cb=V32(T, N, 128),
    cs_src=V32(N, 16, 128), cs_recv=V32(N, 16, 128), cs_sem=S(2, 16), so=V32(N, 8, 128), si=V32(N, 8, 128), so_sem=S(2, 16),
    rc_src=V32(N, 8, 128), rc_recv=V32(N, 8, 128), rc_sem=S(2, 16), ro_sem=S(2, 16),
    H=V32(T + 1, N, C), scan_out=V32(T, C),
    rs1_src=V(4, 32, D), rs1_dst=V(3, 32, D), rs1_sem=S(2, 3, 4), rs2_src=V(4, 32, D), rs2_dst=V(3, 32, D), rs2_sem=S(2, 3, 4),
    rs3_dst=V(3, 32, D), rs3_sem=S(2, 3, 4), rs4_sem=S(2, 3, 4),
    middle=V32(32, D), gmid=V32(32, D), n2=V(4, 32, D), n2_sem=S(2, 4), gmo=V(4, 32, D), gmo_sem=S(2, 4),
    outg_sem=S(2, 4), gtok_sem=S(2, 4),
    gact=V32(T, F), at_cot=V(16, 2, 48, T), at_nrm=V(16, 2, 48, T),
    l_cot=V(16, 48, 2 * T), l_nrm=V(16, 48, 2 * T), l_n2=V(16, 48, 2 * T), l_gmo=V(16, 48, 2 * T), turn_sem=S(2, 4),
    b_out=V(2 * T, C), b_act=V(2 * T, F), b_gg=V(2 * T, F), b_gu=V(2 * T, F), b_gate=V(2 * T, C), b_in=V(2 * T, C), both_sem=S(2, 6),
    gr_fd=V(4, 4, 48, F), x_fd=V(6, 2, 48, F), y_fd=V(6, 48, F), gr_fg=V(4, 4, 48, F), x_fg=V(6, 2, 48, F), y_fg=V(6, 48, F),
    gr_fu=V(2, 4, 4, 48, 512), x_fu=V(2, 6, 2, 48, 512), y_fu=V(2, 6, 48, 512),
    gr_out=V(4, 4, 48, C), x_out=V(6, 2, 48, C), y_out=V(6, 48, C), gr_gate=V(4, 4, 48, C), x_gate=V(6, 2, 48, C), y_gate=V(6, 48, C),
    gr_in=V(2, 4, 4, 48, 384), x_in=V(2, 6, 2, 48, 384), y_in=V(2, 6, 48, 384), one_sem=S(2, 9, 6), two_sem=S(2, 9, 6),
    gso=V32(T, C), gstate=V32(N, C), PR=V32(T, N, 128), PE=V32(T, N, 128), rows=V32(T, C), er=V32(T, 128),
    gsr=V(T, C), pz2_sem=S(2, 4), gcs=V32(T + 8, C), halo2=V32(8, C), dn=V32(8, D), dg=V32(8, 128),
    nz=V32(4, 32, 128), nz_sem=S(2, 4), small=V32(16, 2, SMALL, 128), small_recv=V32(16, SMALL, 128),
    small_sem=S(2, 1), gr_small=V32(4, 4, SMALL, 128), x_small=V32(6, 2, SMALL, 128), y_small=V32(6, SMALL, 128),
)


def local(
    tokens, cotangent, norm_first, in_inner, in_gate, conv_weight, conv_bias, projector, projector_gains, step_weight, step_bias,
    log_rates, skip_gain, out_weight, norm_second, gate_weight, up_weight, down_weight,
):
    vec = jnp.concatenate([conv_weight, conv_bias[None], step_bias[None], skip_gain[None], skip_gain[None]], axis=0)
    norms = jnp.stack([norm_first, norm_second])
    y, gt, big, small = pl.pallas_call(
        kernel,
        out_shape=[jax.ShapeDtypeStruct(shape, dtype) for shape, dtype in OUTS.values()],
        in_specs=[pl.BlockSpec(memory_space=m) for m in INS.values()],
        out_specs=[pl.BlockSpec(memory_space=m) for m in (HBM, HBM, VMEM, VMEM)],
        scratch_shapes=list(SCRATCH.values()),
        compiler_params=pltpu.CompilerParams(collective_id=0, has_side_effects=True, vmem_limit_bytes=int(63.9 * 2**20)),
    )(
        tokens, cotangent, in_inner, in_gate, projector, step_weight, out_weight, gate_weight, up_weight, down_weight,
        vec, norms, projector_gains[None], log_rates,
    )
    fd, fg, fu, out, gate, inn = jnp.split(big, [F, 2 * F, 3 * F, 3 * F + C, 3 * F + 2 * C], axis=1)
    proj = small[0:24].reshape(4, C).T
    chan = small[24:48]
    gains = small[48]
    cut = R + N
    return (
        y.reshape(T, D), gt.reshape(T, D), gains[0:48], inn, gate, chan[:, cut : cut + 4].T, chan[:, cut + 4], proj, gains[96:100],
        chan[:, 0:R].T, chan[:, cut + 5], chan[:, R:cut], chan[:, cut + 6], out.T, gains[48:96], fg, fu, fd.T,
    )


def solution(mesh):
    row, col = P("seq", None), P(None, "head")
    flat, deep = P("head"), P("head", None)
    in_specs = (row, row, P(), col, col, col, flat, deep, P(), col, flat, deep, flat, deep, P(), col, col, deep)
    both, mix = ("head", "seq"), P("seq", "head")
    turned = P("head", "seq")
    out_specs = (
        row, row, P("seq"), mix, mix, P(None, both), P(both), turned, P("seq"), P(None, both), P(both), P(both, None), P(both),
        turned, P("seq"), mix, mix, turned,
    )
    return jax.shard_map(local, mesh=mesh, in_specs=in_specs, out_specs=out_specs, check_vma=False)
```

```python
import types

import jax
import jax.numpy as jnp
from jax import lax
from jax.experimental import pallas as pl
from jax.experimental.pallas import tpu as pltpu
from jax.sharding import PartitionSpec as P

F32 = jnp.float32
BF16 = jnp.bfloat16
T, D, C, F, N, R = 128, 1536, 768, 1024, 16, 96
GROUP = 16
EPS = 1e-5
LOG2E = 1.4426950408889634
HIGH = lax.Precision.HIGHEST
MESH = pl.DeviceIdType.MESH
SMALL = 48
SEMS = 131
W = 384


def dot(a, b, precision=None):
    return jnp.dot(a, b, precision=precision, preferred_element_type=F32)


def dot_nt(a, b, precision=None):
    return lax.dot_general(a, b, (((1,), (1,)), ((), ())), precision=precision, preferred_element_type=F32)


def tiles(total, width):
    return [slice(i, i + width) for i in range(0, total, width)]


def wide(v):
    return jnp.concatenate([v] * (W // 128), axis=1)


def rcopy(src, dst, sems, device):
    return pltpu.make_async_remote_copy(
        src_ref=src, dst_ref=dst, send_sem=sems[0], recv_sem=sems[1], device_id=device, device_id_type=MESH
    )


def start(copies):
    for c in copies:
        c.start()
    return copies


def finish(copies):
    for c in copies:
        c.wait()


class Burst:
    def __init__(self, sems, src, dst, device):
        self.sems, self.all = sems, rcopy(src, dst, sems, device)

    def send(self, src, dst, device):
        rcopy(src, dst, self.sems, device).start()

    def wait(self):
        self.all.wait()


class Ring:
    def __init__(self, part, land, two, four, new, place, at):
        self.part, self.land, self.at, self.me = part, land, at, place
        self.right, self.left, self.far = lax.rem(place + 1, 4), lax.rem(place + 3, 4), lax.rem(place + 2, 4)
        self.first = Burst(new(), two, two, at(self.right))
        self.rest = Burst(new(), four, four, at(self.right))

    def begin(self):
        part, land, at, right, left, far = self.part, self.land, self.at, self.right, self.left, self.far
        self.first.send(part(far, 0), land(0, 0), at(right))
        self.first.send(part(far, 1), land(1, 1), at(left))
        self.rest.send(part(right, 1), land(2, 1), at(right))
        self.rest.send(part(left, 0), land(3, 0), at(left))

    def pass_on(self):
        self.first.wait()
        for h, d in enumerate((self.right, self.left)):
            own = self.part(d, h)
            own[...] = (own[...].astype(F32) + self.land(h, h)[...].astype(F32)).astype(own.dtype)
            self.rest.send(own, self.land(4 + h, h), self.at(d))

    def totals(self):
        self.rest.wait()
        for h, (a, b) in enumerate(((4, 3), (5, 2))):
            own = self.part(self.me, h)
            yield own, own[...].astype(F32) + (self.land(a, h)[...].astype(F32) + self.land(b, h)[...].astype(F32))


class Straight:
    def __init__(self, part, land, new, place, at):
        self.part, self.land, self.at, self.me = part, land, at, place
        self.burst = Burst(new(), land, land, at(lax.rem(place + 1, 4)))

    def begin(self):
        for k in (2, 1, 3):
            d = lax.rem(self.me + k, 4)
            self.burst.send(self.part(d), self.land.at[k - 1], self.at(d))

    def totals(self):
        self.burst.wait()
        own, land = self.part(self.me), self.land
        yield own, own[...].astype(F32) + ((land[0].astype(F32) + land[2].astype(F32)) + land[1].astype(F32))


class Unit:
    def __init__(self, grid, land_one, land_two, new, x, y, at, x_first, both_ways, split=0):
        along_x, along_y = (x, lambda d: at(d, y)), (y, lambda d: at(x, d))
        one, two = (along_x, along_y) if x_first else (along_y, along_x)

        def chunk(d, half=slice(0, 4)):
            return grid.at[half, d] if x_first else grid.at[d, half]

        def piece(d):
            return grid.at[d, x] if x_first else grid.at[y, d]

        if both_ways:
            self.one = Ring(
                lambda d, h: chunk(d, slice(2 * h, 2 * h + 2)), lambda i, h: land_one.at[i], land_one.at[0:2], land_one.at[2:6], new, *one
            )
        else:
            self.one = Straight(chunk, land_one, new, *one)
        if split:

            def side(ref, h):
                return ref.at[:, split:] if h else ref.at[:, 0:split]

            self.two = Ring(
                lambda d, h: side(piece(d), h), lambda i, h: side(land_two.at[i], h), land_two.at[0], land_two.at[0:2], new, *two
            )
        else:
            self.two = Straight(piece, land_two, new, *two)

    def a0(self):
        self.one.begin()

    def a1(self):
        self.one.pass_on()

    def a2(self):
        for own, v in self.one.totals():
            own[...] = v.astype(own.dtype)
        self.two.begin()

    def b1(self):
        self.two.pass_on()

    def done(self):
        return [v for _, v in self.two.totals()]


def kernel(*refs):
    r = types.SimpleNamespace(**dict(zip([*INS, *OUTS, *SCRATCH], refs, strict=True)))
    s = lax.axis_index("seq")
    z = lax.axis_index("head")
    p = lax.rem(s, GROUP)
    base = s - p
    core = lax.rem(s, 2)
    x = lax.rem(s // 2, 4)
    y = s // 8

    def zdev(k):
        return (s, lax.rem(z + k, 4))

    def gdev(k):
        return (base + lax.rem(p + k, GROUP), z)

    def chip(cx, cy):
        return (cy * 8 + cx * 2 + core, z)

    sibling = (s + 1 - 2 * core, z)
    taken = []

    def new():
        taken.append(0)
        return r.sem.at[len(taken) - 1]

    def pair():
        return new(), new()

    barrier = pltpu.get_barrier_semaphore()
    for k in range(1, 4):
        pl.semaphore_signal(barrier, 1, device_id=zdev(k), device_id_type=MESH)

    mates = sorted(((dy + min(dx, 4 - dx), dy, dx) for dy in range(2) for dx in range(4)), reverse=True)[:7]

    def mate(dy, dx):
        return base + lax.rem(y + dy, 2) * 8 + lax.rem(x + dx, 4) * 2 + core

    others = [(mate(dy, dx), z) for _, dy, dx in mates]
    for device in (*others, sibling, gdev(15 - 14 * core), (s + 8 * (3 - 2 * y), z)):
        pl.semaphore_signal(barrier, 1, device_id=device, device_id_type=MESH)

    def load(src, dst):
        c = pltpu.make_async_copy(src, dst, new())
        c.start()
        return c

    ld_tok = load(r.in_tok, r.tok)
    ld_in = load(r.in_w_in, r.w_in)
    ld_gate = load(r.in_w_gate, r.w_gate)
    ld_cot = load(r.in_cot, r.cot)
    ld_fd = load(r.in_w_fd, r.w_fd)
    ld_proj = load(r.in_w_proj, r.w_proj)
    r.w_step[...] = jnp.zeros((T, C), BF16)
    ld_step = load(r.in_w_step, r.w_step.at[0:R])
    ld_out = load(r.in_w_out, r.w_out)
    ld_fg = load(r.in_w_fg, r.w_fg)
    ld_fu = load(r.in_w_fu, r.w_fu)

    vec = r.vec
    vec[0:4, :] = r.in_taps[...]
    for i, v in enumerate((r.in_cbias, r.in_sbias, r.in_skip)):
        vec[4 + i : 5 + i, :] = v[...].reshape(1, C)
    g1 = r.in_first[...].reshape(1, D)
    g2 = r.in_second[...].reshape(1, D)
    nr = -jnp.exp(r.in_rates[...])
    r.nr[...] = nr
    nr2 = nr * LOG2E
    r.nr2[...] = nr2
    for j, c in enumerate(tiles(C, W)):
        r.nr2h[j] = nr2[:, c]

    ld_tok.wait()
    for rows in tiles(T, 32):
        v = r.tok[rows, :].astype(F32)
        rs = lax.rsqrt(jnp.mean(v * v, axis=-1, keepdims=True) + EPS)
        r.rinv[rows, :] = jnp.broadcast_to(rs, (32, 128))
        r.normed[rows, :] = (v * rs * g1).astype(BF16)
    ld_in.wait()
    nrm = r.normed[...]
    for c in tiles(C, 256):
        r.ext[8 : 8 + T, c] = dot(nrm, r.w_in[:, c]).astype(BF16).astype(F32)
    pl.semaphore_wait(barrier, 3 + 7 + 3)
    halo = start([rcopy(r.ext.at[T : T + 8], r.halo, pair(), gdev(1))])
    ld_gate.wait()
    for c in tiles(C, 256):
        r.gate_in[:, c] = dot(nrm, r.w_gate[:, c])

    def turned(value, at, lhs):
        at[...] = value.T.reshape(16, 2, 48, T)
        lhs[:, :, 0:T] = at[:, core]
        return start([rcopy(at.at[:, 1 - core], lhs.at[:, :, T : 2 * T], pair(), sibling)])

    def both(b):
        return start([rcopy(b.at[0:T], b.at[T : 2 * T], pair(), sibling)])

    ld_cot.wait()
    ld_fd.wait()
    cot = r.cot[...]
    for c in tiles(F, 256):
        r.gact[:, c] = dot_nt(cot, r.w_fd[c, :])

    tn_cot = turned(cot, r.at_cot, r.l_cot)
    tn_nrm = turned(nrm, r.at_nrm, r.l_nrm)

    finish(halo)
    r.ext[0:8, :] = jnp.where(p == 0, 0.0, r.halo[...])
    for c in tiles(C, 128):
        tot = vec[4:5, c] + vec[0:1, c] * r.ext[5 : 5 + T, c]
        for k in range(1, 4):
            tot = tot + vec[k : k + 1, c] * r.ext[5 + k : 5 + k + T, c]
        r.conv_sum[:, c] = tot
        r.inner[:, c] = (tot * jax.nn.sigmoid(tot)).astype(BF16)

    def zgather(buf):
        burst = Burst(pair(), buf.at[0:3], buf.at[0:3], zdev(1))
        for k in (2, 1, 3):
            burst.send(buf.at[z], buf.at[z], zdev(k))
        return burst

    def zsum(buf):
        burst = zgather(buf)

        def result():
            burst.wait()
            return (buf[0].astype(F32) + buf[1].astype(F32)) + (buf[2].astype(F32) + buf[3].astype(F32))

        return result

    ld_proj.wait()
    r.pz[z] = dot(r.inner[...], r.w_proj[...]).astype(BF16)
    projected = zsum(r.pz)

    proj = projected()
    r.proj[...] = proj
    lane = lax.broadcasted_iota(jnp.int32, (1, 128), 1)
    m1 = (lane < R).astype(F32)
    m3 = (lane >= R + N).astype(F32)
    m2 = 1.0 - m1 - m3

    def by_part(v):
        return (
            m1 * (jnp.sum(v * m1, -1, keepdims=True) / R)
            + m2 * (jnp.sum(v * m2, -1, keepdims=True) / N)
            + m3 * (jnp.sum(v * m3, -1, keepdims=True) / N)
        )

    rr = lax.rsqrt(by_part(proj * proj) + EPS)
    r.proj_r[...] = rr
    gains_in = r.in_gains[...].reshape(1, 128)
    pn = proj * rr * gains_in
    r.pn[...] = pn
    step_in = (pn * m1).astype(BF16)
    r.step_in[...] = step_in
    ld_step.wait()
    for c in tiles(C, 256):
        raw = dot(step_in, r.w_step[:, c]) + vec[5:6, c]
        r.raw[:, c] = raw
        st = jnp.maximum(raw, 0.0) + jnp.log1p(jnp.exp(-jnp.abs(raw)))
        r.step[:, c] = st
        r.u[:, c] = st * r.inner[:, c].astype(F32)
    rown = lax.broadcasted_iota(jnp.int32, (N, 128), 0)
    lanes = lax.broadcasted_iota(jnp.int32, (N, 128), 1)
    selb = (lanes == rown + R).astype(F32)
    selc = (lanes == rown + R + N).astype(F32)
    sel = selb + selc
    part_of = lax.broadcasted_iota(jnp.int32, (128, 256), 0) - jnp.where(lax.broadcasted_iota(jnp.int32, (128, 256), 1) < 128, R, R + N)
    to_lanes = ((part_of >= 0) & (part_of < N)).astype(BF16)

    for rows in tiles(T, 32):
        some = r.pn[rows, :]
        one = jnp.concatenate([jnp.broadcast_to(some[i : i + 1, :], (N, 128)) * sel for i in range(32)], axis=0)
        high = one.astype(BF16)
        low = (one - high.astype(F32)).astype(BF16)
        v = dot(high, to_lanes) + dot(low, to_lanes)
        r.Bb[rows] = v[:, 0:128].reshape(32, N, 128)
        r.Cb[rows] = v[:, 128:256].reshape(32, N, 128)

    top = lax.broadcasted_iota(jnp.int32, (N, W), 0) < 8

    def coded(ref, h, tot):
        high = tot.astype(BF16).astype(F32)
        ref[0:N, :] = h.astype(BF16)
        ref[N : 2 * N, :] = jnp.where(top, high, tot - high).astype(BF16)

    def state_of(ref):
        return ref[0:N, :].astype(F32)

    def steps_of(ref):
        v = ref[N : 2 * N, :].astype(F32)
        return v[0:1, :] + v[8:9, :]

    for half, c in enumerate(tiles(C, W)):
        a2 = r.nr2[:, c]

        def first(b, h):
            st = r.step[pl.ds(b * 8, 8), c]
            uu = r.u[pl.ds(b * 8, 8), c]
            for i in range(8):
                h = jnp.exp2(a2 * st[i : i + 1, :]) * h + uu[i : i + 1, :] * wide(r.Bb[b * 8 + i])
            return h

        h = lax.fori_loop(0, T // 8, first, jnp.zeros((N, W), F32))
        coded(r.pack.at[half], h, jnp.sum(r.step[:, c], axis=0, keepdims=True))

    nth = p // 2
    is_first = core == 0
    a2c = r.nr2h[core]

    def to_mates(src, land):
        burst = Burst(pair(), land.at[0:7], land.at[0:7], sibling)
        for device in others:
            burst.send(src, land.at[nth], device)
        land[nth] = src[...]
        return burst.wait

    def to_sibling(src, dst):
        return start([rcopy(src, dst, pair(), sibling)])

    finish(to_sibling(r.pack.at[1 - core], r.pack_sib))
    h_own, h_sib = state_of(r.pack.at[core]), state_of(r.pack_sib)
    t_own, t_sib = steps_of(r.pack.at[core]), steps_of(r.pack_sib)
    h0, h1 = jnp.where(is_first, h_own, h_sib), jnp.where(is_first, h_sib, h_own)
    t0, t1 = jnp.where(is_first, t_own, t_sib), jnp.where(is_first, t_sib, t_own)
    r.t01[0:1, :] = t0
    r.t01[8:9, :] = t1
    coded(r.chip_src, jnp.exp2(a2c * t1) * h0 + h1, t0 + t1)
    swapped = to_mates(r.chip_src, r.chips)
    finish(tn_cot)
    finish(tn_nrm)
    swapped()
    state = jnp.zeros((N, W), F32)
    for j in range(7):
        at = r.chips.at[j]
        state = jnp.where(j < nth, jnp.exp2(a2c * steps_of(at)) * state + state_of(at), state)
    later = jnp.exp2(a2c * t0) * state + h0
    r.st_src[...] = jnp.where(is_first, later, state)
    entering = to_sibling(r.st_src, r.st_sib)
    state = jnp.where(is_first, state, later)
    finish(entering)
    for half, c in enumerate(tiles(C, W)):
        r.H[0, :, c] = jnp.where(core == half, state, r.st_sib[...])

    for c in tiles(C, W):
        a2 = r.nr2[:, c]

        def second(b, h):
            st = r.step[pl.ds(b * 8, 8), c]
            uu = r.u[pl.ds(b * 8, 8), c]
            rows = []
            for i in range(8):
                h = jnp.exp2(a2 * st[i : i + 1, :]) * h + uu[i : i + 1, :] * wide(r.Bb[b * 8 + i])
                r.H[b * 8 + i + 1, :, c] = h
                rows.append(jnp.sum(h * wide(r.Cb[b * 8 + i]), axis=0, keepdims=True))
            r.scan_out[pl.ds(b * 8, 8), c] = jnp.concatenate(rows, axis=0)
            return h

        lax.fori_loop(0, T // 8, second, r.H[0, :, c])

    for c in tiles(C, 128):
        so = r.scan_out[:, c] + vec[6:7, c] * r.inner[:, c].astype(F32)
        r.scan_out[:, c] = so
        gi = r.gate_in[:, c]
        r.b_out[0:T, c] = (so * (gi * jax.nn.sigmoid(gi))).astype(BF16)
    by_out = both(r.b_out)

    def zscatter(src, dst):
        return Burst(pair(), src.at[0:3], dst, zdev(1))

    def zsend(burst, src, dst, j):
        c = slice(512 * j, 512 * j + 512)
        for k in (2, 1, 3):
            burst.send(src.at[lax.rem(z + k, 4), :, c], dst.at[k - 1, :, c], zdev(k))

    def zsummed(src, dst, burst):
        burst.wait()
        return (src[z].astype(F32) + dst[0].astype(F32)) + (dst[1].astype(F32) + dst[2].astype(F32))

    def fours(v):
        return v.astype(BF16).reshape(4, 32, v.shape[-1])

    ld_out.wait()
    mixed = r.b_out[0:T, :]
    sent = zscatter(r.rs1_src, r.rs1_dst)
    for j, c in enumerate(tiles(D, 512)):
        r.rs1_src[:, :, c] = fours(dot(mixed, r.w_out[:, c]))
        zsend(sent, r.rs1_src, r.rs1_dst, j)
    own = pl.ds(pl.multiple_of(z * 32, 32), 32)
    middle = r.tok[own, :].astype(F32) + zsummed(r.rs1_src, r.rs1_dst, sent)
    r.middle[...] = middle
    r2 = lax.rsqrt(jnp.mean(middle * middle, axis=-1, keepdims=True) + EPS)
    r.n2[z] = (middle * r2 * g2).astype(BF16)
    zgather(r.n2).wait()

    n2 = r.n2[...].reshape(T, D)
    ld_fg.wait()
    ld_fu.wait()
    for c in tiles(F, 256):
        g = dot(n2, r.w_fg[:, c])
        u = dot(n2, r.w_fu[:, c])
        ga = r.gact[:, c]
        sg = jax.nn.sigmoid(g)
        sl = g * sg
        r.b_act[0:T, c] = (sl * u).astype(BF16)
        r.b_gg[0:T, c] = (ga * u * (sg * (1.0 + g * (1.0 - sg)))).astype(BF16)
        r.b_gu[0:T, c] = (ga * sl).astype(BF16)
    by_act = both(r.b_act)
    gg = r.b_gg[0:T, :]
    gu = r.b_gu[0:T, :]
    sent = zscatter(r.rs2_src, r.rs2_dst)
    for j, c in enumerate(tiles(D, 512)):
        r.rs2_src[:, :, c] = fours(dot_nt(gg, r.w_fg[c, :]) + dot_nt(gu, r.w_fu[c, :]))
        zsend(sent, r.rs2_src, r.rs2_dst, j)
    by_gg = both(r.b_gg)
    by_gu = both(r.b_gu)
    tn_n2 = turned(n2, r.at_cot, r.l_n2)

    def unit(grid, land_one, land_two, x_first, both_ways=True, split=0):
        return Unit(grid, land_one, land_two, pair, x, y, chip, x_first, both_ways, split)

    def product_of(grid, lhs, b, lo, n):
        left = lhs[...].reshape(D // 2, 2 * T)
        for c in tiles(n, 256 if n % 256 == 0 else 128):
            cols = slice(lo + c.start, lo + c.stop)
            grid[:, :, :, c] = dot(left, b[:, cols]).astype(BF16).reshape(4, 4, 48, c.stop - c.start)

    leaving = new()

    def store_out(u, lo, n):
        c = slice(lo, lo + n)
        at = lo
        for v in u.done():
            r.big[:, at : at + v.shape[1]] = v
            at += v.shape[1]
        pltpu.make_async_copy(r.big.at[:, c], r.out_big.at[:, c], leaving).start()

    u_fd = unit(r.gr_fd, r.x_fd, r.y_fd, True, split=F // 2)
    u_fg = unit(r.gr_fg, r.x_fg, r.y_fg, False, split=F // 2)
    u_fu = [unit(r.gr_fu.at[i], r.x_fu.at[i], r.y_fu.at[i], i == 0) for i in range(2)]
    u_out = unit(r.gr_out, r.x_out, r.y_out, True)
    u_gate = unit(r.gr_gate, r.x_gate, r.y_gate, False)
    u_in = [unit(r.gr_in.at[i], r.x_in.at[i], r.y_in.at[i], i == 0, False) for i in range(2)]
    u_small = unit(r.gr_small, r.x_small, r.y_small, True, False)
    u_first = unit(r.gr_first, r.x_first, r.y_first, False, False)

    finish(by_act)
    product_of(r.gr_fd, r.l_cot, r.b_act, 0, F)
    u_fd.a0()
    finish(tn_n2)
    finish(by_gg)
    product_of(r.gr_fg, r.l_n2, r.b_gg, 0, F)
    u_fg.a0()
    finish(by_gu)
    for i in range(2):
        product_of(r.gr_fu.at[i], r.l_n2, r.b_gu, 512 * i, 512)
        u_fu[i].a0()

    gy = zsummed(r.rs2_src, r.rs2_dst, sent)
    v = r.middle[...]
    r2 = lax.rsqrt(jnp.mean(v * v, axis=-1, keepdims=True) + EPS)
    vr = v * r2
    gn = gy * g2
    gm = r.cot[own, :].astype(F32) + r2 * (gn - vr * jnp.mean(vr * gn, axis=-1, keepdims=True))
    r.gmid[...] = gm
    r.gmo[z] = gm.astype(BF16)
    got = zgather(r.gmo)
    r.dn[1:2, :] = jnp.sum(vr * gy, axis=0, keepdims=True)
    act = r.b_act[0:T, :]
    sent3 = zscatter(r.rs1_src, r.rs3_dst)
    for j, c in enumerate(tiles(D, 512)):
        r.rs1_src[:, :, c] = fours(dot(act, r.w_fd[:, c]))
        zsend(sent3, r.rs1_src, r.rs3_dst, j)

    def owner(shape):
        i = lax.broadcasted_iota(jnp.int32, shape, 0)
        return 2 * (i & 15) + (i >> 4)

    def rows_of(v, width, hot):
        k = lax.broadcasted_iota(jnp.int32, (32, v.shape[1]), 1) - width * owner((32, v.shape[1]))
        one = jnp.where((k >= 0) & (k < width), v, 0.0)
        high = one.astype(BF16)
        return dot(high, hot) + dot((one - high.astype(F32)).astype(BF16), hot)

    kk = lax.broadcasted_iota(jnp.int32, (D, 128), 0)
    hot = lax.broadcasted_iota(jnp.int32, (D, 128), 1) == kk - 48 * ((kk * 683) >> 15)
    r.at_cot[...] = hot.astype(BF16).reshape(16, 2, 48, T)
    got.wait()

    gmo = r.gmo[...].reshape(T, D)
    for c in tiles(C, 256):
        gmx = dot_nt(gmo, r.w_out[c, :])
        gi = r.gate_in[:, c]
        sg = jax.nn.sigmoid(gi)
        r.gso[:, c] = gmx * (gi * sg)
        r.b_gate[0:T, c] = (gmx * r.scan_out[:, c] * (sg * (1.0 + gi * (1.0 - sg)))).astype(BF16)
    by_gate = both(r.b_gate)
    tn_gmo = turned(gmo, r.at_nrm, r.l_gmo)

    def rev_first(c):
        a2 = r.nr2[:, c]

        def body(k, cr):
            b = T // 8 - 1 - k
            st = r.step[pl.ds(b * 8, 8), c]
            gs = r.gso[pl.ds(b * 8, 8), c]
            for i in range(7, -1, -1):
                cr = jnp.exp2(a2 * st[i : i + 1, :]) * (gs[i : i + 1, :] * wide(r.Cb[b * 8 + i]) + cr)
            return cr

        cr = lax.fori_loop(0, T // 8, body, jnp.zeros((N, W), F32))
        r.pack_b[0 if c.start == 0 else 1] = cr.astype(BF16)

    for c in tiles(C, W):
        rev_first(c)
    finish(to_sibling(r.pack_b.at[1 - core], r.pack_b_sib))
    c_own, c_sib = r.pack_b[core].astype(F32), r.pack_b_sib[...].astype(F32)
    c0, c1 = jnp.where(is_first, c_own, c_sib), jnp.where(is_first, c_sib, c_own)
    t0, t1 = r.t01[0:1, :], r.t01[8:9, :]
    r.chip_b_src[...] = (c0 + jnp.exp2(a2c * t0) * c1).astype(BF16)
    swapped = to_mates(r.chip_b_src, r.chips_b)
    u_fd.a1()
    u_fg.a1()
    hot = r.at_cot[...].reshape(D, 128)
    finish(by_gate)
    product_of(r.gr_gate, r.l_nrm, r.b_gate, 0, C)
    u_gate.a0()
    finish(tn_gmo)
    finish(by_out)
    product_of(r.gr_out, r.l_gmo, r.b_out, 0, C)
    u_out.a0()
    swapped()
    for u in u_fu:
        u.a1()
    state = jnp.zeros((N, W), F32)
    for j in range(7, 0, -1):
        state = jnp.where(j > nth, r.chips_b[j].astype(F32) + jnp.exp2(a2c * steps_of(r.chips.at[j])) * state, state)
    later = c1 + jnp.exp2(a2c * t1) * state
    r.st_src[...] = jnp.where(is_first, state, later)
    entering = to_sibling(r.st_src, r.st_sib)
    state = jnp.where(is_first, later, state)
    r.n2[z] = (r.middle[...] + zsummed(r.rs1_src, r.rs3_dst, sent3)).astype(BF16)
    sent_out = zgather(r.n2)
    finish(entering)
    for half, c in enumerate(tiles(C, W)):
        r.gstate[:, c] = jnp.where(core == half, state, r.st_sib[...])

    def rev_second(c):
        a2 = r.nr2[:, c]
        a = r.nr[:, c]

        def body(k, state):
            cr, gl = state
            b = T // 8 - 1 - k
            st = r.step[pl.ds(b * 8, 8), c]
            gs = r.gso[pl.ds(b * 8, 8), c]
            uu = r.u[pl.ds(b * 8, 8), c]
            s1, s2 = [None] * 8, [None] * 8
            for i in range(7, -1, -1):
                t = b * 8 + i
                si, gi, ui = st[i : i + 1, :], gs[i : i + 1, :], uu[i : i + 1, :]
                g = gi * wide(r.Cb[t]) + cr
                s1[i] = jnp.sum(g * wide(r.Bb[t]), axis=0, keepdims=True)
                pr = gi * r.H[t + 1, :, c]
                pe = g * ui
                pr = (pr[:, 0:128] + pr[:, 128:256]) + pr[:, 256:384]
                pe = (pe[:, 0:128] + pe[:, 128:256]) + pe[:, 256:384]
                if c.start:
                    pr = pr + r.PR[t]
                    pe = pe + r.PE[t]
                r.PR[t] = pr
                r.PE[t] = pe
                cr = jnp.exp2(a2 * si) * g
                q = cr * r.H[t, :, c]
                s2[i] = jnp.sum(q * a, axis=0, keepdims=True)
                gl = gl + q * si
            r.gate_in[pl.ds(b * 8, 8), c] = jnp.concatenate(s1, axis=0)
            r.scan_out[pl.ds(b * 8, 8), c] = jnp.concatenate(s2, axis=0)
            return cr, gl

        _, gl = lax.fori_loop(0, T // 8, body, (r.gstate[:, c], jnp.zeros((N, W), F32)))
        r.rows[R : R + N, c] = gl * a

    for c in tiles(C, W):
        rev_second(c)

    ones = jnp.ones((128, 128), BF16)

    for tok in tiles(T, 32):
        pe = dot(r.PE[tok].reshape(32 * N, 128).astype(BF16), ones).reshape(32, N, 128)
        pr = dot(r.PR[tok].reshape(32 * N, 128).astype(BF16), ones).reshape(32, N, 128)
        r.er[tok, :] = jnp.sum(pe * selb[None] + pr * selc[None], axis=1)
    for c in tiles(C, 256):
        inner = r.inner[:, c].astype(F32)
        s1 = r.gate_in[:, c]
        raw_g = (r.scan_out[:, c] + s1 * inner) * jax.nn.sigmoid(r.raw[:, c])
        r.gsr[:, c] = raw_g.astype(BF16)
        r.rows[R + N + 5 : R + N + 6, c] = jnp.sum(raw_g, axis=0, keepdims=True)
        gso = r.gso[:, c]
        r.rows[R + N + 6 : R + N + 7, c] = jnp.sum(gso * inner, axis=0, keepdims=True)
        r.gate_in[:, c] = gso * vec[6:7, c] + s1 * r.step[:, c]
    r.pz[z] = (dot_nt(r.gsr[...], r.w_step[...]) + r.er[...]).astype(BF16)
    summed = zsum(r.pz)
    gy = summed()
    vr = r.proj[...] * r.proj_r[...]
    gn = gy * gains_in
    gpj = (r.proj_r[...] * (gn - vr * by_part(vr * gn))).astype(BF16)
    r.dg[...] = jnp.broadcast_to(jnp.sum(vr * gy, axis=0, keepdims=True), (8, 128))
    for c in tiles(C, 256):
        gi = r.gate_in[:, c] + dot_nt(gpj, r.w_proj[c, :])
        cs = r.conv_sum[:, c]
        sg = jax.nn.sigmoid(cs)
        r.gcs[0:T, c] = gi * (sg * (1.0 + cs * (1.0 - sg)))
    halo = start([rcopy(r.gcs.at[0:8], r.halo2, pair(), gdev(15))])
    for c in tiles(C, 128):
        gc = r.gcs[0:T, c]
        for k in range(4):
            r.rows[R + N + k : R + N + k + 1, c] = jnp.sum(gc * r.ext[5 + k : 5 + k + T, c], axis=0, keepdims=True)
        r.rows[R + N + 4 : R + N + 5, c] = jnp.sum(gc, axis=0, keepdims=True)
    r.rows[0:R, :] = jnp.zeros((R, C), F32)
    r.rows[R + N + 7 : T, :] = jnp.zeros((T - R - N - 7, C), F32)
    chan = (dot(r.gsr[...].T, r.step_in[...]) + r.rows[...].T).reshape(16, 2, 24, 128)
    ll = lax.broadcasted_iota(jnp.int32, (128, 128), 0)
    order = (lax.broadcasted_iota(jnp.int32, (128, 128), 1) == 4 * (2 * (ll & 15) + ((ll >> 4) & 1)) + (ll >> 5)).astype(BF16)
    pt = dot(dot_nt(order, gpj).astype(BF16), r.inner[...])
    for h in range(2):
        r.small[:, h, 24:48, :] = chan[:, h]
        for i in range(4):
            for j in range(6):
                r.small[:, h, i * 6 + j, :] = pt[32 * i + 16 * h : 32 * i + 16 * h + 16, 128 * j : 128 * j + 128]
    by_small = start([rcopy(r.small.at[:, 1 - core], r.small_recv, pair(), sibling)])
    u_fd.a2()
    u_fg.a2()
    for u in u_fu:
        u.a2()
    finish(halo)
    r.gcs[T : T + 8, :] = jnp.where(p == GROUP - 1, 0.0, r.halo2[...])
    for c in tiles(C, 128):
        tot = vec[3:4, c] * r.gcs[0:T, c]
        for k in range(3):
            tot = tot + vec[k : k + 1, c] * r.gcs[3 - k : 3 - k + T, c]
        r.b_in[0:T, c] = tot.astype(BF16)
    by_in = both(r.b_in)
    finish(by_small)
    r.gr_small[...] = (r.small[:, core] + r.small_recv[...]).astype(BF16).reshape(4, 4, SMALL, 128)
    u_small.a0()
    u_out.a1()
    u_gate.a1()
    gip = r.b_in[0:T, :]
    ggi = r.b_gate[0:T, :]
    sent = zscatter(r.rs2_src, r.rs1_dst)
    for j, c in enumerate(tiles(D, 512)):
        gnp = dot_nt(gip, r.w_in[c, :]) + dot_nt(ggi, r.w_gate[c, :])
        r.rs2_src[:, :, c] = fours(gnp)
        if j < 2:
            zsend(sent, r.rs2_src, r.rs1_dst, j)
        r.dn[0:1, c] = jnp.sum(r.tok[:, c].astype(F32) * (r.rinv[:, 0:1] * gnp), axis=0, keepdims=True)
    k4 = lax.broadcasted_iota(jnp.int32, (128, 128), 0)
    hot4 = (lax.broadcasted_iota(jnp.int32, (128, 128), 1) == (k4 & 3)).astype(BF16)
    r.gr_first[...] = jnp.zeros((4, 4, 8, 128), F32)
    for i, v in enumerate((rows_of(r.dn[0:1, :], 48, hot), rows_of(r.dn[1:2, :], 48, hot), rows_of(r.dg[0:1, :] * 0.25, 4, hot4))):
        for h in range(2):
            r.gr_first[:, :, 2 * i + h, :] = v[16 * h : 16 * h + 16, :].reshape(4, 4, 128)
    u_first.a0()
    zsend(sent, r.rs2_src, r.rs1_dst, 2)
    finish(by_in)
    for i in range(2):
        product_of(r.gr_in.at[i], r.l_nrm, r.b_in, 384 * i, 384)
        u_in[i].a0()
    u_fd.b1()
    u_fg.b1()
    u_small.a2()
    u_first.a2()
    gn1 = zsummed(r.rs2_src, r.rs1_dst, sent)
    v = r.tok[own, :].astype(F32)
    rs = lax.rsqrt(jnp.mean(v * v, axis=-1, keepdims=True) + EPS)
    vr = v * rs
    gn = gn1 * g1
    r.gmo[z] = (r.gmid[...] + rs * (gn - vr * jnp.mean(vr * gn, axis=-1, keepdims=True))).astype(BF16)
    sent_tok = zgather(r.gmo)
    u_out.a2()
    u_gate.a2()
    for u in u_in:
        u.a2()
    r.first[...] = u_first.done()[0]
    finish(start([rcopy(r.first, r.first_recv, pair(), sibling)]))
    r.nz2[z] = r.first[...] + r.first_recv[...]
    first = zsum(r.nz2)
    for i in range(2):
        store_out(u_fu[i], 2 * F + 512 * i, 512)
    store_out(u_fd, 0, F)
    store_out(u_fg, F, F)
    r.out_small[0:SMALL, :] = u_small.done()[0]
    store_out(u_out, 3 * F, C)
    store_out(u_gate, 3 * F + C, C)
    for i in range(2):
        store_out(u_in[i], 3 * F + 2 * C + 384 * i, 384)
    r.nz2[z] = first()
    for i in range(3):
        r.out_small[SMALL + i : SMALL + i + 1, :] = r.nz2[z, pl.ds(2 * i + core, 1), :]
    sent_out.wait()
    y_out = pltpu.make_async_copy(r.n2, r.out_y, new())
    y_out.start()
    sent_tok.wait()
    gt_out = pltpu.make_async_copy(r.gmo, r.out_gt, new())
    gt_out.start()
    finish([y_out, gt_out, pltpu.make_async_copy(r.big, r.out_big, leaving)])
    assert len(taken) == SEMS


def V(*shape, dtype=BF16):
    return pltpu.VMEM(shape, dtype)


def V32(*shape):
    return pltpu.VMEM(shape, F32)


def S(*shape):
    return pltpu.SemaphoreType.DMA(shape)


BIG = 3 * F + 3 * C
HBM, VMEM = pl.ANY, pltpu.VMEM
INS = dict(
    in_tok=HBM, in_cot=HBM, in_w_in=HBM, in_w_gate=HBM, in_w_proj=HBM, in_w_step=HBM, in_w_out=HBM, in_w_fg=HBM, in_w_fu=HBM,
    in_w_fd=HBM, in_taps=VMEM, in_cbias=VMEM, in_sbias=VMEM, in_skip=VMEM, in_first=VMEM, in_second=VMEM, in_gains=VMEM, in_rates=VMEM,
)
OUTS = dict(out_y=((4, 32, D), BF16), out_gt=((4, 32, D), BF16), out_big=((48, BIG), F32), out_small=((56, 128), F32))
SCRATCH = dict(
    sem=S(SEMS),
    tok=V(T, D), cot=V(T, D), w_in=V(D, C), w_gate=V(D, C), w_proj=V(C, 128), w_step=V(T, C), w_out=V(C, D), w_fg=V(D, F), w_fu=V(D, F),
    w_fd=V(F, D),
    big=V32(48, BIG), vec=V32(8, C), nr=V32(N, C), nr2=V32(N, C), rinv=V32(T, 128), normed=V(T, D), ext=V32(T + 8, C), halo=V32(8, C),
    gate_in=V32(T, C), conv_sum=V32(T, C), inner=V(T, C),
    pz=V(4, T, 128), proj=V32(T, 128), proj_r=V32(T, 128), pn=V32(T, 128), step_in=V(T, 128),
    raw=V32(T, C), step=V32(T, C), u=V32(T, C), Bb=V32(T, N, 128), Cb=V32(T, N, 128),
    nr2h=V32(2, N, W), pack=V(2, 2 * N, W), pack_sib=V(2 * N, W), chip_src=V(2 * N, W), chips=V(8, 2 * N, W), t01=V32(16, W),
    st_src=V32(N, W), st_sib=V32(N, W),
    pack_b=V(2, N, W), pack_b_sib=V(N, W), chip_b_src=V(N, W), chips_b=V(8, N, W),
    H=V32(T + 1, N, C), scan_out=V32(T, C),
    rs1_src=V(4, 32, D), rs1_dst=V(3, 32, D), rs2_src=V(4, 32, D), rs2_dst=V(3, 32, D),
    rs3_dst=V(3, 32, D),
    middle=V32(32, D), gmid=V32(32, D), n2=V(4, 32, D), gmo=V(4, 32, D),

    gact=V32(T, F), at_cot=V(16, 2, 48, T), at_nrm=V(16, 2, 48, T),
    l_cot=V(16, 48, 2 * T), l_nrm=V(16, 48, 2 * T), l_n2=V(16, 48, 2 * T), l_gmo=V(16, 48, 2 * T),
    b_out=V(2 * T, C), b_act=V(2 * T, F), b_gg=V(2 * T, F), b_gu=V(2 * T, F), b_gate=V(2 * T, C), b_in=V(2 * T, C),
    gr_fd=V(4, 4, 48, F), x_fd=V(6, 2, 48, F), y_fd=V(6, 48, F), gr_fg=V(4, 4, 48, F), x_fg=V(6, 2, 48, F), y_fg=V(6, 48, F),
    gr_fu=V(2, 4, 4, 48, 512), x_fu=V(2, 6, 2, 48, 512), y_fu=V(2, 3, 48, 512),
    gr_out=V(4, 4, 48, C), x_out=V(6, 2, 48, C), y_out=V(3, 48, C), gr_gate=V(4, 4, 48, C), x_gate=V(6, 2, 48, C), y_gate=V(3, 48, C),
    gr_in=V(2, 4, 4, 48, 384), x_in=V(2, 3, 4, 48, 384), y_in=V(2, 3, 48, 384),
    gso=V32(T, C), gstate=V32(N, C), PR=V32(T, N, 128), PE=V32(T, N, 128), rows=V32(T, C), er=V32(T, 128),
    gsr=V(T, C), gcs=V32(T + 8, C), halo2=V32(8, C), dn=V32(8, D), dg=V32(8, 128),
    nz2=V32(4, 8, 128), first=V32(8, 128), first_recv=V32(8, 128), gr_first=V32(4, 4, 8, 128), x_first=V32(3, 4, 8, 128), y_first=V32(3, 8, 128), small=V32(16, 2, SMALL, 128), small_recv=V32(16, SMALL, 128),
    gr_small=V(4, 4, SMALL, 128), x_small=V(3, 4, SMALL, 128), y_small=V(3, SMALL, 128),
)


def local(
    tokens, cotangent, norm_first, in_inner, in_gate, conv_weight, conv_bias, projector, projector_gains, step_weight, step_bias,
    log_rates, skip_gain, out_weight, norm_second, gate_weight, up_weight, down_weight,
):
    y, gt, big, small = pl.pallas_call(
        kernel,
        out_shape=[jax.ShapeDtypeStruct(shape, dtype) for shape, dtype in OUTS.values()],
        in_specs=[pl.BlockSpec(memory_space=m) for m in INS.values()],
        out_specs=[pl.BlockSpec(memory_space=m) for m in (HBM, HBM, HBM, VMEM)],
        scratch_shapes=list(SCRATCH.values()),
        compiler_params=pltpu.CompilerParams(collective_id=0, has_side_effects=True, vmem_limit_bytes=int(63.9 * 2**20)),
    )(
        tokens, cotangent, in_inner, in_gate, projector, step_weight, out_weight, gate_weight, up_weight, down_weight,
        conv_weight, conv_bias, step_bias, skip_gain, norm_first, norm_second, projector_gains, log_rates.T,
    )
    widths = (F, F, F, C, C, C)
    shapes = [(T, D)] * 2 + [(48, w) for w in widths] + [(4, C), (24, R), (N, 24), (4, 24)] + [(1, 24)] * 3 + [(1, 48)] * 2 + [(1, 4)]
    res = pl.pallas_call(
        hand_out,
        out_shape=[jax.ShapeDtypeStruct(sh, F32 if i > 1 else BF16) for i, sh in enumerate(shapes)],
        in_specs=[pl.BlockSpec(memory_space=HBM)] * 4,
        out_specs=[pl.BlockSpec(memory_space=HBM if i < 8 else VMEM) for i in range(len(shapes))],
        scratch_shapes=[V(T, D), V(T, D), V32(48, BIG), V32(56, 128), S(12)],
        compiler_params=pltpu.CompilerParams(vmem_limit_bytes=int(63.9 * 2**20)),
    )(y.reshape(T, D), gt.reshape(T, D), big, small)
    y, gt, fd, fg, fu, out, gate, inn, proj, step_w, rates, taps, cbias, sbias, skip, first, second, gains = res
    return (
        y, gt, first[0], inn, gate, taps, cbias[0], proj.T, gains[0], step_w.T, sbias[0], rates.T, skip[0], out.T, second[0], fg, fu, fd.T,
    )


def hand_out(y, gt, big, small_in, *refs):
    outs, (y_v, gt_v, big_v, small, sem) = refs[:-5], refs[-5:]
    ins = [pltpu.make_async_copy(v, o, sem.at[i]) for i, (v, o) in enumerate(((small_in, small), (big, big_v), (y, y_v), (gt, gt_v)))]
    start(ins)
    parts, at = [], 0
    for o in outs[2:8]:
        parts.append(big_v.at[:, at : at + o.shape[1]])
        at += o.shape[1]
    parts = [pltpu.make_async_copy(v, o, sem.at[4 + i]) for i, (v, o) in enumerate(zip([*parts, y_v, gt_v], [*outs[2:8], *outs[:2]]))]
    finish(ins[1:2])
    start(parts[:6])
    finish(ins[2:])
    start(parts[6:])
    finish(ins[:1])
    proj, step_w, rates, taps, cbias, sbias, skip, first, second, gains = outs[8:]
    for i in range(4):
        for j in range(6):
            proj[i : i + 1, 128 * j : 128 * j + 128] = small[i * 6 + j : i * 6 + j + 1, :]
    step_w[...] = small[24:48, 0:R]
    turned = jnp.concatenate([small[24:48, :], jnp.zeros((104, 128), F32)], axis=0).T
    rates[...] = turned[R : R + N, 0:24]
    taps[...] = turned[R + N : R + N + 4, 0:24]
    for i, o in enumerate((cbias, sbias, skip)):
        o[...] = turned[R + N + 4 + i : R + N + 5 + i, 0:24]
    first[...] = small[48:49, 0:48]
    second[...] = small[49:50, 0:48]
    gains[...] = small[50:51, 0:4]
    finish(parts)


def solution(mesh):
    row, col = P("seq", None), P(None, "head")
    flat, deep = P("head"), P("head", None)
    in_specs = (row, row, P(), col, col, col, flat, deep, P(), col, flat, deep, flat, deep, P(), col, col, deep)
    both, mix = ("head", "seq"), P("seq", "head")
    turned = P("head", "seq")
    out_specs = (
        row, row, P("seq"), mix, mix, P(None, both), P(both), turned, P("seq"), P(None, both), P(both), P(both, None), P(both),
        turned, P("seq"), mix, mix, turned,
    )
    return jax.shard_map(local, mesh=mesh, in_specs=in_specs, out_specs=out_specs, check_vma=False)
```

```python
import types

import jax
import jax.numpy as jnp
from jax import lax
from jax.experimental import pallas as pl
from jax.experimental.pallas import tpu as pltpu
from jax.sharding import PartitionSpec as P

F32 = jnp.float32
BF16 = jnp.bfloat16
T, D, C, F, N, R = 128, 1536, 768, 1024, 16, 96
GROUP = 16
EPS = 1e-5
LOG2E = 1.4426950408889634
HIGH = lax.Precision.HIGHEST
MESH = pl.DeviceIdType.MESH
SMALL = 48
SEMS = 137
W = 384


def dot(a, b, precision=None):
    return jnp.dot(a, b, precision=precision, preferred_element_type=F32)


def dot_nt(a, b, precision=None):
    return lax.dot_general(a, b, (((1,), (1,)), ((), ())), precision=precision, preferred_element_type=F32)


def tiles(total, width):
    return [slice(i, i + width) for i in range(0, total, width)]


def wide(v):
    return jnp.concatenate([v] * (W // 128), axis=1)


def rcopy(src, dst, sems, device):
    return pltpu.make_async_remote_copy(
        src_ref=src, dst_ref=dst, send_sem=sems[0], recv_sem=sems[1], device_id=device, device_id_type=MESH
    )


def start(copies):
    for c in copies:
        c.start()
    return copies


def finish(copies):
    for c in copies:
        c.wait()


class Burst:
    def __init__(self, sems, src, dst, device):
        self.sems, self.all = sems, rcopy(src, dst, sems, device)

    def send(self, src, dst, device):
        rcopy(src, dst, self.sems, device).start()

    def wait(self):
        self.all.wait()


class Ring:
    def __init__(self, part, land, two, four, new, place, at):
        self.part, self.land, self.at, self.me = part, land, at, place
        self.right, self.left, self.far = lax.rem(place + 1, 4), lax.rem(place + 3, 4), lax.rem(place + 2, 4)
        self.first = Burst(new(), two, two, at(self.right))
        self.rest = Burst(new(), four, four, at(self.right))

    def begin(self):
        part, land, at, right, left, far = self.part, self.land, self.at, self.right, self.left, self.far
        self.first.send(part(far, 0), land(0, 0), at(right))
        self.first.send(part(far, 1), land(1, 1), at(left))
        self.rest.send(part(right, 1), land(2, 1), at(right))
        self.rest.send(part(left, 0), land(3, 0), at(left))

    def pass_on(self):
        self.first.wait()
        for h, d in enumerate((self.right, self.left)):
            own = self.part(d, h)
            own[...] = (own[...].astype(F32) + self.land(h, h)[...].astype(F32)).astype(own.dtype)
            self.rest.send(own, self.land(4 + h, h), self.at(d))

    def totals(self):
        self.rest.wait()
        for h, (a, b) in enumerate(((4, 3), (5, 2))):
            own = self.part(self.me, h)
            yield own, own[...].astype(F32) + (self.land(a, h)[...].astype(F32) + self.land(b, h)[...].astype(F32))


class Straight:
    def __init__(self, part, land, new, place, at):
        self.part, self.land, self.at, self.me = part, land, at, place
        self.burst = Burst(new(), land, land, at(lax.rem(place + 1, 4)))

    def begin(self):
        for k in (2, 1, 3):
            d = lax.rem(self.me + k, 4)
            self.burst.send(self.part(d), self.land.at[k - 1], self.at(d))

    def totals(self):
        self.burst.wait()
        own, land = self.part(self.me), self.land
        yield own, own[...].astype(F32) + ((land[0].astype(F32) + land[2].astype(F32)) + land[1].astype(F32))


class Unit:
    def __init__(self, grid, land_one, land_two, new, x, y, at, x_first, both_ways, split=0):
        along_x, along_y = (x, lambda d: at(d, y)), (y, lambda d: at(x, d))
        one, two = (along_x, along_y) if x_first else (along_y, along_x)

        def chunk(d, half=slice(0, 4)):
            return grid.at[half, d] if x_first else grid.at[d, half]

        def piece(d):
            return grid.at[d, x] if x_first else grid.at[y, d]

        if both_ways:
            self.one = Ring(
                lambda d, h: chunk(d, slice(2 * h, 2 * h + 2)), lambda i, h: land_one.at[i], land_one.at[0:2], land_one.at[2:6], new, *one
            )
        else:
            self.one = Straight(chunk, land_one, new, *one)
        if split:

            def side(ref, h):
                return ref.at[:, split:] if h else ref.at[:, 0:split]

            self.two = Ring(
                lambda d, h: side(piece(d), h), lambda i, h: side(land_two.at[i], h), land_two.at[0], land_two.at[0:2], new, *two
            )
        else:
            self.two = Straight(piece, land_two, new, *two)

    def a0(self):
        self.one.begin()

    def a1(self):
        self.one.pass_on()

    def add(self):
        for own, v in self.one.totals():
            own[...] = v.astype(own.dtype)

    def a2(self):
        self.add()
        self.two.begin()

    def b1(self):
        self.two.pass_on()

    def done(self):
        return [v for _, v in self.two.totals()]


def kernel(*refs):
    r = types.SimpleNamespace(**dict(zip([*INS, *OUTS, *SCRATCH], refs, strict=True)))
    s = lax.axis_index("seq")
    z = lax.axis_index("head")
    p = lax.rem(s, GROUP)
    base = s - p
    core = lax.rem(s, 2)
    x = lax.rem(s // 2, 4)
    y = s // 8

    def zdev(k):
        return (s, lax.rem(z + k, 4))

    def gdev(k):
        return (base + lax.rem(p + k, GROUP), z)

    def chip(cx, cy):
        return (cy * 8 + cx * 2 + core, z)

    sibling = (s + 1 - 2 * core, z)
    taken = []

    def new():
        taken.append(0)
        return r.sem.at[len(taken) - 1]

    def pair():
        return new(), new()

    barrier = pltpu.get_barrier_semaphore()
    for k in range(1, 4):
        pl.semaphore_signal(barrier, 1, device_id=zdev(k), device_id_type=MESH)

    mates = sorted(((dy + min(dx, 4 - dx), dy, dx) for dy in range(2) for dx in range(4)), reverse=True)[:7]

    def mate(dy, dx):
        return base + lax.rem(y + dy, 2) * 8 + lax.rem(x + dx, 4) * 2 + core

    others = [(mate(dy, dx), z) for _, dy, dx in mates]
    for device in (*others, sibling, gdev(15 - 14 * core), (s + 8 * (3 - 2 * y), z)):
        pl.semaphore_signal(barrier, 1, device_id=device, device_id_type=MESH)

    def load(src, dst):
        c = pltpu.make_async_copy(src, dst, new())
        c.start()
        return c

    ld_tok = load(r.in_tok, r.tok)
    ld_in = load(r.in_w_in, r.w_in)
    ld_gate = load(r.in_w_gate, r.w_gate)
    ld_cot = load(r.in_cot, r.cot)
    ld_fd = load(r.in_w_fd, r.w_fd)
    ld_proj = load(r.in_w_proj, r.w_proj)
    r.w_step[...] = jnp.zeros((T, C), BF16)
    ld_step = load(r.in_w_step, r.w_step.at[0:R])
    ld_out = load(r.in_w_out, r.w_out)
    ld_fg = load(r.in_w_fg, r.w_fg)
    ld_fu = load(r.in_w_fu, r.w_fu)

    vec = r.vec
    vec[0:4, :] = r.in_taps[...]
    for i, v in enumerate((r.in_cbias, r.in_sbias, r.in_skip)):
        vec[4 + i : 5 + i, :] = v[...].reshape(1, C)
    g1 = r.in_first[...].reshape(1, D)
    g2 = r.in_second[...].reshape(1, D)
    nr = -jnp.exp(r.in_rates[...])
    r.nr[...] = nr
    nr2 = nr * LOG2E
    r.nr2[...] = nr2
    for j, c in enumerate(tiles(C, W)):
        r.nr2h[j] = nr2[:, c]

    ld_tok.wait()
    for rows in tiles(T, 32):
        v = r.tok[rows, :].astype(F32)
        rs = lax.rsqrt(jnp.mean(v * v, axis=-1, keepdims=True) + EPS)
        r.rinv[rows, :] = jnp.broadcast_to(rs, (32, 128))
        r.normed[rows, :] = (v * rs * g1).astype(BF16)
    ld_in.wait()
    nrm = r.normed[...]
    for c in tiles(C, 256):
        r.ext[8 : 8 + T, c] = dot(nrm, r.w_in[:, c]).astype(BF16).astype(F32)
    pl.semaphore_wait(barrier, 3 + 7 + 3)
    halo = start([rcopy(r.ext.at[T : T + 8], r.halo, pair(), gdev(1))])
    ld_gate.wait()
    for c in tiles(C, 256):
        r.gate_in[:, c] = dot(nrm, r.w_gate[:, c])

    def turned(value, at, lhs):
        at[...] = value.T.reshape(16, 2, 48, T)
        lhs[:, :, 0:T] = at[:, core]
        return start([rcopy(at.at[:, 1 - core], lhs.at[:, :, T : 2 * T], pair(), sibling)])

    def both(b):
        return start([rcopy(b.at[0:T], b.at[T : 2 * T], pair(), sibling)])

    finish(halo)
    r.ext[0:8, :] = jnp.where(p == 0, 0.0, r.halo[...])
    for c in tiles(C, 128):
        tot = vec[4:5, c] + vec[0:1, c] * r.ext[5 : 5 + T, c]
        for k in range(1, 4):
            tot = tot + vec[k : k + 1, c] * r.ext[5 + k : 5 + k + T, c]
        r.conv_sum[:, c] = tot
        r.inner[:, c] = (tot * jax.nn.sigmoid(tot)).astype(BF16)

    def zgather(buf):
        burst = Burst(pair(), buf.at[0:3], buf.at[0:3], zdev(1))
        for k in (2, 1, 3):
            burst.send(buf.at[z], buf.at[z], zdev(k))
        return burst

    def zsum(buf):
        burst = zgather(buf)

        def result():
            burst.wait()
            return (buf[0].astype(F32) + buf[1].astype(F32)) + (buf[2].astype(F32) + buf[3].astype(F32))

        return result

    ld_proj.wait()
    r.pz[z] = dot(r.inner[...], r.w_proj[...]).astype(BF16)
    projected = zsum(r.pz)

    ld_cot.wait()
    ld_fd.wait()
    cot = r.cot[...]
    for c in tiles(F, 256):
        r.gact[:, :, c] = dot_nt(cot, r.w_fd[c, :]).reshape(4, 32, 256)

    tn_cot = turned(cot, r.at_cot, r.l_cot)
    tn_nrm = turned(nrm, r.at_nrm, r.l_nrm)

    proj = projected()
    r.proj[...] = proj
    lane = lax.broadcasted_iota(jnp.int32, (1, 128), 1)
    m1 = (lane < R).astype(F32)
    m3 = (lane >= R + N).astype(F32)
    m2 = 1.0 - m1 - m3

    def by_part(v):
        return (
            m1 * (jnp.sum(v * m1, -1, keepdims=True) / R)
            + m2 * (jnp.sum(v * m2, -1, keepdims=True) / N)
            + m3 * (jnp.sum(v * m3, -1, keepdims=True) / N)
        )

    rr = lax.rsqrt(by_part(proj * proj) + EPS)
    r.proj_r[...] = rr
    gains_in = r.in_gains[...].reshape(1, 128)
    pn = proj * rr * gains_in
    r.pn[...] = pn
    step_in = (pn * m1).astype(BF16)
    r.step_in[...] = step_in
    ld_step.wait()
    for c in tiles(C, 256):
        raw = dot(step_in, r.w_step[:, c]) + vec[5:6, c]
        r.raw[:, c] = raw
        st = jnp.maximum(raw, 0.0) + jnp.log1p(jnp.exp(-jnp.abs(raw)))
        r.step[:, c] = st
        r.u[:, c] = st * r.inner[:, c].astype(F32)
    rown = lax.broadcasted_iota(jnp.int32, (N, 128), 0)
    lanes = lax.broadcasted_iota(jnp.int32, (N, 128), 1)
    selb = (lanes == rown + R).astype(F32)
    selc = (lanes == rown + R + N).astype(F32)
    sel = selb + selc
    part_of = lax.broadcasted_iota(jnp.int32, (128, 256), 0) - jnp.where(lax.broadcasted_iota(jnp.int32, (128, 256), 1) < 128, R, R + N)
    to_lanes = ((part_of >= 0) & (part_of < N)).astype(BF16)

    for rows in tiles(T, 32):
        some = r.pn[rows, :]
        one = jnp.concatenate([jnp.broadcast_to(some[i : i + 1, :], (N, 128)) * sel for i in range(32)], axis=0)
        high = one.astype(BF16)
        low = (one - high.astype(F32)).astype(BF16)
        v = dot(high, to_lanes) + dot(low, to_lanes)
        r.Bb[rows] = v[:, 0:128].reshape(32, N, 128)
        r.Cb[rows] = v[:, 128:256].reshape(32, N, 128)

    top = lax.broadcasted_iota(jnp.int32, (N, W), 0) < 8

    def coded(ref, h, tot):
        high = tot.astype(BF16).astype(F32)
        ref[0:N, :] = h.astype(BF16)
        ref[N : 2 * N, :] = jnp.where(top, high, tot - high).astype(BF16)

    def state_of(ref):
        return ref[0:N, :].astype(F32)

    def steps_of(ref):
        v = ref[N : 2 * N, :].astype(F32)
        return v[0:1, :] + v[8:9, :]

    for half, c in enumerate(tiles(C, W)):
        a2 = r.nr2[:, c]

        def first(b, h):
            st = r.step[pl.ds(b * 8, 8), c]
            uu = r.u[pl.ds(b * 8, 8), c]
            for i in range(8):
                h = jnp.exp2(a2 * st[i : i + 1, :]) * h + uu[i : i + 1, :] * wide(r.Bb[b * 8 + i])
            return h

        h = lax.fori_loop(0, T // 8, first, jnp.zeros((N, W), F32))
        coded(r.pack.at[half], h, jnp.sum(r.step[:, c], axis=0, keepdims=True))

    nth = p // 2
    is_first = core == 0
    a2c = r.nr2h[core]

    def to_mates(src, land):
        burst = Burst(pair(), land.at[0:7], land.at[0:7], sibling)
        for device in others:
            burst.send(src, land.at[nth], device)
        land[nth] = src[...]
        return burst.wait

    def to_sibling(src, dst):
        return start([rcopy(src, dst, pair(), sibling)])

    finish(to_sibling(r.pack.at[1 - core], r.pack_sib))
    h_own, h_sib = state_of(r.pack.at[core]), state_of(r.pack_sib)
    t_own, t_sib = steps_of(r.pack.at[core]), steps_of(r.pack_sib)
    h0, h1 = jnp.where(is_first, h_own, h_sib), jnp.where(is_first, h_sib, h_own)
    t0, t1 = jnp.where(is_first, t_own, t_sib), jnp.where(is_first, t_sib, t_own)
    r.t01[0:1, :] = t0
    r.t01[8:9, :] = t1
    coded(r.chip_src, jnp.exp2(a2c * t1) * h0 + h1, t0 + t1)
    swapped = to_mates(r.chip_src, r.chips)
    ld_fu.wait()
    for c in tiles(F, 256):
        r.w_fd[c, :] = r.w_fu[:, c].T
    finish(tn_cot)
    finish(tn_nrm)
    swapped()
    state = jnp.zeros((N, W), F32)
    for j in range(7):
        at = r.chips.at[j]
        state = jnp.where(j < nth, jnp.exp2(a2c * steps_of(at)) * state + state_of(at), state)
    later = jnp.exp2(a2c * t0) * state + h0
    r.st_src[...] = jnp.where(is_first, later, state)
    entering = to_sibling(r.st_src, r.st_sib)
    state = jnp.where(is_first, state, later)
    finish(entering)
    for half, c in enumerate(tiles(C, W)):
        r.H[0, :, c] = jnp.where(core == half, state, r.st_sib[...])

    eights = (lax.broadcasted_iota(jnp.int32, (16, 128), 1) // 8 == lax.broadcasted_iota(jnp.int32, (16, 128), 0)).astype(BF16)

    def folded(v):
        return v[0:8, :] + v[8:16, :]

    def finished(part, out):
        for j in range(8):
            out[16 * j : 16 * j + 16, :] = dot(eights, part[128 * j : 128 * j + 128, :])

    for c in tiles(C, W):
        a2 = r.nr2[:, c]

        def second(b, h):
            st = r.step[pl.ds(b * 8, 8), c]
            uu = r.u[pl.ds(b * 8, 8), c]
            rows = []
            for i in range(8):
                h = jnp.exp2(a2 * st[i : i + 1, :]) * h + uu[i : i + 1, :] * wide(r.Bb[b * 8 + i])
                r.H[b * 8 + i + 1, :, c] = h
                rows.append(folded(h * wide(r.Cb[b * 8 + i])))
            r.part_one[pl.ds(pl.multiple_of(b * 64, 64), 64), c] = jnp.concatenate(rows, axis=0).astype(BF16)
            return h

        lax.fori_loop(0, T // 8, second, r.H[0, :, c])

    finished(r.part_one, r.scan_out)
    for c in tiles(C, 128):
        so = r.scan_out[:, c] + vec[6:7, c] * r.inner[:, c].astype(F32)
        r.scan_out[:, c] = so
        gi = r.gate_in[:, c]
        r.b_out[0:T, c] = (so * (gi * jax.nn.sigmoid(gi))).astype(BF16)
    by_out = both(r.b_out)

    def zscatter(src, dst):
        return Burst(pair(), src.at[0:3], dst, zdev(1))

    def zsend(burst, src, dst, j):
        c = slice(512 * j, 512 * j + 512)
        for k in (2, 1, 3):
            burst.send(src.at[lax.rem(z + k, 4), :, c], dst.at[k - 1, :, c], zdev(k))

    def zsummed(src, dst, burst):
        burst.wait()
        return (src[z].astype(F32) + dst[0].astype(F32)) + (dst[1].astype(F32) + dst[2].astype(F32))

    def fours(v):
        return v.astype(BF16).reshape(4, 32, v.shape[-1])

    ld_out.wait()
    own = pl.ds(pl.multiple_of(z * 32, 32), 32)
    halves = tiles(32, 16)
    mixed = r.b_out[0:T, :].reshape(4, 32, C)
    sent = []
    for hs in halves:
        some = mixed[:, hs].reshape(64, C)
        for c in tiles(D, 512):
            r.rs1_src[:, hs, c] = dot(some, r.w_out[:, c]).astype(BF16).reshape(4, 16, 512)
        burst = Burst(pair(), r.rs1_src.at[0:3, hs], r.rs1_dst.at[:, hs], zdev(1))
        for k in (2, 1, 3):
            burst.send(r.rs1_src.at[lax.rem(z + k, 4), hs], r.rs1_dst.at[k - 1, hs], zdev(k))
        sent.append(burst)
    gathered = []
    for hs, burst in zip(halves, sent):
        burst.wait()
        terms = [r.rs1_src[z, hs], *(r.rs1_dst[k, hs] for k in range(3))]
        rows = pl.ds(pl.multiple_of(z * 32 + hs.start, 16), 16)
        middle = r.tok[rows, :].astype(F32) + sum((v.astype(F32) for v in terms[1:]), terms[0].astype(F32))
        r.middle[hs, :] = middle
        r2 = lax.rsqrt(jnp.mean(middle * middle, axis=-1, keepdims=True) + EPS)
        r.n2[z, hs] = (middle * r2 * g2).astype(BF16)
        burst = Burst(pair(), r.n2.at[0:3, hs], r.n2.at[0:3, hs], zdev(1))
        for k in (2, 1, 3):
            burst.send(r.n2.at[z, hs], r.n2.at[z, hs], zdev(k))
        gathered.append(burst)

    def unit(grid, land_one, land_two, x_first, both_ways=True, split=0):
        return Unit(grid, land_one, land_two, pair, x, y, chip, x_first, both_ways, split)

    def product_of(grid, lhs, b, lo, n):
        left = lhs[...].reshape(D // 2, 2 * T)
        for c in tiles(n, 256 if n % 256 == 0 else 128):
            cols = slice(lo + c.start, lo + c.stop)
            grid[:, :, :, c] = dot(left, b[:, cols]).astype(BF16).reshape(4, 4, 48, c.stop - c.start)

    leaving = new()

    def store_out(u, lo, n):
        c = slice(lo, lo + n)
        at = lo
        for v in u.done():
            r.big[:, at : at + v.shape[1]] = v
            at += v.shape[1]
        pltpu.make_async_copy(r.big.at[:, c], r.out_big.at[:, c], leaving).start()

    u_fd = unit(r.gr_fd, r.x_fd, r.y_fd, True, split=F // 2)
    u_fg = unit(r.gr_fg, r.x_fg, r.y_fg, False, split=F // 2)
    u_fu = [unit(r.gr_fu.at[i], r.x_fu.at[i], r.y_fu.at[i], i == 0) for i in range(2)]
    u_out = unit(r.gr_out, r.x_out, r.y_out, True)
    u_gate = unit(r.gr_gate, r.x_gate, r.y_gate, False)
    u_in = [unit(r.gr_in.at[i], r.x_in.at[i], r.y_in.at[i], i == 0, False) for i in range(2)]
    u_small = unit(r.gr_small, r.x_small, r.y_small, True, False)
    u_first = unit(r.gr_first, r.x_first, r.y_first, False, False)

    ld_fg.wait()
    for hs, burst in zip(halves, gathered):
        burst.wait()
        some = r.n2[:, hs].reshape(64, D)
        for c in tiles(F, 256):
            g = dot(some, r.w_fg[:, c])
            u = dot(some, r.w_fu[:, c])
            ga = r.gact[:, hs, c].reshape(64, 256)
            sg = jax.nn.sigmoid(g)
            sl = g * sg
            for b, v in ((r.b_act, sl * u), (r.b_gg, ga * u * (sg * (1.0 + g * (1.0 - sg)))), (r.b_gu, ga * sl)):
                v = v.astype(BF16)
                for q in range(4):
                    b[32 * q + hs.start : 32 * q + hs.stop, c] = v[16 * q : 16 * q + 16, :]
    n2 = r.n2[...].reshape(T, D)
    by_act = both(r.b_act)
    gg = r.b_gg[0:T, :]
    gu = r.b_gu[0:T, :]
    sent = zscatter(r.rs2_src, r.rs2_dst)
    for j, c in enumerate(tiles(D, 512)):
        r.rs2_src[:, :, c] = fours(dot_nt(gg, r.w_fg[c, :]) + dot(gu, r.w_fd[:, c]))
        zsend(sent, r.rs2_src, r.rs2_dst, j)
        if j == 1:
            finish(by_act)
            product_of(r.gr_fd, r.l_cot, r.b_act, 0, F)
            u_fd.a0()
    ld_fd = load(r.in_w_fd, r.w_fd)
    by_gg = both(r.b_gg)
    by_gu = both(r.b_gu)
    tn_n2 = turned(n2, r.at_cot, r.l_n2)

    finish(tn_n2)
    finish(by_gg)
    product_of(r.gr_fg, r.l_n2, r.b_gg, 0, F)
    u_fg.a0()
    finish(by_gu)
    for i in range(2):
        product_of(r.gr_fu.at[i], r.l_n2, r.b_gu, 512 * i, 512)
        u_fu[i].a0()

    gy = zsummed(r.rs2_src, r.rs2_dst, sent)
    v = r.middle[...]
    r2 = lax.rsqrt(jnp.mean(v * v, axis=-1, keepdims=True) + EPS)
    vr = v * r2
    gn = gy * g2
    gm = r.cot[own, :].astype(F32) + r2 * (gn - vr * jnp.mean(vr * gn, axis=-1, keepdims=True))
    r.gmid[...] = gm
    r.gmo[z] = gm.astype(BF16)
    got = zgather(r.gmo)
    r.dn[1:2, :] = jnp.sum(vr * gy, axis=0, keepdims=True)
    act = r.b_act[0:T, :]
    ld_fd.wait()
    sent3 = zscatter(r.rs1_src, r.rs3_dst)
    for j, c in enumerate(tiles(D, 512)):
        r.rs1_src[:, :, c] = fours(dot(act, r.w_fd[:, c]))
        zsend(sent3, r.rs1_src, r.rs3_dst, j)

    def owner(shape):
        i = lax.broadcasted_iota(jnp.int32, shape, 0)
        return 2 * (i & 15) + (i >> 4)

    def rows_of(v, width, hot):
        k = lax.broadcasted_iota(jnp.int32, (32, v.shape[1]), 1) - width * owner((32, v.shape[1]))
        one = jnp.where((k >= 0) & (k < width), v, 0.0)
        high = one.astype(BF16)
        return dot(high, hot) + dot((one - high.astype(F32)).astype(BF16), hot)

    kk = lax.broadcasted_iota(jnp.int32, (D, 128), 0)
    hot = lax.broadcasted_iota(jnp.int32, (D, 128), 1) == kk - 48 * ((kk * 683) >> 15)
    r.at_cot[...] = hot.astype(BF16).reshape(16, 2, 48, T)
    got.wait()

    gmo = r.gmo[...].reshape(T, D)
    for c in tiles(C, 256):
        gmx = dot_nt(gmo, r.w_out[c, :])
        gi = r.gate_in[:, c]
        sg = jax.nn.sigmoid(gi)
        r.gso[:, c] = gmx * (gi * sg)
        r.b_gate[0:T, c] = (gmx * r.scan_out[:, c] * (sg * (1.0 + gi * (1.0 - sg)))).astype(BF16)
    by_gate = both(r.b_gate)
    tn_gmo = turned(gmo, r.at_nrm, r.l_gmo)

    def rev_first(c):
        a2 = r.nr2[:, c]

        def body(k, cr):
            b = T // 8 - 1 - k
            st = r.step[pl.ds(b * 8, 8), c]
            gs = r.gso[pl.ds(b * 8, 8), c]
            for i in range(7, -1, -1):
                cr = jnp.exp2(a2 * st[i : i + 1, :]) * (gs[i : i + 1, :] * wide(r.Cb[b * 8 + i]) + cr)
            return cr

        cr = lax.fori_loop(0, T // 8, body, jnp.zeros((N, W), F32))
        r.pack_b[0 if c.start == 0 else 1] = cr.astype(BF16)

    for c in tiles(C, W):
        rev_first(c)
    finish(to_sibling(r.pack_b.at[1 - core], r.pack_b_sib))
    c_own, c_sib = r.pack_b[core].astype(F32), r.pack_b_sib[...].astype(F32)
    c0, c1 = jnp.where(is_first, c_own, c_sib), jnp.where(is_first, c_sib, c_own)
    t0, t1 = r.t01[0:1, :], r.t01[8:9, :]
    r.chip_b_src[...] = (c0 + jnp.exp2(a2c * t0) * c1).astype(BF16)
    swapped = to_mates(r.chip_b_src, r.chips_b)
    u_fd.a1()
    u_fg.a1()
    hot = r.at_cot[...].reshape(D, 128)
    finish(by_gate)
    product_of(r.gr_gate, r.l_nrm, r.b_gate, 0, C)
    u_gate.a0()
    finish(tn_gmo)
    finish(by_out)
    product_of(r.gr_out, r.l_gmo, r.b_out, 0, C)
    u_out.a0()

    def read_rows(b, carry):
        gs = r.gso[pl.ds(b * 8, 8), :]
        for i in range(8):
            pr = gs[i : i + 1, :] * r.H[b * 8 + i + 1]
            r.PR[b * 8 + i] = sum((pr[:, k] for k in tiles(C, 128)[1:]), pr[:, 0:128])
        return carry

    lax.fori_loop(0, T // 8, read_rows, 0)
    for c in tiles(C, 256):
        r.w_out[c, :] = r.w_gate[:, c].T
    swapped()
    for u in u_fu:
        u.a1()
    state = jnp.zeros((N, W), F32)
    for j in range(7, 0, -1):
        state = jnp.where(j > nth, r.chips_b[j].astype(F32) + jnp.exp2(a2c * steps_of(r.chips.at[j])) * state, state)
    later = c1 + jnp.exp2(a2c * t1) * state
    r.st_src[...] = jnp.where(is_first, state, later)
    entering = to_sibling(r.st_src, r.st_sib)
    state = jnp.where(is_first, later, state)
    r.n2[z] = (r.middle[...] + zsummed(r.rs1_src, r.rs3_dst, sent3)).astype(BF16)
    sent_out = zgather(r.n2)
    finish(entering)
    for half, c in enumerate(tiles(C, W)):
        r.gstate[:, c] = jnp.where(core == half, state, r.st_sib[...])

    def rev_second(c):
        a2 = r.nr2[:, c]
        a = r.nr[:, c]

        def body(k, state):
            cr, gl = state
            b = T // 8 - 1 - k
            st = r.step[pl.ds(b * 8, 8), c]
            gs = r.gso[pl.ds(b * 8, 8), c]
            uu = r.u[pl.ds(b * 8, 8), c]
            s1, s2 = [None] * 8, [None] * 8
            for i in range(7, -1, -1):
                t = b * 8 + i
                si, gi, ui = st[i : i + 1, :], gs[i : i + 1, :], uu[i : i + 1, :]
                g = gi * wide(r.Cb[t]) + cr
                s1[i] = folded(g * wide(r.Bb[t]))
                pe = g * ui
                pe = (pe[:, 0:128] + pe[:, 128:256]) + pe[:, 256:384]
                if c.start:
                    pe = pe + r.PE[t]
                r.PE[t] = pe
                cr = jnp.exp2(a2 * si) * g
                q = cr * r.H[t, :, c]
                s2[i] = folded(q * a)
                gl = gl + q * si
            rows = pl.ds(pl.multiple_of(b * 64, 64), 64)
            r.part_one[rows, c] = jnp.concatenate(s1, axis=0).astype(BF16)
            r.part_two[rows, c] = jnp.concatenate(s2, axis=0).astype(BF16)
            return cr, gl

        _, gl = lax.fori_loop(0, T // 8, body, (r.gstate[:, c], jnp.zeros((N, W), F32)))
        r.rows[R : R + N, c] = gl * a

    for c in tiles(C, W):
        rev_second(c)
    finished(r.part_one, r.gate_in)
    finished(r.part_two, r.scan_out)

    ones = jnp.ones((128, 128), BF16)

    for tok in tiles(T, 32):
        pe = dot(r.PE[tok].reshape(32 * N, 128).astype(BF16), ones).reshape(32, N, 128)
        pr = dot(r.PR[tok].reshape(32 * N, 128).astype(BF16), ones).reshape(32, N, 128)
        r.er[tok, :] = jnp.sum(pe * selb[None] + pr * selc[None], axis=1)
    for c in tiles(C, 256):
        inner = r.inner[:, c].astype(F32)
        s1 = r.gate_in[:, c]
        raw_g = (r.scan_out[:, c] + s1 * inner) * jax.nn.sigmoid(r.raw[:, c])
        r.gsr[:, c] = raw_g.astype(BF16)
        r.rows[R + N + 5 : R + N + 6, c] = jnp.sum(raw_g, axis=0, keepdims=True)
        gso = r.gso[:, c]
        r.rows[R + N + 6 : R + N + 7, c] = jnp.sum(gso * inner, axis=0, keepdims=True)
        r.gate_in[:, c] = gso * vec[6:7, c] + s1 * r.step[:, c]
    r.pz[z] = (dot_nt(r.gsr[...], r.w_step[...]) + r.er[...]).astype(BF16)
    summed = zsum(r.pz)
    for c in tiles(C, 256):
        r.w_fd[c, :] = r.w_in[:, c].T
    u_out.a1()
    u_gate.a1()
    gy = summed()
    vr = r.proj[...] * r.proj_r[...]
    gn = gy * gains_in
    gpj = (r.proj_r[...] * (gn - vr * by_part(vr * gn))).astype(BF16)
    r.dg[...] = jnp.broadcast_to(jnp.sum(vr * gy, axis=0, keepdims=True), (8, 128))
    for c in tiles(C, 256):
        gi = r.gate_in[:, c] + dot_nt(gpj, r.w_proj[c, :])
        cs = r.conv_sum[:, c]
        sg = jax.nn.sigmoid(cs)
        r.gcs[0:T, c] = gi * (sg * (1.0 + cs * (1.0 - sg)))
    halo = start([rcopy(r.gcs.at[0:8], r.halo2, pair(), gdev(15))])
    for c in tiles(C, 128):
        gc = r.gcs[0:T, c]
        for k in range(4):
            r.rows[R + N + k : R + N + k + 1, c] = jnp.sum(gc * r.ext[5 + k : 5 + k + T, c], axis=0, keepdims=True)
        r.rows[R + N + 4 : R + N + 5, c] = jnp.sum(gc, axis=0, keepdims=True)
    r.rows[0:R, :] = jnp.zeros((R, C), F32)
    r.rows[R + N + 7 : T, :] = jnp.zeros((T - R - N - 7, C), F32)
    chan = (dot(r.gsr[...].T, r.step_in[...]) + r.rows[...].T).reshape(16, 2, 24, 128)
    ll = lax.broadcasted_iota(jnp.int32, (128, 128), 0)
    order = (lax.broadcasted_iota(jnp.int32, (128, 128), 1) == 4 * (2 * (ll & 15) + ((ll >> 4) & 1)) + (ll >> 5)).astype(BF16)
    pt = dot(dot_nt(order, gpj).astype(BF16), r.inner[...])
    for h in range(2):
        r.small[:, h, 24:48, :] = chan[:, h]
        for i in range(4):
            for j in range(6):
                r.small[:, h, i * 6 + j, :] = pt[32 * i + 16 * h : 32 * i + 16 * h + 16, 128 * j : 128 * j + 128]
    by_small = start([rcopy(r.small.at[:, 1 - core], r.small_recv, pair(), sibling)])
    u_fd.a2()
    u_fg.a2()
    for u in u_fu:
        u.a2()
    finish(halo)
    r.gcs[T : T + 8, :] = jnp.where(p == GROUP - 1, 0.0, r.halo2[...])
    for c in tiles(C, 128):
        tot = vec[3:4, c] * r.gcs[0:T, c]
        for k in range(3):
            tot = tot + vec[k : k + 1, c] * r.gcs[3 - k : 3 - k + T, c]
        r.b_in[0:T, c] = tot.astype(BF16)
    by_in = both(r.b_in)
    finish(by_small)
    r.gr_small[...] = (r.small[:, core] + r.small_recv[...]).astype(BF16).reshape(4, 4, SMALL, 128)
    u_small.a0()
    gip = r.b_in[0:T, :]
    ggi = r.b_gate[0:T, :]
    sent = zscatter(r.rs2_src, r.rs1_dst)
    for j, c in enumerate(tiles(D, 512)):
        gnp = dot(gip, r.w_fd[0:C, c]) + dot(ggi, r.w_out[:, c])
        r.rs2_src[:, :, c] = fours(gnp)
        if j < 2:
            zsend(sent, r.rs2_src, r.rs1_dst, j)
        r.dn[0:1, c] = jnp.sum(r.tok[:, c].astype(F32) * (r.rinv[:, 0:1] * gnp), axis=0, keepdims=True)
    k4 = lax.broadcasted_iota(jnp.int32, (128, 128), 0)
    hot4 = (lax.broadcasted_iota(jnp.int32, (128, 128), 1) == (k4 & 3)).astype(BF16)
    r.gr_first[...] = jnp.zeros((4, 4, 8, 128), F32)
    for i, v in enumerate((rows_of(r.dn[0:1, :], 48, hot), rows_of(r.dn[1:2, :], 48, hot), rows_of(r.dg[0:1, :] * 0.25, 4, hot4))):
        for h in range(2):
            r.gr_first[:, :, 2 * i + h, :] = v[16 * h : 16 * h + 16, :].reshape(4, 4, 128)
    u_first.a0()
    zsend(sent, r.rs2_src, r.rs1_dst, 2)
    finish(by_in)
    for i in range(2):
        product_of(r.gr_in.at[i], r.l_nrm, r.b_in, 384 * i, 384)
        u_in[i].a0()
    u_fd.b1()
    u_fg.b1()
    u_small.a2()
    u_first.add()
    r.nz2[z] = r.gr_first[y]
    first = zsum(r.nz2)
    gn1 = zsummed(r.rs2_src, r.rs1_dst, sent)
    v = r.tok[own, :].astype(F32)
    rs = lax.rsqrt(jnp.mean(v * v, axis=-1, keepdims=True) + EPS)
    vr = v * rs
    gn = gn1 * g1
    r.gmo[z] = (r.gmid[...] + rs * (gn - vr * jnp.mean(vr * gn, axis=-1, keepdims=True))).astype(BF16)
    sent_tok = zgather(r.gmo)
    u_out.a2()
    u_gate.a2()
    r.gr_first[y] = first()
    u_first.two.begin()
    for u in u_in:
        u.a2()
    for i in range(2):
        store_out(u_fu[i], 2 * F + 512 * i, 512)
    store_out(u_fd, 0, F)
    store_out(u_fg, F, F)
    r.small_res[0:SMALL, :] = u_small.done()[0]
    store_out(u_out, 3 * F, C)
    store_out(u_gate, 3 * F + C, C)
    r.first[...] = u_first.done()[0]
    by_first = start([rcopy(r.first, r.first_recv, pair(), sibling)])
    for i in range(2):
        store_out(u_in[i], 3 * F + 2 * C + 384 * i, 384)
    finish(by_first)
    r.first[...] = r.first[...] + r.first_recv[...]
    for i in range(3):
        r.small_res[SMALL + i : SMALL + i + 1, :] = r.first[pl.ds(2 * i + core, 1), :]
    sent_out.wait()
    y_out = pltpu.make_async_copy(r.n2, r.out_y, new())
    y_out.start()
    sent_tok.wait()
    gt_out = pltpu.make_async_copy(r.gmo, r.out_gt, new())
    gt_out.start()
    small_out = pltpu.make_async_copy(r.small_res, r.out_small, new())
    small_out.start()
    finish([small_out, y_out, gt_out, pltpu.make_async_copy(r.big, r.out_big, leaving)])
    assert len(taken) == SEMS


def V(*shape, dtype=BF16):
    return pltpu.VMEM(shape, dtype)


def V32(*shape):
    return pltpu.VMEM(shape, F32)


def S(*shape):
    return pltpu.SemaphoreType.DMA(shape)


BIG = 3 * F + 3 * C
HBM, VMEM = pl.ANY, pltpu.VMEM
INS = dict(
    in_tok=HBM, in_cot=HBM, in_w_in=HBM, in_w_gate=HBM, in_w_proj=HBM, in_w_step=HBM, in_w_out=HBM, in_w_fg=HBM, in_w_fu=HBM,
    in_w_fd=HBM, in_taps=VMEM, in_cbias=VMEM, in_sbias=VMEM, in_skip=VMEM, in_first=VMEM, in_second=VMEM, in_gains=VMEM, in_rates=VMEM,
)
OUTS = dict(out_y=((4, 32, D), BF16), out_gt=((4, 32, D), BF16), out_big=((48, BIG), F32), out_small=((56, 128), F32))
SCRATCH = dict(
    sem=S(SEMS),
    tok=V(T, D), cot=V(T, D), w_in=V(D, C), w_gate=V(D, C), w_proj=V(C, 128), w_step=V(T, C), w_out=V(C, D), w_fg=V(D, F), w_fu=V(D, F),
    w_fd=V(F, D),
    big=V32(48, BIG), small_res=V32(56, 128), vec=V32(8, C), nr=V32(N, C), nr2=V32(N, C), rinv=V32(T, 128), normed=V(T, D), ext=V32(T + 8, C), halo=V32(8, C),
    gate_in=V32(T, C), conv_sum=V32(T, C), inner=V(T, C),
    pz=V(4, T, 128), proj=V32(T, 128), proj_r=V32(T, 128), pn=V32(T, 128), step_in=V(T, 128),
    raw=V32(T, C), step=V32(T, C), u=V32(T, C), Bb=V32(T, N, 128), Cb=V32(T, N, 128),
    nr2h=V32(2, N, W), pack=V(2, 2 * N, W), pack_sib=V(2 * N, W), chip_src=V(2 * N, W), chips=V(8, 2 * N, W), t01=V32(16, W),
    st_src=V32(N, W), st_sib=V32(N, W),
    pack_b=V(2, N, W), pack_b_sib=V(N, W), chip_b_src=V(N, W), chips_b=V(8, N, W),
    H=V32(T + 1, N, C), scan_out=V32(T, C),
    rs1_src=V(4, 32, D), rs1_dst=V(3, 32, D), rs2_src=V(4, 32, D), rs2_dst=V(3, 32, D),
    rs3_dst=V(3, 32, D),
    middle=V32(32, D), gmid=V32(32, D), n2=V(4, 32, D), gmo=V(4, 32, D),

    gact=V32(4, 32, F), at_cot=V(16, 2, 48, T), at_nrm=V(16, 2, 48, T),
    l_cot=V(16, 48, 2 * T), l_nrm=V(16, 48, 2 * T), l_n2=V(16, 48, 2 * T), l_gmo=V(16, 48, 2 * T),
    b_out=V(2 * T, C), b_act=V(2 * T, F), b_gg=V(2 * T, F), b_gu=V(2 * T, F), b_gate=V(2 * T, C), b_in=V(2 * T, C),
    gr_fd=V(4, 4, 48, F), x_fd=V(6, 2, 48, F), y_fd=V(6, 48, F), gr_fg=V(4, 4, 48, F), x_fg=V(6, 2, 48, F), y_fg=V(6, 48, F),
    gr_fu=V(2, 4, 4, 48, 512), x_fu=V(2, 6, 2, 48, 512), y_fu=V(2, 3, 48, 512),
    gr_out=V(4, 4, 48, C), x_out=V(6, 2, 48, C), y_out=V(3, 48, C), gr_gate=V(4, 4, 48, C), x_gate=V(6, 2, 48, C), y_gate=V(3, 48, C),
    gr_in=V(2, 4, 4, 48, 384), x_in=V(2, 3, 4, 48, 384), y_in=V(2, 3, 48, 384),
    gso=V32(T, C), gstate=V32(N, C), PR=V32(T, N, 128), part_one=V(8 * T, C), part_two=V(8 * T, C), PE=V32(T, N, 128), rows=V32(T, C), er=V32(T, 128),
    gsr=V(T, C), gcs=V32(T + 8, C), halo2=V32(8, C), dn=V32(8, D), dg=V32(8, 128),
    nz2=V32(4, 4, 8, 128), first=V32(8, 128), first_recv=V32(8, 128), gr_first=V32(4, 4, 8, 128), x_first=V32(3, 4, 8, 128), y_first=V32(3, 8, 128), small=V32(16, 2, SMALL, 128), small_recv=V32(16, SMALL, 128),
    gr_small=V(4, 4, SMALL, 128), x_small=V(3, 4, SMALL, 128), y_small=V(3, SMALL, 128),
)


def local(
    tokens, cotangent, norm_first, in_inner, in_gate, conv_weight, conv_bias, projector, projector_gains, step_weight, step_bias,
    log_rates, skip_gain, out_weight, norm_second, gate_weight, up_weight, down_weight,
):
    y, gt, big, small = pl.pallas_call(
        kernel,
        out_shape=[jax.ShapeDtypeStruct(shape, dtype) for shape, dtype in OUTS.values()],
        in_specs=[pl.BlockSpec(memory_space=m) for m in INS.values()],
        out_specs=[pl.BlockSpec(memory_space=m) for m in (HBM,) * 4],
        scratch_shapes=list(SCRATCH.values()),
        compiler_params=pltpu.CompilerParams(collective_id=0, has_side_effects=True, vmem_limit_bytes=int(63.9 * 2**20)),
    )(
        tokens, cotangent, in_inner, in_gate, projector, step_weight, out_weight, gate_weight, up_weight, down_weight,
        conv_weight, conv_bias, step_bias, skip_gain, norm_first, norm_second, projector_gains, log_rates.T,
    )
    widths = (F, F, F, C, C, C)
    shapes = [(T, D)] * 2 + [(48, w) for w in widths] + [(4, C), (24, R), (N, 24), (4, 24)] + [(1, 24)] * 3 + [(1, 48)] * 2 + [(1, 4)]
    res = pl.pallas_call(
        hand_out,
        out_shape=[jax.ShapeDtypeStruct(sh, F32 if i > 1 else BF16) for i, sh in enumerate(shapes)],
        in_specs=[pl.BlockSpec(memory_space=HBM)] * 4,
        out_specs=[pl.BlockSpec(memory_space=HBM if i < 8 else VMEM) for i in range(len(shapes))],
        scratch_shapes=[V(T, D), V(T, D), V32(48, BIG), V32(56, 128), S(12)],
        compiler_params=pltpu.CompilerParams(vmem_limit_bytes=int(63.9 * 2**20)),
    )(y.reshape(T, D), gt.reshape(T, D), big, small)
    y, gt, fd, fg, fu, out, gate, inn, proj, step_w, rates, taps, cbias, sbias, skip, first, second, gains = res
    return (
        y, gt, first[0], inn, gate, taps, cbias[0], proj.T, gains[0], step_w.T, sbias[0], rates.T, skip[0], out.T, second[0], fg, fu, fd.T,
    )


def hand_out(y, gt, big, small_in, *refs):
    outs, (y_v, gt_v, big_v, small, sem) = refs[:-5], refs[-5:]
    ins = [pltpu.make_async_copy(v, o, sem.at[i]) for i, (v, o) in enumerate(((small_in, small), (big, big_v), (y, y_v), (gt, gt_v)))]
    start(ins)
    parts, at = [], 0
    for o in outs[2:8]:
        parts.append(big_v.at[:, at : at + o.shape[1]])
        at += o.shape[1]
    parts = [pltpu.make_async_copy(v, o, sem.at[4 + i]) for i, (v, o) in enumerate(zip([*parts, y_v, gt_v], [*outs[2:8], *outs[:2]]))]
    finish(ins[1:2])
    start(parts[:6])
    finish(ins[2:])
    start(parts[6:])
    finish(ins[:1])
    proj, step_w, rates, taps, cbias, sbias, skip, first, second, gains = outs[8:]
    for i in range(4):
        for j in range(6):
            proj[i : i + 1, 128 * j : 128 * j + 128] = small[i * 6 + j : i * 6 + j + 1, :]
    step_w[...] = small[24:48, 0:R]
    turned = jnp.concatenate([small[24:48, :], jnp.zeros((104, 128), F32)], axis=0).T
    rates[...] = turned[R : R + N, 0:24]
    taps[...] = turned[R + N : R + N + 4, 0:24]
    for i, o in enumerate((cbias, sbias, skip)):
        o[...] = turned[R + N + 4 + i : R + N + 5 + i, 0:24]
    first[...] = small[48:49, 0:48]
    second[...] = small[49:50, 0:48]
    gains[...] = small[50:51, 0:4]
    finish(parts)


def solution(mesh):
    row, col = P("seq", None), P(None, "head")
    flat, deep = P("head"), P("head", None)
    in_specs = (row, row, P(), col, col, col, flat, deep, P(), col, flat, deep, flat, deep, P(), col, col, deep)
    both, mix = ("head", "seq"), P("seq", "head")
    turned = P("head", "seq")
    out_specs = (
        row, row, P("seq"), mix, mix, P(None, both), P(both), turned, P("seq"), P(None, both), P(both), P(both, None), P(both),
        turned, P("seq"), mix, mix, turned,
    )
    return jax.shard_map(local, mesh=mesh, in_specs=in_specs, out_specs=out_specs, check_vma=False)
```

```python
import types

import jax
import jax.numpy as jnp
from jax import lax
from jax.experimental import pallas as pl
from jax.experimental.pallas import tpu as pltpu
from jax.sharding import PartitionSpec as P

F32 = jnp.float32
BF16 = jnp.bfloat16
T, D, C, F, N, R = 128, 1536, 768, 1024, 16, 96
GROUP = 16
EPS = 1e-5
LOG2E = 1.4426950408889634
HIGH = lax.Precision.HIGHEST
MESH = pl.DeviceIdType.MESH
SMALL = 48
SEMS = 111
W = 384


def dot(a, b, precision=None):
    return jnp.dot(a, b, precision=precision, preferred_element_type=F32)


def dot_nt(a, b, precision=None):
    return lax.dot_general(a, b, (((1,), (1,)), ((), ())), precision=precision, preferred_element_type=F32)


def tiles(total, width):
    return [slice(i, i + width) for i in range(0, total, width)]


def wide(v):
    return jnp.concatenate([v] * (W // 128), axis=1)


class Copy:
    def __init__(self, copy, sem, free):
        self.copy, self.sem, self.free = copy, sem, free

    def start(self):
        self.copy.start()

    def wait(self):
        self.copy.wait()
        self.free.append(self.sem)


def rcopy(src, dst, sems, device):
    send, recv, free = sems
    copy = pltpu.make_async_remote_copy(
        src_ref=src, dst_ref=dst, send_sem=send, recv_sem=recv, device_id=device, device_id_type=MESH
    )
    return Copy(copy, send, free)


def start(copies):
    for c in copies:
        c.start()
    return copies


def finish(copies):
    for c in copies:
        c.wait()


class Burst:
    def __init__(self, sems, src, dst, device):
        self.sems, self.all = sems, rcopy(src, dst, sems, device)

    def send(self, src, dst, device):
        rcopy(src, dst, self.sems, device).start()

    def wait(self):
        self.all.wait()


class Ring:
    def __init__(self, part, land, two, four, new, place, at):
        self.part, self.land, self.at, self.me = part, land, at, place
        self.right, self.left, self.far = lax.rem(place + 1, 4), lax.rem(place + 3, 4), lax.rem(place + 2, 4)
        self.first = Burst(new(), two, two, at(self.right))
        self.rest = Burst(new(), four, four, at(self.right))

    def begin(self):
        part, land, at, right, left, far = self.part, self.land, self.at, self.right, self.left, self.far
        self.first.send(part(far, 0), land(0, 0), at(right))
        self.first.send(part(far, 1), land(1, 1), at(left))
        self.rest.send(part(right, 1), land(2, 1), at(right))
        self.rest.send(part(left, 0), land(3, 0), at(left))

    def pass_on(self):
        self.first.wait()
        for h, d in enumerate((self.right, self.left)):
            own = self.part(d, h)
            own[...] = (own[...].astype(F32) + self.land(h, h)[...].astype(F32)).astype(own.dtype)
            self.rest.send(own, self.land(4 + h, h), self.at(d))

    def totals(self):
        self.rest.wait()
        for h, (a, b) in enumerate(((4, 3), (5, 2))):
            own = self.part(self.me, h)
            yield own, own[...].astype(F32) + (self.land(a, h)[...].astype(F32) + self.land(b, h)[...].astype(F32))


class Straight:
    def __init__(self, part, land, new, place, at):
        self.part, self.land, self.at, self.me = part, land, at, place
        self.burst = Burst(new(), land, land, at(lax.rem(place + 1, 4)))

    def begin(self):
        for k in (2, 1, 3):
            d = lax.rem(self.me + k, 4)
            self.burst.send(self.part(d), self.land.at[k - 1], self.at(d))

    def totals(self):
        self.burst.wait()
        own, land = self.part(self.me), self.land
        yield own, own[...].astype(F32) + ((land[0].astype(F32) + land[2].astype(F32)) + land[1].astype(F32))


class Unit:
    def __init__(self, grid, land_one, land_two, new, x, y, at, x_first, both_ways, split=0):
        along_x, along_y = (x, lambda d: at(d, y)), (y, lambda d: at(x, d))
        one, two = (along_x, along_y) if x_first else (along_y, along_x)

        def chunk(d, half=slice(0, 4)):
            return grid.at[half, d] if x_first else grid.at[d, half]

        def piece(d):
            return grid.at[d, x] if x_first else grid.at[y, d]

        if both_ways:
            self.one = Ring(
                lambda d, h: chunk(d, slice(2 * h, 2 * h + 2)), lambda i, h: land_one.at[i], land_one.at[0:2], land_one.at[2:6], new, *one
            )
        else:
            self.one = Straight(chunk, land_one, new, *one)
        if split:

            def side(ref, h):
                return ref.at[:, split:] if h else ref.at[:, 0:split]

            self.two = Ring(
                lambda d, h: side(piece(d), h), lambda i, h: side(land_two.at[i], h), land_two.at[0], land_two.at[0:2], new, *two
            )
        else:
            self.two = Straight(piece, land_two, new, *two)

    def a0(self):
        self.one.begin()

    def a1(self):
        self.one.pass_on()

    def add(self):
        for own, v in self.one.totals():
            own[...] = v.astype(own.dtype)

    def a2(self):
        self.add()
        self.two.begin()

    def b1(self):
        self.two.pass_on()

    def done(self):
        return [v for _, v in self.two.totals()]


def kernel(*refs):
    r = types.SimpleNamespace(**dict(zip([*INS, *OUTS, *SCRATCH], refs, strict=True)))
    s = lax.axis_index("seq")
    z = lax.axis_index("head")
    p = lax.rem(s, GROUP)
    base = s - p
    core = lax.rem(s, 2)
    x = lax.rem(s // 2, 4)
    y = s // 8

    def zdev(k):
        return (s, lax.rem(z + k, 4))

    def gdev(k):
        return (base + lax.rem(p + k, GROUP), z)

    def chip(cx, cy):
        return (cy * 8 + cx * 2 + core, z)

    sibling = (s + 1 - 2 * core, z)
    taken = []

    def new():
        taken.append(0)
        return r.sem.at[len(taken) - 1]

    free = []

    def sender():
        return free.pop() if free else new()

    def pair():
        return sender(), new(), free

    def local(src, dst):
        sem = sender()
        return Copy(pltpu.make_async_copy(src, dst, sem), sem, free)

    barrier = pltpu.get_barrier_semaphore()
    for k in range(1, 4):
        pl.semaphore_signal(barrier, 1, device_id=zdev(k), device_id_type=MESH)

    mates = sorted(((dy + min(dx, 4 - dx), dy, dx) for dy in range(2) for dx in range(4)), reverse=True)[:7]

    def mate(dy, dx):
        return base + lax.rem(y + dy, 2) * 8 + lax.rem(x + dx, 4) * 2 + core

    others = [(mate(dy, dx), z) for _, dy, dx in mates]
    for device in (*others, sibling, gdev(15 - 14 * core), (s + 8 * (3 - 2 * y), z)):
        pl.semaphore_signal(barrier, 1, device_id=device, device_id_type=MESH)

    def load(src, dst):
        c = local(src, dst)
        c.start()
        return c

    ld_tok = load(r.in_tok, r.tok)
    ld_in = load(r.in_w_in, r.w_in)
    ld_gate = load(r.in_w_gate, r.w_gate)
    ld_cot = load(r.in_cot, r.cot)
    ld_fd = load(r.in_w_fd, r.w_fd)
    ld_proj = load(r.in_w_proj, r.w_proj)
    r.w_step[...] = jnp.zeros((T, C), BF16)
    ld_step = load(r.in_w_step, r.w_step.at[0:R])
    ld_out = load(r.in_w_out, r.w_out)
    ld_fg = load(r.in_w_fg, r.w_fg)
    ld_fu = load(r.in_w_fu, r.w_fu)

    vec = r.vec
    vec[0:4, :] = r.in_taps[...]
    for i, v in enumerate((r.in_cbias, r.in_sbias, r.in_skip)):
        vec[4 + i : 5 + i, :] = v[...].reshape(1, C)
    g1 = r.in_first[...].reshape(1, D)
    g2 = r.in_second[...].reshape(1, D)
    nr = -jnp.exp(r.in_rates[...])
    r.nr[...] = nr
    nr2 = nr * LOG2E
    r.nr2[...] = nr2
    for j, c in enumerate(tiles(C, W)):
        r.nr2h[j] = nr2[:, c]

    ld_tok.wait()
    for rows in tiles(T, 32):
        v = r.tok[rows, :].astype(F32)
        rs = lax.rsqrt(jnp.mean(v * v, axis=-1, keepdims=True) + EPS)
        r.rinv[rows, :] = jnp.broadcast_to(rs, (32, 128))
        r.normed[rows, :] = (v * rs * g1).astype(BF16)
    ld_in.wait()
    nrm = r.normed[...]
    for c in tiles(C, 256):
        r.ext[8 : 8 + T, c] = dot(nrm, r.w_in[:, c]).astype(BF16).astype(F32)
    pl.semaphore_wait(barrier, 3 + 7 + 3)
    halo = start([rcopy(r.ext.at[T : T + 8], r.halo, pair(), gdev(1))])
    ld_gate.wait()
    for c in tiles(C, 256):
        r.gate_in[:, c] = dot(nrm, r.w_gate[:, c])

    def turned(value, at, lhs):
        at[...] = value.T.reshape(16, 2, 48, T)
        lhs[:, :, 0:T] = at[:, core]
        return start([rcopy(at.at[:, 1 - core], lhs.at[:, :, T : 2 * T], pair(), sibling)])

    def both(b):
        return start([rcopy(b.at[0:T], b.at[T : 2 * T], pair(), sibling)])

    finish(halo)
    r.ext[0:8, :] = jnp.where(p == 0, 0.0, r.halo[...])
    for c in tiles(C, 128):
        tot = vec[4:5, c] + vec[0:1, c] * r.ext[5 : 5 + T, c]
        for k in range(1, 4):
            tot = tot + vec[k : k + 1, c] * r.ext[5 + k : 5 + k + T, c]
        r.conv_sum[:, c] = tot
        r.inner[:, c] = (tot * jax.nn.sigmoid(tot)).astype(BF16)

    def zgather(buf):
        burst = Burst(pair(), buf.at[0:3], buf.at[0:3], zdev(1))
        for k in (2, 1, 3):
            burst.send(buf.at[z], buf.at[z], zdev(k))
        return burst

    def zsum(buf):
        burst = zgather(buf)

        def result():
            burst.wait()
            return (buf[0].astype(F32) + buf[1].astype(F32)) + (buf[2].astype(F32) + buf[3].astype(F32))

        return result

    ld_proj.wait()
    r.pz[z] = dot(r.inner[...], r.w_proj[...]).astype(BF16)
    projected = zsum(r.pz)

    ld_cot.wait()
    ld_fd.wait()
    cot = r.cot[...]
    for c in tiles(F, 256):
        r.gact[:, :, c] = dot_nt(cot, r.w_fd[c, :]).reshape(4, 32, 256)

    tn_cot = turned(cot, r.at_cot, r.l_cot)
    tn_nrm = turned(nrm, r.at_nrm, r.l_nrm)

    proj = projected()
    r.proj[...] = proj
    lane = lax.broadcasted_iota(jnp.int32, (1, 128), 1)
    m1 = (lane < R).astype(F32)
    m3 = (lane >= R + N).astype(F32)
    m2 = 1.0 - m1 - m3

    def by_part(v):
        return (
            m1 * (jnp.sum(v * m1, -1, keepdims=True) / R)
            + m2 * (jnp.sum(v * m2, -1, keepdims=True) / N)
            + m3 * (jnp.sum(v * m3, -1, keepdims=True) / N)
        )

    rr = lax.rsqrt(by_part(proj * proj) + EPS)
    r.proj_r[...] = rr
    gains_in = r.in_gains[...].reshape(1, 128)
    pn = proj * rr * gains_in
    r.pn[...] = pn
    step_in = (pn * m1).astype(BF16)
    r.step_in[...] = step_in
    ld_step.wait()
    for c in tiles(C, 256):
        raw = dot(step_in, r.w_step[:, c]) + vec[5:6, c]
        r.raw[:, c] = raw
        st = jnp.maximum(raw, 0.0) + jnp.log1p(jnp.exp(-jnp.abs(raw)))
        r.step[:, c] = st
        r.u[:, c] = st * r.inner[:, c].astype(F32)
    rown = lax.broadcasted_iota(jnp.int32, (N, 128), 0)
    lanes = lax.broadcasted_iota(jnp.int32, (N, 128), 1)
    selb = (lanes == rown + R).astype(F32)
    selc = (lanes == rown + R + N).astype(F32)
    sel = selb + selc
    part_of = lax.broadcasted_iota(jnp.int32, (128, 256), 0) - jnp.where(lax.broadcasted_iota(jnp.int32, (128, 256), 1) < 128, R, R + N)
    to_lanes = ((part_of >= 0) & (part_of < N)).astype(BF16)

    for rows in tiles(T, 32):
        some = r.pn[rows, :]
        one = jnp.concatenate([jnp.broadcast_to(some[i : i + 1, :], (N, 128)) * sel for i in range(32)], axis=0)
        high = one.astype(BF16)
        low = (one - high.astype(F32)).astype(BF16)
        v = dot(high, to_lanes) + dot(low, to_lanes)
        r.Bb[rows] = v[:, 0:128].reshape(32, N, 128)
        r.Cb[rows] = v[:, 128:256].reshape(32, N, 128)

    top = lax.broadcasted_iota(jnp.int32, (N, W), 0) < 8

    def coded(ref, h, tot):
        high = tot.astype(BF16).astype(F32)
        ref[0:N, :] = h.astype(BF16)
        ref[N : 2 * N, :] = jnp.where(top, high, tot - high).astype(BF16)

    def state_of(ref):
        return ref[0:N, :].astype(F32)

    def steps_of(ref):
        v = ref[N : 2 * N, :].astype(F32)
        return v[0:1, :] + v[8:9, :]

    for half, c in enumerate(tiles(C, W)):
        a2 = r.nr2[:, c]

        def first(b, h):
            st = r.step[pl.ds(b * 8, 8), c]
            uu = r.u[pl.ds(b * 8, 8), c]
            for i in range(8):
                h = jnp.exp2(a2 * st[i : i + 1, :]) * h + uu[i : i + 1, :] * wide(r.Bb[b * 8 + i])
            return h

        h = lax.fori_loop(0, T // 8, first, jnp.zeros((N, W), F32))
        coded(r.pack.at[half], h, jnp.sum(r.step[:, c], axis=0, keepdims=True))

    nth = p // 2
    is_first = core == 0
    a2c = r.nr2h[core]

    def to_mates(src, land):
        burst = Burst(pair(), land.at[0:7], land.at[0:7], sibling)
        for device in others:
            burst.send(src, land.at[nth], device)
        land[nth] = src[...]
        return burst.wait

    def to_sibling(src, dst):
        return start([rcopy(src, dst, pair(), sibling)])

    finish(to_sibling(r.pack.at[1 - core], r.pack_sib))
    h_own, h_sib = state_of(r.pack.at[core]), state_of(r.pack_sib)
    t_own, t_sib = steps_of(r.pack.at[core]), steps_of(r.pack_sib)
    h0, h1 = jnp.where(is_first, h_own, h_sib), jnp.where(is_first, h_sib, h_own)
    t0, t1 = jnp.where(is_first, t_own, t_sib), jnp.where(is_first, t_sib, t_own)
    r.t01[0:1, :] = t0
    r.t01[8:9, :] = t1
    coded(r.chip_src, jnp.exp2(a2c * t1) * h0 + h1, t0 + t1)
    swapped = to_mates(r.chip_src, r.chips)
    ld_fu.wait()
    for c in tiles(F, 256):
        r.w_fd[c, :] = r.w_fu[:, c].T
    finish(tn_cot)
    finish(tn_nrm)
    swapped()
    state = jnp.zeros((N, W), F32)
    for j in range(7):
        at = r.chips.at[j]
        state = jnp.where(j < nth, jnp.exp2(a2c * steps_of(at)) * state + state_of(at), state)
    later = jnp.exp2(a2c * t0) * state + h0
    r.st_src[...] = jnp.where(is_first, later, state)
    entering = to_sibling(r.st_src, r.st_sib)
    state = jnp.where(is_first, state, later)
    finish(entering)
    for half, c in enumerate(tiles(C, W)):
        r.H[0, :, c] = jnp.where(core == half, state, r.st_sib[...])

    eights = (lax.broadcasted_iota(jnp.int32, (16, 128), 1) // 8 == lax.broadcasted_iota(jnp.int32, (16, 128), 0)).astype(BF16)

    def folded(v):
        return v[0:8, :] + v[8:16, :]

    def finished(part, out):
        for j in range(8):
            out[16 * j : 16 * j + 16, :] = dot(eights, part[128 * j : 128 * j + 128, :])

    for c in tiles(C, W):
        a2 = r.nr2[:, c]

        def second(b, h):
            st = r.step[pl.ds(b * 8, 8), c]
            uu = r.u[pl.ds(b * 8, 8), c]
            rows = []
            for i in range(8):
                h = jnp.exp2(a2 * st[i : i + 1, :]) * h + uu[i : i + 1, :] * wide(r.Bb[b * 8 + i])
                r.H[b * 8 + i + 1, :, c] = h
                rows.append(folded(h * wide(r.Cb[b * 8 + i])))
            r.part_one[pl.ds(pl.multiple_of(b * 64, 64), 64), c] = jnp.concatenate(rows, axis=0).astype(BF16)
            return h

        lax.fori_loop(0, T // 8, second, r.H[0, :, c])

    finished(r.part_one, r.scan_out)
    for c in tiles(C, 128):
        so = r.scan_out[:, c] + vec[6:7, c] * r.inner[:, c].astype(F32)
        r.scan_out[:, c] = so
        gi = r.gate_in[:, c]
        r.b_out[0:T, c] = (so * (gi * jax.nn.sigmoid(gi))).astype(BF16)
    by_out = both(r.b_out)

    def zscatter(src, dst):
        return Burst(pair(), src.at[0:3], dst, zdev(1))

    def zsend(burst, src, dst, j):
        c = slice(512 * j, 512 * j + 512)
        for k in (2, 1, 3):
            burst.send(src.at[lax.rem(z + k, 4), :, c], dst.at[k - 1, :, c], zdev(k))

    def zsummed(src, dst, burst):
        burst.wait()
        return (src[z].astype(F32) + dst[0].astype(F32)) + (dst[1].astype(F32) + dst[2].astype(F32))

    def fours(v):
        return v.astype(BF16).reshape(4, 32, v.shape[-1])

    ld_out.wait()
    own = pl.ds(pl.multiple_of(z * 32, 32), 32)
    halves = tiles(32, 16)
    mixed = r.b_out[0:T, :].reshape(4, 32, C)
    sent = []
    for hs in halves:
        some = mixed[:, hs].reshape(64, C)
        for c in tiles(D, 512):
            r.rs1_src[:, hs, c] = dot(some, r.w_out[:, c]).astype(BF16).reshape(4, 16, 512)
        burst = Burst(pair(), r.rs1_src.at[0:3, hs], r.rs1_dst.at[:, hs], zdev(1))
        for k in (2, 1, 3):
            burst.send(r.rs1_src.at[lax.rem(z + k, 4), hs], r.rs1_dst.at[k - 1, hs], zdev(k))
        sent.append(burst)
    gathered = []
    for hs, burst in zip(halves, sent):
        burst.wait()
        terms = [r.rs1_src[z, hs], *(r.rs1_dst[k, hs] for k in range(3))]
        rows = pl.ds(pl.multiple_of(z * 32 + hs.start, 16), 16)
        middle = r.tok[rows, :].astype(F32) + sum((v.astype(F32) for v in terms[1:]), terms[0].astype(F32))
        r.middle[hs, :] = middle
        r2 = lax.rsqrt(jnp.mean(middle * middle, axis=-1, keepdims=True) + EPS)
        r.out_y[z, hs] = (middle * r2 * g2).astype(BF16)
        burst = Burst(pair(), r.out_y.at[0:3, hs], r.out_y.at[0:3, hs], zdev(1))
        for k in (2, 1, 3):
            burst.send(r.out_y.at[z, hs], r.out_y.at[z, hs], zdev(k))
        gathered.append(burst)

    def unit(grid, land_one, land_two, x_first, both_ways=True, split=0):
        return Unit(grid, land_one, land_two, pair, x, y, chip, x_first, both_ways, split)

    def product_of(grid, lhs, b, lo, n):
        left = lhs[...].reshape(D // 2, 2 * T)
        for c in tiles(n, 256 if n % 256 == 0 else 128):
            cols = slice(lo + c.start, lo + c.stop)
            grid[:, :, :, c] = dot(left, b[:, cols]).astype(BF16).reshape(4, 4, 48, c.stop - c.start)

    def store_out(u, lo, n):
        at = lo
        for v in u.done():
            r.out_big[:, at : at + v.shape[1]] = v
            at += v.shape[1]

    u_fd = [unit(r.gr_fd.at[i], r.x_fd.at[i], r.y_fd.at[i], i == 0, split=256) for i in range(2)]
    u_fg = [unit(r.gr_fg.at[i], r.x_fg.at[i], r.y_fg.at[i], i == 0, split=256) for i in range(2)]
    u_fu = [unit(r.gr_fu.at[i], r.x_fu.at[i], r.y_fu.at[i], i == 0) for i in range(2)]

    def halves_of(units, grids, lhs, b):
        for i in range(2):
            product_of(grids.at[i], lhs, b, 512 * i, 512)
            units[i].a0()

    u_out = unit(r.gr_out, r.x_out, r.y_out, True)
    u_gate = unit(r.gr_gate, r.x_gate, r.y_gate, False)
    u_in = [unit(r.gr_in.at[i], r.x_in.at[i], r.y_in.at[i], i == 0, False) for i in range(2)]
    u_small = unit(r.gr_small, r.x_small, r.y_small, True, False)
    u_first = unit(r.gr_first, r.x_first, r.y_first, False, False)

    ld_fg.wait()
    for hs, burst in zip(halves, gathered):
        burst.wait()
        some = r.out_y[:, hs].reshape(64, D)
        for c in tiles(F, 256):
            g = dot(some, r.w_fg[:, c])
            u = dot(some, r.w_fu[:, c])
            ga = r.gact[:, hs, c].reshape(64, 256)
            sg = jax.nn.sigmoid(g)
            sl = g * sg
            for b, v in ((r.b_act, sl * u), (r.b_gg, ga * u * (sg * (1.0 + g * (1.0 - sg)))), (r.b_gu, ga * sl)):
                v = v.astype(BF16)
                for q in range(4):
                    b[32 * q + hs.start : 32 * q + hs.stop, c] = v[16 * q : 16 * q + 16, :]
    n2 = r.out_y[...].reshape(T, D)
    by_act = both(r.b_act)
    gg = r.b_gg[0:T, :]
    gu = r.b_gu[0:T, :]
    sent = zscatter(r.rs2_src, r.rs2_dst)
    for j, c in enumerate(tiles(D, 512)):
        r.rs2_src[:, :, c] = fours(dot_nt(gg, r.w_fg[c, :]) + dot(gu, r.w_fd[:, c]))
        zsend(sent, r.rs2_src, r.rs2_dst, j)
        if j == 1:
            finish(by_act)
            halves_of(u_fd, r.gr_fd, r.l_cot, r.b_act)
    ld_fd = load(r.in_w_fd, r.w_fd)
    by_gg = both(r.b_gg)
    by_gu = both(r.b_gu)
    tn_n2 = turned(n2, r.at_cot, r.l_n2)

    finish(tn_n2)
    finish(by_gg)
    halves_of(u_fg, r.gr_fg, r.l_n2, r.b_gg)
    finish(by_gu)
    halves_of(u_fu, r.gr_fu, r.l_n2, r.b_gu)

    gy = zsummed(r.rs2_src, r.rs2_dst, sent)
    v = r.middle[...]
    r2 = lax.rsqrt(jnp.mean(v * v, axis=-1, keepdims=True) + EPS)
    vr = v * r2
    gn = gy * g2
    gm = r.cot[own, :].astype(F32) + r2 * (gn - vr * jnp.mean(vr * gn, axis=-1, keepdims=True))
    r.gmid[...] = gm
    r.out_gt[z] = gm.astype(BF16)
    got = zgather(r.out_gt)
    r.dn[1:2, :] = jnp.sum(vr * gy, axis=0, keepdims=True)
    act = r.b_act[0:T, :]
    ld_fd.wait()
    sent3 = zscatter(r.rs1_src, r.rs3_dst)
    for j, c in enumerate(tiles(D, 512)):
        r.rs1_src[:, :, c] = fours(dot(act, r.w_fd[:, c]))
        zsend(sent3, r.rs1_src, r.rs3_dst, j)

    def owner(shape):
        i = lax.broadcasted_iota(jnp.int32, shape, 0)
        return 2 * (i & 15) + (i >> 4)

    def rows_of(v, width, hot):
        k = lax.broadcasted_iota(jnp.int32, (32, v.shape[1]), 1) - width * owner((32, v.shape[1]))
        one = jnp.where((k >= 0) & (k < width), v, 0.0)
        high = one.astype(BF16)
        return dot(high, hot) + dot((one - high.astype(F32)).astype(BF16), hot)

    kk = lax.broadcasted_iota(jnp.int32, (D, 128), 0)
    hot = lax.broadcasted_iota(jnp.int32, (D, 128), 1) == kk - 48 * ((kk * 683) >> 15)
    r.at_cot[...] = hot.astype(BF16).reshape(16, 2, 48, T)
    got.wait()
    for u in u_fd:
        u.a1()

    gmo = r.out_gt[...].reshape(T, D)
    for c in tiles(C, 256):
        gmx = dot_nt(gmo, r.w_out[c, :])
        gi = r.gate_in[:, c]
        sg = jax.nn.sigmoid(gi)
        r.gso[:, c] = gmx * (gi * sg)
        r.b_gate[0:T, c] = (gmx * r.scan_out[:, c] * (sg * (1.0 + gi * (1.0 - sg)))).astype(BF16)
    by_gate = both(r.b_gate)
    tn_gmo = turned(gmo, r.at_nrm, r.l_gmo)

    def rev_first(c):
        a2 = r.nr2[:, c]

        def body(k, cr):
            b = T // 8 - 1 - k
            st = r.step[pl.ds(b * 8, 8), c]
            gs = r.gso[pl.ds(b * 8, 8), c]
            for i in range(7, -1, -1):
                cr = jnp.exp2(a2 * st[i : i + 1, :]) * (gs[i : i + 1, :] * wide(r.Cb[b * 8 + i]) + cr)
            return cr

        cr = lax.fori_loop(0, T // 8, body, jnp.zeros((N, W), F32))
        r.pack_b[0 if c.start == 0 else 1] = cr.astype(BF16)

    for c in tiles(C, W):
        rev_first(c)
    finish(to_sibling(r.pack_b.at[1 - core], r.pack_b_sib))
    c_own, c_sib = r.pack_b[core].astype(F32), r.pack_b_sib[...].astype(F32)
    c0, c1 = jnp.where(is_first, c_own, c_sib), jnp.where(is_first, c_sib, c_own)
    t0, t1 = r.t01[0:1, :], r.t01[8:9, :]
    r.chip_b_src[...] = (c0 + jnp.exp2(a2c * t0) * c1).astype(BF16)
    swapped = to_mates(r.chip_b_src, r.chips_b)
    for u in u_fg:
        u.a1()
    hot = r.at_cot[...].reshape(D, 128)
    finish(by_gate)
    product_of(r.gr_gate, r.l_nrm, r.b_gate, 0, C)
    u_gate.a0()
    finish(tn_gmo)
    finish(by_out)
    product_of(r.gr_out, r.l_gmo, r.b_out, 0, C)
    u_out.a0()

    def read_rows(b, carry):
        gs = r.gso[pl.ds(b * 8, 8), :]
        for i in range(8):
            pr = gs[i : i + 1, :] * r.H[b * 8 + i + 1]
            r.PR[b * 8 + i] = sum((pr[:, k] for k in tiles(C, 128)[1:]), pr[:, 0:128])
        return carry

    lax.fori_loop(0, T // 8, read_rows, 0)
    for c in tiles(C, 256):
        r.w_out[c, :] = r.w_gate[:, c].T
    swapped()
    for u in u_fu:
        u.a1()
    state = jnp.zeros((N, W), F32)
    for j in range(7, 0, -1):
        state = jnp.where(j > nth, r.chips_b[j].astype(F32) + jnp.exp2(a2c * steps_of(r.chips.at[j])) * state, state)
    later = c1 + jnp.exp2(a2c * t1) * state
    r.st_src[...] = jnp.where(is_first, state, later)
    entering = to_sibling(r.st_src, r.st_sib)
    state = jnp.where(is_first, later, state)
    r.out_y[z] = (r.middle[...] + zsummed(r.rs1_src, r.rs3_dst, sent3)).astype(BF16)
    sent_out = zgather(r.out_y)
    finish(entering)
    for half, c in enumerate(tiles(C, W)):
        r.gstate[:, c] = jnp.where(core == half, state, r.st_sib[...])

    def rev_second(c):
        a2 = r.nr2[:, c]
        a = r.nr[:, c]

        def body(k, state):
            cr, gl = state
            b = T // 8 - 1 - k
            st = r.step[pl.ds(b * 8, 8), c]
            gs = r.gso[pl.ds(b * 8, 8), c]
            uu = r.u[pl.ds(b * 8, 8), c]
            s1, s2 = [None] * 8, [None] * 8
            for i in range(7, -1, -1):
                t = b * 8 + i
                si, gi, ui = st[i : i + 1, :], gs[i : i + 1, :], uu[i : i + 1, :]
                g = gi * wide(r.Cb[t]) + cr
                s1[i] = folded(g * wide(r.Bb[t]))
                pe = g * ui
                pe = (pe[:, 0:128] + pe[:, 128:256]) + pe[:, 256:384]
                if c.start:
                    pe = pe + r.PE[t]
                r.PE[t] = pe
                cr = jnp.exp2(a2 * si) * g
                q = cr * r.H[t, :, c]
                s2[i] = folded(q * a)
                gl = gl + q * si
            rows = pl.ds(pl.multiple_of(b * 64, 64), 64)
            r.part_one[rows, c] = jnp.concatenate(s1, axis=0).astype(BF16)
            r.part_two[rows, c] = jnp.concatenate(s2, axis=0).astype(BF16)
            return cr, gl

        _, gl = lax.fori_loop(0, T // 8, body, (r.gstate[:, c], jnp.zeros((N, W), F32)))
        r.rows[R : R + N, c] = gl * a

    for c in tiles(C, W):
        rev_second(c)
    finished(r.part_one, r.gate_in)
    finished(r.part_two, r.scan_out)

    ones = jnp.ones((128, 128), BF16)

    for tok in tiles(T, 32):
        pe = dot(r.PE[tok].reshape(32 * N, 128).astype(BF16), ones).reshape(32, N, 128)
        pr = dot(r.PR[tok].reshape(32 * N, 128).astype(BF16), ones).reshape(32, N, 128)
        r.er[tok, :] = jnp.sum(pe * selb[None] + pr * selc[None], axis=1)
    for c in tiles(C, 256):
        inner = r.inner[:, c].astype(F32)
        s1 = r.gate_in[:, c]
        raw_g = (r.scan_out[:, c] + s1 * inner) * jax.nn.sigmoid(r.raw[:, c])
        r.gsr[:, c] = raw_g.astype(BF16)
        r.rows[R + N + 5 : R + N + 6, c] = jnp.sum(raw_g, axis=0, keepdims=True)
        gso = r.gso[:, c]
        r.rows[R + N + 6 : R + N + 7, c] = jnp.sum(gso * inner, axis=0, keepdims=True)
        r.gate_in[:, c] = gso * vec[6:7, c] + s1 * r.step[:, c]
    r.pz[z] = (dot_nt(r.gsr[...], r.w_step[...]) + r.er[...]).astype(BF16)
    summed = zsum(r.pz)
    for c in tiles(C, 256):
        r.w_fd[c, :] = r.w_in[:, c].T
    u_out.a1()
    u_gate.a1()
    gy = summed()
    vr = r.proj[...] * r.proj_r[...]
    gn = gy * gains_in
    gpj = (r.proj_r[...] * (gn - vr * by_part(vr * gn))).astype(BF16)
    r.dg[...] = jnp.broadcast_to(jnp.sum(vr * gy, axis=0, keepdims=True), (8, 128))
    for c in tiles(C, 256):
        gi = r.gate_in[:, c] + dot_nt(gpj, r.w_proj[c, :])
        cs = r.conv_sum[:, c]
        sg = jax.nn.sigmoid(cs)
        r.gcs[0:T, c] = gi * (sg * (1.0 + cs * (1.0 - sg)))
    halo = start([rcopy(r.gcs.at[0:8], r.halo2, pair(), gdev(15))])
    for c in tiles(C, 128):
        gc = r.gcs[0:T, c]
        for k in range(4):
            r.rows[R + N + k : R + N + k + 1, c] = jnp.sum(gc * r.ext[5 + k : 5 + k + T, c], axis=0, keepdims=True)
        r.rows[R + N + 4 : R + N + 5, c] = jnp.sum(gc, axis=0, keepdims=True)
    r.rows[0:R, :] = jnp.zeros((R, C), F32)
    r.rows[R + N + 7 : T, :] = jnp.zeros((T - R - N - 7, C), F32)
    chan = (dot(r.gsr[...].T, r.step_in[...]) + r.rows[...].T).reshape(16, 2, 24, 128)
    ll = lax.broadcasted_iota(jnp.int32, (128, 128), 0)
    order = (lax.broadcasted_iota(jnp.int32, (128, 128), 1) == 4 * (2 * (ll & 15) + ((ll >> 4) & 1)) + (ll >> 5)).astype(BF16)
    pt = dot(dot_nt(order, gpj).astype(BF16), r.inner[...])
    for h in range(2):
        r.small[:, h, 24:48, :] = chan[:, h]
        for i in range(4):
            for j in range(6):
                r.small[:, h, i * 6 + j, :] = pt[32 * i + 16 * h : 32 * i + 16 * h + 16, 128 * j : 128 * j + 128]
    by_small = start([rcopy(r.small.at[:, 1 - core], r.small_recv, pair(), sibling)])
    for u in (*u_fd, *u_fg, *u_fu,):
        u.a2()
    finish(halo)
    r.gcs[T : T + 8, :] = jnp.where(p == GROUP - 1, 0.0, r.halo2[...])
    for c in tiles(C, 128):
        tot = vec[3:4, c] * r.gcs[0:T, c]
        for k in range(3):
            tot = tot + vec[k : k + 1, c] * r.gcs[3 - k : 3 - k + T, c]
        r.b_in[0:T, c] = tot.astype(BF16)
    by_in = both(r.b_in)
    finish(by_small)
    r.gr_small[...] = (r.small[:, core] + r.small_recv[...]).astype(BF16).reshape(4, 4, SMALL, 128)
    u_small.a0()
    gip = r.b_in[0:T, :]
    ggi = r.b_gate[0:T, :]
    sent = zscatter(r.rs2_src, r.rs1_dst)
    for j, c in enumerate(tiles(D, 512)):
        gnp = dot(gip, r.w_fd[0:C, c]) + dot(ggi, r.w_out[:, c])
        r.rs2_src[:, :, c] = fours(gnp)
        if j < 2:
            zsend(sent, r.rs2_src, r.rs1_dst, j)
        r.dn[0:1, c] = jnp.sum(r.tok[:, c].astype(F32) * (r.rinv[:, 0:1] * gnp), axis=0, keepdims=True)
    k4 = lax.broadcasted_iota(jnp.int32, (128, 128), 0)
    hot4 = (lax.broadcasted_iota(jnp.int32, (128, 128), 1) == (k4 & 3)).astype(BF16)
    r.gr_first[...] = jnp.zeros((4, 4, 8, 128), F32)
    for i, v in enumerate((rows_of(r.dn[0:1, :], 48, hot), rows_of(r.dn[1:2, :], 48, hot), rows_of(r.dg[0:1, :] * 0.25, 4, hot4))):
        for h in range(2):
            r.gr_first[:, :, 2 * i + h, :] = v[16 * h : 16 * h + 16, :].reshape(4, 4, 128)
    u_first.a0()
    zsend(sent, r.rs2_src, r.rs1_dst, 2)
    finish(by_in)
    for i in range(2):
        product_of(r.gr_in.at[i], r.l_nrm, r.b_in, 384 * i, 384)
        u_in[i].a0()
    for u in (*u_fd, *u_fg):
        u.b1()
    u_small.a2()
    u_first.add()
    r.nz2[z] = r.gr_first[y]
    first = zsum(r.nz2)
    gn1 = zsummed(r.rs2_src, r.rs1_dst, sent)
    v = r.tok[own, :].astype(F32)
    rs = lax.rsqrt(jnp.mean(v * v, axis=-1, keepdims=True) + EPS)
    vr = v * rs
    gn = gn1 * g1
    r.out_gt[z] = (r.gmid[...] + rs * (gn - vr * jnp.mean(vr * gn, axis=-1, keepdims=True))).astype(BF16)
    sent_tok = zgather(r.out_gt)
    u_out.a2()
    u_gate.a2()
    r.gr_first[y] = first()
    u_first.two.begin()
    for u in u_in:
        u.a2()
    for i in range(2):
        store_out(u_fd[i], 512 * i, 512)
        store_out(u_fg[i], F + 512 * i, 512)
        store_out(u_fu[i], 2 * F + 512 * i, 512)
    r.out_small[0:SMALL, :] = u_small.done()[0]
    store_out(u_out, 3 * F, C)
    store_out(u_gate, 3 * F + C, C)
    r.first[...] = u_first.done()[0]
    by_first = start([rcopy(r.first, r.first_recv, pair(), sibling)])
    for i in range(2):
        store_out(u_in[i], 3 * F + 2 * C + 384 * i, 384)
    finish(by_first)
    r.first[...] = r.first[...] + r.first_recv[...]
    for i in range(3):
        r.out_small[SMALL + i : SMALL + i + 1, :] = r.first[pl.ds(2 * i + core, 1), :]
    sent_out.wait()
    sent_tok.wait()
    assert len(taken) == SEMS


def V(*shape, dtype=BF16):
    return pltpu.VMEM(shape, dtype)


def V32(*shape):
    return pltpu.VMEM(shape, F32)


def S(*shape):
    return pltpu.SemaphoreType.DMA(shape)


BIG = 3 * F + 3 * C
HBM, VMEM = pl.ANY, pltpu.VMEM
INS = dict(
    in_tok=HBM, in_cot=HBM, in_w_in=HBM, in_w_gate=HBM, in_w_proj=HBM, in_w_step=HBM, in_w_out=HBM, in_w_fg=HBM, in_w_fu=HBM,
    in_w_fd=HBM, in_taps=VMEM, in_cbias=VMEM, in_sbias=VMEM, in_skip=VMEM, in_first=VMEM, in_second=VMEM, in_gains=VMEM, in_rates=VMEM,
)
OUTS = dict(out_y=((4, 32, D), BF16), out_gt=((4, 32, D), BF16), out_big=((48, BIG), F32), out_small=((56, 128), F32))
SCRATCH = dict(
    sem=S(SEMS),
    tok=V(T, D), cot=V(T, D), w_in=V(D, C), w_gate=V(D, C), w_proj=V(C, 128), w_step=V(T, C), w_out=V(C, D), w_fg=V(D, F), w_fu=V(D, F),
    w_fd=V(F, D),
    vec=V32(8, C), nr=V32(N, C), nr2=V32(N, C), rinv=V32(T, 128), normed=V(T, D), ext=V32(T + 8, C), halo=V32(8, C),
    gate_in=V32(T, C), conv_sum=V32(T, C), inner=V(T, C),
    pz=V(4, T, 128), proj=V32(T, 128), proj_r=V32(T, 128), pn=V32(T, 128), step_in=V(T, 128),
    raw=V32(T, C), step=V32(T, C), u=V32(T, C), Bb=V32(T, N, 128), Cb=V32(T, N, 128),
    nr2h=V32(2, N, W), pack=V(2, 2 * N, W), pack_sib=V(2 * N, W), chip_src=V(2 * N, W), chips=V(8, 2 * N, W), t01=V32(16, W),
    st_src=V32(N, W), st_sib=V32(N, W),
    pack_b=V(2, N, W), pack_b_sib=V(N, W), chip_b_src=V(N, W), chips_b=V(8, N, W),
    H=V32(T + 1, N, C), scan_out=V32(T, C),
    rs1_src=V(4, 32, D), rs1_dst=V(3, 32, D), rs2_src=V(4, 32, D), rs2_dst=V(3, 32, D),
    rs3_dst=V(3, 32, D),
    middle=V32(32, D), gmid=V32(32, D),

    gact=V32(4, 32, F), at_cot=V(16, 2, 48, T), at_nrm=V(16, 2, 48, T),
    l_cot=V(16, 48, 2 * T), l_nrm=V(16, 48, 2 * T), l_n2=V(16, 48, 2 * T), l_gmo=V(16, 48, 2 * T),
    b_out=V(2 * T, C), b_act=V(2 * T, F), b_gg=V(2 * T, F), b_gu=V(2 * T, F), b_gate=V(2 * T, C), b_in=V(2 * T, C),
    gr_fd=V(2, 4, 4, 48, 512), x_fd=V(2, 6, 2, 48, 512), y_fd=V(2, 6, 48, 512), gr_fg=V(2, 4, 4, 48, 512), x_fg=V(2, 6, 2, 48, 512), y_fg=V(2, 6, 48, 512),
    gr_fu=V(2, 4, 4, 48, 512), x_fu=V(2, 6, 2, 48, 512), y_fu=V(2, 3, 48, 512),
    gr_out=V(4, 4, 48, C), x_out=V(6, 2, 48, C), y_out=V(3, 48, C), gr_gate=V(4, 4, 48, C), x_gate=V(6, 2, 48, C), y_gate=V(3, 48, C),
    gr_in=V(2, 4, 4, 48, 384), x_in=V(2, 3, 4, 48, 384), y_in=V(2, 3, 48, 384),
    gso=V32(T, C), gstate=V32(N, C), PR=V32(T, N, 128), part_one=V(8 * T, C), part_two=V(8 * T, C), PE=V32(T, N, 128), rows=V32(T, C), er=V32(T, 128),
    gsr=V(T, C), gcs=V32(T + 8, C), halo2=V32(8, C), dn=V32(8, D), dg=V32(8, 128),
    nz2=V32(4, 4, 8, 128), first=V32(8, 128), first_recv=V32(8, 128), gr_first=V32(4, 4, 8, 128), x_first=V32(3, 4, 8, 128), y_first=V32(3, 8, 128), small=V32(16, 2, SMALL, 128), small_recv=V32(16, SMALL, 128),
    gr_small=V(4, 4, SMALL, 128), x_small=V(3, 4, SMALL, 128), y_small=V(3, SMALL, 128),
)


def local(
    tokens, cotangent, norm_first, in_inner, in_gate, conv_weight, conv_bias, projector, projector_gains, step_weight, step_bias,
    log_rates, skip_gain, out_weight, norm_second, gate_weight, up_weight, down_weight,
):
    y, gt, big, small = pl.pallas_call(
        kernel,
        out_shape=[pltpu.VMEM(shape, dtype) for shape, dtype in OUTS.values()],
        in_specs=[pl.BlockSpec(memory_space=m) for m in INS.values()],
        out_specs=[pl.BlockSpec(memory_space=VMEM) for _ in OUTS],
        scratch_shapes=list(SCRATCH.values()),
        compiler_params=pltpu.CompilerParams(collective_id=0, has_side_effects=True, vmem_limit_bytes=int(61.9 * 2**20)),
    )(
        tokens, cotangent, in_inner, in_gate, projector, step_weight, out_weight, gate_weight, up_weight, down_weight,
        conv_weight, conv_bias, step_bias, skip_gain, norm_first, norm_second, projector_gains, log_rates.T,
    )
    widths = (F, F, F, C, C, C)
    shapes = [(T, D)] * 2 + [(48, w) for w in widths] + [(4, C), (24, R), (N, 24), (4, 24)] + [(1, 24)] * 3 + [(1, 48)] * 2 + [(1, 4)]
    res = pl.pallas_call(
        hand_out,
        out_shape=[jax.ShapeDtypeStruct(sh, F32 if i > 1 else BF16) for i, sh in enumerate(shapes)],
        in_specs=[pl.BlockSpec(memory_space=VMEM)] * 4,
        out_specs=[pl.BlockSpec(memory_space=HBM if i < 8 else VMEM) for i in range(len(shapes))],
        scratch_shapes=[S(8)],
        compiler_params=pltpu.CompilerParams(vmem_limit_bytes=2 * 2**20),
    )(*(pltpu.with_memory_space_constraint(v, VMEM) for v in (y.reshape(T, D), gt.reshape(T, D), big, small)))
    y, gt, fd, fg, fu, out, gate, inn, proj, step_w, rates, taps, cbias, sbias, skip, first, second, gains = res
    return (
        y, gt, first[0], inn, gate, taps, cbias[0], proj.T, gains[0], step_w.T, sbias[0], rates.T, skip[0], out.T, second[0], fg, fu, fd.T,
    )


def hand_out(y, gt, big, small, *refs):
    outs, sem = refs[:-1], refs[-1]
    parts, at = [], 0
    for o in outs[2:8]:
        parts.append(big.at[:, at : at + o.shape[1]])
        at += o.shape[1]
    parts = [pltpu.make_async_copy(v, o, sem.at[i]) for i, (v, o) in enumerate(zip([*parts, y, gt], [*outs[2:8], *outs[:2]]))]
    start(parts)
    proj, step_w, rates, taps, cbias, sbias, skip, first, second, gains = outs[8:]
    for i in range(4):
        for j in range(6):
            proj[i : i + 1, 128 * j : 128 * j + 128] = small[i * 6 + j : i * 6 + j + 1, :]
    step_w[...] = small[24:48, 0:R]
    turned = jnp.concatenate([small[24:48, :], jnp.zeros((104, 128), F32)], axis=0).T
    rates[...] = turned[R : R + N, 0:24]
    taps[...] = turned[R + N : R + N + 4, 0:24]
    for i, o in enumerate((cbias, sbias, skip)):
        o[...] = turned[R + N + 4 + i : R + N + 5 + i, 0:24]
    first[...] = small[48:49, 0:48]
    second[...] = small[49:50, 0:48]
    gains[...] = small[50:51, 0:4]
    finish(parts)


def solution(mesh):
    row, col = P("seq", None), P(None, "head")
    flat, deep = P("head"), P("head", None)
    in_specs = (row, row, P(), col, col, col, flat, deep, P(), col, flat, deep, flat, deep, P(), col, col, deep)
    both, mix = ("head", "seq"), P("seq", "head")
    turned = P("head", "seq")
    out_specs = (
        row, row, P("seq"), mix, mix, P(None, both), P(both), turned, P("seq"), P(None, both), P(both), P(both, None), P(both),
        turned, P("seq"), mix, mix, turned,
    )
    return jax.shard_map(local, mesh=mesh, in_specs=in_specs, out_specs=out_specs, check_vma=False)
```

```python
import types

import jax
import jax.numpy as jnp
from jax import lax
from jax.experimental import pallas as pl
from jax.experimental.pallas import tpu as pltpu
from jax.sharding import PartitionSpec as P

F32 = jnp.float32
BF16 = jnp.bfloat16
T, D, C, F, N, R = 128, 1536, 768, 1024, 16, 96
GROUP = 16
EPS = 1e-5
LOG2E = 1.4426950408889634
HIGH = lax.Precision.HIGHEST
MESH = pl.DeviceIdType.MESH
SMALL = 48
SEMS = 112
W = 384


def dot(a, b, precision=None):
    return jnp.dot(a, b, precision=precision, preferred_element_type=F32)


def dot_nt(a, b, precision=None):
    return lax.dot_general(a, b, (((1,), (1,)), ((), ())), precision=precision, preferred_element_type=F32)


def tiles(total, width):
    return [slice(i, i + width) for i in range(0, total, width)]


def wide(v):
    return jnp.concatenate([v] * (W // 128), axis=1)


class Copy:
    def __init__(self, copy, sem, free):
        self.copy, self.sem, self.free = copy, sem, free

    def start(self):
        self.copy.start()

    def wait(self):
        self.copy.wait()
        self.free.append(self.sem)


def rcopy(src, dst, sems, device):
    send, recv, free = sems
    copy = pltpu.make_async_remote_copy(
        src_ref=src, dst_ref=dst, send_sem=send, recv_sem=recv, device_id=device, device_id_type=MESH
    )
    return Copy(copy, send, free)


def start(copies):
    for c in copies:
        c.start()
    return copies


def finish(copies):
    for c in copies:
        c.wait()


class Burst:
    def __init__(self, sems, src, dst, device):
        self.sems, self.all = sems, rcopy(src, dst, sems, device)

    def send(self, src, dst, device):
        rcopy(src, dst, self.sems, device).start()

    def wait(self):
        self.all.wait()


class Ring:
    def __init__(self, part, land, two, four, new, place, at):
        self.part, self.land, self.at, self.me = part, land, at, place
        self.right, self.left, self.far = lax.rem(place + 1, 4), lax.rem(place + 3, 4), lax.rem(place + 2, 4)
        self.first = Burst(new(), two, two, at(self.right))
        self.rest = Burst(new(), four, four, at(self.right))

    def begin(self):
        part, land, at, right, left, far = self.part, self.land, self.at, self.right, self.left, self.far
        self.first.send(part(far, 0), land(0, 0), at(right))
        self.first.send(part(far, 1), land(1, 1), at(left))
        self.rest.send(part(right, 1), land(2, 1), at(right))
        self.rest.send(part(left, 0), land(3, 0), at(left))

    def pass_on(self):
        self.first.wait()
        for h, d in enumerate((self.right, self.left)):
            own = self.part(d, h)
            own[...] = (own[...].astype(F32) + self.land(h, h)[...].astype(F32)).astype(own.dtype)
            self.rest.send(own, self.land(4 + h, h), self.at(d))

    def totals(self):
        self.rest.wait()
        for h, (a, b) in enumerate(((4, 3), (5, 2))):
            own = self.part(self.me, h)
            yield own, own[...].astype(F32) + (self.land(a, h)[...].astype(F32) + self.land(b, h)[...].astype(F32))


class Straight:
    def __init__(self, part, land, new, place, at):
        self.part, self.land, self.at, self.me = part, land, at, place
        self.burst = Burst(new(), land, land, at(lax.rem(place + 1, 4)))

    def begin(self):
        for k in (2, 1, 3):
            d = lax.rem(self.me + k, 4)
            self.burst.send(self.part(d), self.land.at[k - 1], self.at(d))

    def totals(self):
        self.burst.wait()
        own, land = self.part(self.me), self.land
        yield own, own[...].astype(F32) + ((land[0].astype(F32) + land[2].astype(F32)) + land[1].astype(F32))


class Unit:
    def __init__(self, grid, land_one, land_two, new, x, y, at, x_first, both_ways, split=0):
        along_x, along_y = (x, lambda d: at(d, y)), (y, lambda d: at(x, d))
        one, two = (along_x, along_y) if x_first else (along_y, along_x)

        def chunk(d, half=slice(0, 4)):
            return grid.at[half, d] if x_first else grid.at[d, half]

        def piece(d):
            return grid.at[d, x] if x_first else grid.at[y, d]

        if both_ways:
            self.one = Ring(
                lambda d, h: chunk(d, slice(2 * h, 2 * h + 2)), lambda i, h: land_one.at[i], land_one.at[0:2], land_one.at[2:6], new, *one
            )
        else:
            self.one = Straight(chunk, land_one, new, *one)
        if split:

            def side(ref, h):
                return ref.at[:, split:] if h else ref.at[:, 0:split]

            self.two = Ring(
                lambda d, h: side(piece(d), h), lambda i, h: side(land_two.at[i], h), land_two.at[0], land_two.at[0:2], new, *two
            )
        else:
            self.two = Straight(piece, land_two, new, *two)

    def a0(self):
        self.one.begin()

    def a1(self):
        self.one.pass_on()

    def add(self):
        for own, v in self.one.totals():
            own[...] = v.astype(own.dtype)

    def a2(self):
        self.add()
        self.two.begin()

    def b1(self):
        self.two.pass_on()

    def done(self):
        return [v for _, v in self.two.totals()]


def kernel(*refs):
    r = types.SimpleNamespace(**dict(zip([*INS, *OUTS, *SCRATCH], refs, strict=True)))
    s = lax.axis_index("seq")
    z = lax.axis_index("head")
    p = lax.rem(s, GROUP)
    base = s - p
    core = lax.rem(s, 2)
    x = lax.rem(s // 2, 4)
    y = s // 8

    def zdev(k):
        return (s, lax.rem(z + k, 4))

    def gdev(k):
        return (base + lax.rem(p + k, GROUP), z)

    def chip(cx, cy):
        return (cy * 8 + cx * 2 + core, z)

    sibling = (s + 1 - 2 * core, z)
    taken = []

    def new():
        taken.append(0)
        return r.sem.at[len(taken) - 1]

    free = []

    def sender():
        return free.pop() if free else new()

    def pair():
        return sender(), new(), free

    def local(src, dst):
        sem = sender()
        return Copy(pltpu.make_async_copy(src, dst, sem), sem, free)

    barrier = pltpu.get_barrier_semaphore()
    for k in range(1, 4):
        pl.semaphore_signal(barrier, 1, device_id=zdev(k), device_id_type=MESH)

    mates = sorted(((dy + min(dx, 4 - dx), dy, dx) for dy in range(2) for dx in range(4)), reverse=True)[:7]

    def mate(dy, dx):
        return base + lax.rem(y + dy, 2) * 8 + lax.rem(x + dx, 4) * 2 + core

    others = [(mate(dy, dx), z) for _, dy, dx in mates]
    for device in (*others, sibling, gdev(15 - 14 * core), (s + 8 * (3 - 2 * y), z)):
        pl.semaphore_signal(barrier, 1, device_id=device, device_id_type=MESH)

    def load(src, dst):
        c = local(src, dst)
        c.start()
        return c

    few = [load(v, o) for v, o in ((r.in_taps, r.s_taps), (r.in_cbias, r.s_cbias), (r.in_sbias, r.s_sbias), (r.in_skip, r.s_skip), (r.in_first, r.s_first), (r.in_second, r.s_second), (r.in_gains, r.s_gains), (r.in_rates, r.s_rates))]
    ld_tok = load(r.in_tok, r.tok)
    ld_in = load(r.in_w_in, r.w_in)

    finish(few)
    vec = r.vec
    vec[0:4, :] = r.s_taps[...]
    for i, v in enumerate((r.s_cbias, r.s_sbias, r.s_skip)):
        vec[4 + i : 5 + i, :] = v[...].reshape(1, C)
    g1 = r.s_first[...].reshape(1, D)
    g2 = r.s_second[...].reshape(1, D)
    nr = -jnp.exp(r.s_rates[...])
    r.nr[...] = nr
    nr2 = nr * LOG2E
    r.nr2[...] = nr2
    for j, c in enumerate(tiles(C, W)):
        r.nr2h[j] = nr2[:, c]

    ld_tok.wait()
    for rows in tiles(T, 32):
        v = r.tok[rows, :].astype(F32)
        rs = lax.rsqrt(jnp.mean(v * v, axis=-1, keepdims=True) + EPS)
        r.rinv[rows, :] = jnp.broadcast_to(rs, (32, 128))
        r.normed[rows, :] = (v * rs * g1).astype(BF16)
    ld_gate = load(r.in_w_gate, r.w_gate)
    ld_cot = load(r.in_cot, r.cot)
    ld_fd = load(r.in_w_fd, r.w_fd)
    ld_proj = load(r.in_w_proj, r.w_proj)
    r.w_step[...] = jnp.zeros((T, C), BF16)
    ld_step = load(r.in_w_step, r.w_step.at[0:R])
    ld_out = load(r.in_w_out, r.w_out)
    ld_fg = load(r.in_w_fg, r.w_fg)
    ld_fu = load(r.in_w_fu, r.w_fu)
    ld_in.wait()
    nrm = r.normed[...]
    for c in tiles(C, 256):
        r.ext[8 : 8 + T, c] = dot(nrm, r.w_in[:, c]).astype(BF16).astype(F32)
    pl.semaphore_wait(barrier, 3 + 7 + 3)
    halo = start([rcopy(r.ext.at[T : T + 8], r.halo, pair(), gdev(1))])
    ld_gate.wait()
    for c in tiles(C, 256):
        r.gate_in[:, c] = dot(nrm, r.w_gate[:, c])

    def turned(value, at, lhs):
        at[...] = value.T.reshape(16, 2, 48, T)
        lhs[:, :, 0:T] = at[:, core]
        return start([rcopy(at.at[:, 1 - core], lhs.at[:, :, T : 2 * T], pair(), sibling)])

    def both(b):
        return start([rcopy(b.at[0:T], b.at[T : 2 * T], pair(), sibling)])

    finish(halo)
    r.ext[0:8, :] = jnp.where(p == 0, 0.0, r.halo[...])
    for c in tiles(C, 128):
        tot = vec[4:5, c] + vec[0:1, c] * r.ext[5 : 5 + T, c]
        for k in range(1, 4):
            tot = tot + vec[k : k + 1, c] * r.ext[5 + k : 5 + k + T, c]
        r.conv_sum[:, c] = tot
        r.inner[:, c] = (tot * jax.nn.sigmoid(tot)).astype(BF16)

    def zgather(buf):
        burst = Burst(pair(), buf.at[0:3], buf.at[0:3], zdev(1))
        for k in (2, 1, 3):
            burst.send(buf.at[z], buf.at[z], zdev(k))
        return burst

    def zsum(buf):
        burst = zgather(buf)

        def result():
            burst.wait()
            return (buf[0].astype(F32) + buf[1].astype(F32)) + (buf[2].astype(F32) + buf[3].astype(F32))

        return result

    ld_proj.wait()
    r.pz[z] = dot(r.inner[...], r.w_proj[...]).astype(BF16)
    projected = zsum(r.pz)

    ld_cot.wait()
    ld_fd.wait()
    cot = r.cot[...]
    for c in tiles(F, 256):
        r.gact[:, :, c] = dot_nt(cot, r.w_fd[c, :]).reshape(4, 32, 256)

    tn_cot = turned(cot, r.at_cot, r.l_cot)
    tn_nrm = turned(nrm, r.at_nrm, r.l_nrm)

    proj = projected()
    r.proj[...] = proj
    lane = lax.broadcasted_iota(jnp.int32, (1, 128), 1)
    m1 = (lane < R).astype(F32)
    m3 = (lane >= R + N).astype(F32)
    m2 = 1.0 - m1 - m3

    def by_part(v):
        return (
            m1 * (jnp.sum(v * m1, -1, keepdims=True) / R)
            + m2 * (jnp.sum(v * m2, -1, keepdims=True) / N)
            + m3 * (jnp.sum(v * m3, -1, keepdims=True) / N)
        )

    rr = lax.rsqrt(by_part(proj * proj) + EPS)
    r.proj_r[...] = rr
    gains_in = r.s_gains[...].reshape(1, 128)
    pn = proj * rr * gains_in
    r.pn[...] = pn
    step_in = (pn * m1).astype(BF16)
    r.step_in[...] = step_in
    ld_step.wait()
    for c in tiles(C, 256):
        raw = dot(step_in, r.w_step[:, c]) + vec[5:6, c]
        r.raw[:, c] = raw
        st = jnp.maximum(raw, 0.0) + jnp.log1p(jnp.exp(-jnp.abs(raw)))
        r.step[:, c] = st
        r.u[:, c] = st * r.inner[:, c].astype(F32)
    rown = lax.broadcasted_iota(jnp.int32, (N, 128), 0)
    lanes = lax.broadcasted_iota(jnp.int32, (N, 128), 1)
    selb = (lanes == rown + R).astype(F32)
    selc = (lanes == rown + R + N).astype(F32)
    sel = selb + selc
    part_of = lax.broadcasted_iota(jnp.int32, (128, 256), 0) - jnp.where(lax.broadcasted_iota(jnp.int32, (128, 256), 1) < 128, R, R + N)
    to_lanes = ((part_of >= 0) & (part_of < N)).astype(BF16)

    for rows in tiles(T, 32):
        some = r.pn[rows, :]
        one = jnp.concatenate([jnp.broadcast_to(some[i : i + 1, :], (N, 128)) * sel for i in range(32)], axis=0)
        high = one.astype(BF16)
        low = (one - high.astype(F32)).astype(BF16)
        v = dot(high, to_lanes) + dot(low, to_lanes)
        r.Bb[rows] = v[:, 0:128].reshape(32, N, 128)
        r.Cb[rows] = v[:, 128:256].reshape(32, N, 128)

    top = lax.broadcasted_iota(jnp.int32, (N, W), 0) < 8

    def coded(ref, h, tot):
        high = tot.astype(BF16).astype(F32)
        ref[0:N, :] = h.astype(BF16)
        ref[N : 2 * N, :] = jnp.where(top, high, tot - high).astype(BF16)

    def state_of(ref):
        return ref[0:N, :].astype(F32)

    def steps_of(ref):
        v = ref[N : 2 * N, :].astype(F32)
        return v[0:1, :] + v[8:9, :]

    for half, c in enumerate(tiles(C, W)):
        a2 = r.nr2[:, c]

        def first(b, h):
            st = r.step[pl.ds(b * 8, 8), c]
            uu = r.u[pl.ds(b * 8, 8), c]
            for i in range(8):
                h = jnp.exp2(a2 * st[i : i + 1, :]) * h + uu[i : i + 1, :] * wide(r.Bb[b * 8 + i])
            return h

        h = lax.fori_loop(0, T // 8, first, jnp.zeros((N, W), F32))
        coded(r.pack.at[half], h, jnp.sum(r.step[:, c], axis=0, keepdims=True))

    nth = p // 2
    is_first = core == 0
    a2c = r.nr2h[core]

    def to_mates(src, land):
        burst = Burst(pair(), land.at[0:7], land.at[0:7], sibling)
        for device in others:
            burst.send(src, land.at[nth], device)
        land[nth] = src[...]
        return burst.wait

    def to_sibling(src, dst):
        return start([rcopy(src, dst, pair(), sibling)])

    finish(to_sibling(r.pack.at[1 - core], r.pack_sib))
    h_own, h_sib = state_of(r.pack.at[core]), state_of(r.pack_sib)
    t_own, t_sib = steps_of(r.pack.at[core]), steps_of(r.pack_sib)
    h0, h1 = jnp.where(is_first, h_own, h_sib), jnp.where(is_first, h_sib, h_own)
    t0, t1 = jnp.where(is_first, t_own, t_sib), jnp.where(is_first, t_sib, t_own)
    r.t01[0:1, :] = t0
    r.t01[8:9, :] = t1
    coded(r.chip_src, jnp.exp2(a2c * t1) * h0 + h1, t0 + t1)
    swapped = to_mates(r.chip_src, r.chips)
    ld_fu.wait()
    for c in tiles(F, 256):
        r.w_fd[c, :] = r.w_fu[:, c].T
    finish(tn_cot)
    finish(tn_nrm)
    swapped()
    state = jnp.zeros((N, W), F32)
    for j in range(7):
        at = r.chips.at[j]
        state = jnp.where(j < nth, jnp.exp2(a2c * steps_of(at)) * state + state_of(at), state)
    later = jnp.exp2(a2c * t0) * state + h0
    r.st_src[...] = jnp.where(is_first, later, state)
    entering = to_sibling(r.st_src, r.st_sib)
    state = jnp.where(is_first, state, later)
    finish(entering)
    for half, c in enumerate(tiles(C, W)):
        r.H[0, :, c] = jnp.where(core == half, state, r.st_sib[...])

    eights = (lax.broadcasted_iota(jnp.int32, (16, 128), 1) // 8 == lax.broadcasted_iota(jnp.int32, (16, 128), 0)).astype(BF16)

    def folded(v):
        return v[0:8, :] + v[8:16, :]

    def finished(part, out):
        for j in range(8):
            out[16 * j : 16 * j + 16, :] = dot(eights, part[128 * j : 128 * j + 128, :])

    for c in tiles(C, W):
        a2 = r.nr2[:, c]

        def second(b, h):
            st = r.step[pl.ds(b * 8, 8), c]
            uu = r.u[pl.ds(b * 8, 8), c]
            rows = []
            for i in range(8):
                h = jnp.exp2(a2 * st[i : i + 1, :]) * h + uu[i : i + 1, :] * wide(r.Bb[b * 8 + i])
                r.H[b * 8 + i + 1, :, c] = h
                rows.append(folded(h * wide(r.Cb[b * 8 + i])))
            r.part_one[pl.ds(pl.multiple_of(b * 64, 64), 64), c] = jnp.concatenate(rows, axis=0).astype(BF16)
            return h

        lax.fori_loop(0, T // 8, second, r.H[0, :, c])

    finished(r.part_one, r.scan_out)
    for c in tiles(C, 128):
        so = r.scan_out[:, c] + vec[6:7, c] * r.inner[:, c].astype(F32)
        r.scan_out[:, c] = so
        gi = r.gate_in[:, c]
        r.b_out[0:T, c] = (so * (gi * jax.nn.sigmoid(gi))).astype(BF16)
    by_out = both(r.b_out)

    def zscatter(src, dst):
        return Burst(pair(), src.at[0:3], dst, zdev(1))

    def zsend(burst, src, dst, j):
        c = slice(512 * j, 512 * j + 512)
        for k in (2, 1, 3):
            burst.send(src.at[lax.rem(z + k, 4), :, c], dst.at[k - 1, :, c], zdev(k))

    def zsummed(src, dst, burst):
        burst.wait()
        return (src[z].astype(F32) + dst[0].astype(F32)) + (dst[1].astype(F32) + dst[2].astype(F32))

    def fours(v):
        return v.astype(BF16).reshape(4, 32, v.shape[-1])

    ld_out.wait()
    own = pl.ds(pl.multiple_of(z * 32, 32), 32)
    halves = tiles(32, 16)
    mixed = r.b_out[0:T, :].reshape(4, 32, C)
    sent = []
    for hs in halves:
        some = mixed[:, hs].reshape(64, C)
        for c in tiles(D, 512):
            r.rs1_src[:, hs, c] = dot(some, r.w_out[:, c]).astype(BF16).reshape(4, 16, 512)
        burst = Burst(pair(), r.rs1_src.at[0:3, hs], r.rs1_dst.at[:, hs], zdev(1))
        for k in (2, 1, 3):
            burst.send(r.rs1_src.at[lax.rem(z + k, 4), hs], r.rs1_dst.at[k - 1, hs], zdev(k))
        sent.append(burst)
    gathered = []
    for hs, burst in zip(halves, sent):
        burst.wait()
        terms = [r.rs1_src[z, hs], *(r.rs1_dst[k, hs] for k in range(3))]
        rows = pl.ds(pl.multiple_of(z * 32 + hs.start, 16), 16)
        middle = r.tok[rows, :].astype(F32) + sum((v.astype(F32) for v in terms[1:]), terms[0].astype(F32))
        r.middle[hs, :] = middle
        r2 = lax.rsqrt(jnp.mean(middle * middle, axis=-1, keepdims=True) + EPS)
        r.out_y[z, hs] = (middle * r2 * g2).astype(BF16)
        burst = Burst(pair(), r.out_y.at[0:3, hs], r.out_y.at[0:3, hs], zdev(1))
        for k in (2, 1, 3):
            burst.send(r.out_y.at[z, hs], r.out_y.at[z, hs], zdev(k))
        gathered.append(burst)

    def unit(grid, land_one, land_two, x_first, both_ways=True, split=0):
        return Unit(grid, land_one, land_two, pair, x, y, chip, x_first, both_ways, split)

    def product_of(grid, lhs, b, lo, n):
        left = lhs[...].reshape(D // 2, 2 * T)
        for c in tiles(n, 256 if n % 256 == 0 else 128):
            cols = slice(lo + c.start, lo + c.stop)
            grid[:, :, :, c] = dot(left, b[:, cols]).astype(BF16).reshape(4, 4, 48, c.stop - c.start)

    def store_out(u, lo, n):
        at = lo
        for v in u.done():
            r.out_big[:, at : at + v.shape[1]] = v
            at += v.shape[1]

    u_fd = [unit(r.gr_fd.at[i], r.x_fd.at[i], r.y_fd.at[i], i == 0, split=256) for i in range(2)]
    u_fg = [unit(r.gr_fg.at[i], r.x_fg.at[i], r.y_fg.at[i], i == 0, split=256) for i in range(2)]
    u_fu = [unit(r.gr_fu.at[i], r.x_fu.at[i], r.y_fu.at[i], i == 0) for i in range(2)]

    def halves_of(units, grids, lhs, b):
        for i in range(2):
            product_of(grids.at[i], lhs, b, 512 * i, 512)
            units[i].a0()

    u_out = unit(r.gr_out, r.x_out, r.y_out, True)
    u_gate = unit(r.gr_gate, r.x_gate, r.y_gate, False)
    u_in = [unit(r.gr_in.at[i], r.x_in.at[i], r.y_in.at[i], i == 0, False) for i in range(2)]
    u_small = unit(r.gr_small, r.x_small, r.y_small, True, False)
    u_first = unit(r.gr_first, r.x_first, r.y_first, False, False)

    ld_fg.wait()
    for hs, burst in zip(halves, gathered):
        burst.wait()
        some = r.out_y[:, hs].reshape(64, D)
        for c in tiles(F, 256):
            g = dot(some, r.w_fg[:, c])
            u = dot(some, r.w_fu[:, c])
            ga = r.gact[:, hs, c].reshape(64, 256)
            sg = jax.nn.sigmoid(g)
            sl = g * sg
            for b, v in ((r.b_act, sl * u), (r.b_gg, ga * u * (sg * (1.0 + g * (1.0 - sg)))), (r.b_gu, ga * sl)):
                v = v.astype(BF16)
                for q in range(4):
                    b[32 * q + hs.start : 32 * q + hs.stop, c] = v[16 * q : 16 * q + 16, :]
    n2 = r.out_y[...].reshape(T, D)
    by_act = both(r.b_act)
    gg = r.b_gg[0:T, :]
    gu = r.b_gu[0:T, :]
    sent = zscatter(r.rs2_src, r.rs2_dst)
    for j, c in enumerate(tiles(D, 512)):
        r.rs2_src[:, :, c] = fours(dot_nt(gg, r.w_fg[c, :]) + dot(gu, r.w_fd[:, c]))
        zsend(sent, r.rs2_src, r.rs2_dst, j)
    ld_fd = load(r.in_w_fd, r.w_fd)
    by_gg = both(r.b_gg)
    by_gu = both(r.b_gu)
    tn_n2 = turned(n2, r.at_cot, r.l_n2)

    finish(by_act)
    halves_of(u_fd, r.gr_fd, r.l_cot, r.b_act)
    finish(tn_n2)
    finish(by_gg)
    halves_of(u_fg, r.gr_fg, r.l_n2, r.b_gg)
    finish(by_gu)
    halves_of(u_fu, r.gr_fu, r.l_n2, r.b_gu)

    gy = zsummed(r.rs2_src, r.rs2_dst, sent)
    v = r.middle[...]
    r2 = lax.rsqrt(jnp.mean(v * v, axis=-1, keepdims=True) + EPS)
    vr = v * r2
    gn = gy * g2
    gm = r.cot[own, :].astype(F32) + r2 * (gn - vr * jnp.mean(vr * gn, axis=-1, keepdims=True))
    r.gmid[...] = gm
    r.out_gt[z] = gm.astype(BF16)
    got = zgather(r.out_gt)
    r.dn[1:2, :] = jnp.sum(vr * gy, axis=0, keepdims=True)
    act = r.b_act[0:T, :]
    ld_fd.wait()
    sent3 = zscatter(r.rs1_src, r.rs3_dst)
    for j, c in enumerate(tiles(D, 512)):
        r.rs1_src[:, :, c] = fours(dot(act, r.w_fd[:, c]))
        zsend(sent3, r.rs1_src, r.rs3_dst, j)

    def owner(shape):
        i = lax.broadcasted_iota(jnp.int32, shape, 0)
        return 2 * (i & 15) + (i >> 4)

    def rows_of(v, width, hot):
        k = lax.broadcasted_iota(jnp.int32, (32, v.shape[1]), 1) - width * owner((32, v.shape[1]))
        one = jnp.where((k >= 0) & (k < width), v, 0.0)
        high = one.astype(BF16)
        return dot(high, hot) + dot((one - high.astype(F32)).astype(BF16), hot)

    kk = lax.broadcasted_iota(jnp.int32, (D, 128), 0)
    hot = lax.broadcasted_iota(jnp.int32, (D, 128), 1) == kk - 48 * ((kk * 683) >> 15)
    r.at_cot[...] = hot.astype(BF16).reshape(16, 2, 48, T)
    got.wait()
    for u in u_fd:
        u.a1()

    gmo = r.out_gt[...].reshape(T, D)
    for c in tiles(C, 256):
        gmx = dot_nt(gmo, r.w_out[c, :])
        gi = r.gate_in[:, c]
        sg = jax.nn.sigmoid(gi)
        r.gso[:, c] = gmx * (gi * sg)
        r.b_gate[0:T, c] = (gmx * r.scan_out[:, c] * (sg * (1.0 + gi * (1.0 - sg)))).astype(BF16)
    by_gate = both(r.b_gate)
    tn_gmo = turned(gmo, r.at_nrm, r.l_gmo)

    def rev_first(c):
        a2 = r.nr2[:, c]

        def body(k, cr):
            b = T // 8 - 1 - k
            st = r.step[pl.ds(b * 8, 8), c]
            gs = r.gso[pl.ds(b * 8, 8), c]
            for i in range(7, -1, -1):
                cr = jnp.exp2(a2 * st[i : i + 1, :]) * (gs[i : i + 1, :] * wide(r.Cb[b * 8 + i]) + cr)
            return cr

        cr = lax.fori_loop(0, T // 8, body, jnp.zeros((N, W), F32))
        r.pack_b[0 if c.start == 0 else 1] = cr.astype(BF16)

    for c in tiles(C, W):
        rev_first(c)
    finish(to_sibling(r.pack_b.at[1 - core], r.pack_b_sib))
    c_own, c_sib = r.pack_b[core].astype(F32), r.pack_b_sib[...].astype(F32)
    c0, c1 = jnp.where(is_first, c_own, c_sib), jnp.where(is_first, c_sib, c_own)
    t0, t1 = r.t01[0:1, :], r.t01[8:9, :]
    r.chip_b_src[...] = (c0 + jnp.exp2(a2c * t0) * c1).astype(BF16)
    swapped = to_mates(r.chip_b_src, r.chips_b)
    for u in u_fg:
        u.a1()
    hot = r.at_cot[...].reshape(D, 128)
    finish(by_gate)
    product_of(r.gr_gate, r.l_nrm, r.b_gate, 0, C)
    u_gate.a0()
    finish(tn_gmo)
    finish(by_out)
    product_of(r.gr_out, r.l_gmo, r.b_out, 0, C)
    u_out.a0()

    def read_rows(b, carry):
        gs = r.gso[pl.ds(b * 8, 8), :]
        for i in range(8):
            pr = gs[i : i + 1, :] * r.H[b * 8 + i + 1]
            r.PR[b * 8 + i] = sum((pr[:, k] for k in tiles(C, 128)[1:]), pr[:, 0:128])
        return carry

    lax.fori_loop(0, T // 8, read_rows, 0)
    for c in tiles(C, 256):
        r.w_out[c, :] = r.w_gate[:, c].T
    swapped()
    for u in u_fu:
        u.a1()
    state = jnp.zeros((N, W), F32)
    for j in range(7, 0, -1):
        state = jnp.where(j > nth, r.chips_b[j].astype(F32) + jnp.exp2(a2c * steps_of(r.chips.at[j])) * state, state)
    later = c1 + jnp.exp2(a2c * t1) * state
    r.st_src[...] = jnp.where(is_first, state, later)
    entering = to_sibling(r.st_src, r.st_sib)
    state = jnp.where(is_first, later, state)
    r.out_y[z] = (r.middle[...] + zsummed(r.rs1_src, r.rs3_dst, sent3)).astype(BF16)
    sent_out = zgather(r.out_y)
    finish(entering)
    for half, c in enumerate(tiles(C, W)):
        r.gstate[:, c] = jnp.where(core == half, state, r.st_sib[...])

    def rev_second(c):
        a2 = r.nr2[:, c]
        a = r.nr[:, c]

        def body(k, state):
            cr, gl = state
            b = T // 8 - 1 - k
            st = r.step[pl.ds(b * 8, 8), c]
            gs = r.gso[pl.ds(b * 8, 8), c]
            uu = r.u[pl.ds(b * 8, 8), c]
            s1, s2 = [None] * 8, [None] * 8
            for i in range(7, -1, -1):
                t = b * 8 + i
                si, gi, ui = st[i : i + 1, :], gs[i : i + 1, :], uu[i : i + 1, :]
                g = gi * wide(r.Cb[t]) + cr
                s1[i] = folded(g * wide(r.Bb[t]))
                pe = g * ui
                pe = (pe[:, 0:128] + pe[:, 128:256]) + pe[:, 256:384]
                if c.start:
                    pe = pe + r.PE[t]
                r.PE[t] = pe
                cr = jnp.exp2(a2 * si) * g
                q = cr * r.H[t, :, c]
                s2[i] = folded(q * a)
                gl = gl + q * si
            rows = pl.ds(pl.multiple_of(b * 64, 64), 64)
            r.part_one[rows, c] = jnp.concatenate(s1, axis=0).astype(BF16)
            r.part_two[rows, c] = jnp.concatenate(s2, axis=0).astype(BF16)
            return cr, gl

        _, gl = lax.fori_loop(0, T // 8, body, (r.gstate[:, c], jnp.zeros((N, W), F32)))
        r.rows[R : R + N, c] = gl * a

    for c in tiles(C, W):
        rev_second(c)
    finished(r.part_one, r.gate_in)
    finished(r.part_two, r.scan_out)

    ones = jnp.ones((128, 128), BF16)

    for tok in tiles(T, 32):
        pe = dot(r.PE[tok].reshape(32 * N, 128).astype(BF16), ones).reshape(32, N, 128)
        pr = dot(r.PR[tok].reshape(32 * N, 128).astype(BF16), ones).reshape(32, N, 128)
        r.er[tok, :] = jnp.sum(pe * selb[None] + pr * selc[None], axis=1)
    for c in tiles(C, 256):
        inner = r.inner[:, c].astype(F32)
        s1 = r.gate_in[:, c]
        raw_g = (r.scan_out[:, c] + s1 * inner) * jax.nn.sigmoid(r.raw[:, c])
        r.gsr[:, c] = raw_g.astype(BF16)
        r.rows[R + N + 5 : R + N + 6, c] = jnp.sum(raw_g, axis=0, keepdims=True)
        gso = r.gso[:, c]
        r.rows[R + N + 6 : R + N + 7, c] = jnp.sum(gso * inner, axis=0, keepdims=True)
        r.gate_in[:, c] = gso * vec[6:7, c] + s1 * r.step[:, c]
    r.pz[z] = (dot_nt(r.gsr[...], r.w_step[...]) + r.er[...]).astype(BF16)
    summed = zsum(r.pz)
    for c in tiles(C, 256):
        r.w_fd[c, :] = r.w_in[:, c].T
    u_out.a1()
    u_gate.a1()
    gy = summed()
    vr = r.proj[...] * r.proj_r[...]
    gn = gy * gains_in
    gpj = (r.proj_r[...] * (gn - vr * by_part(vr * gn))).astype(BF16)
    r.dg[...] = jnp.broadcast_to(jnp.sum(vr * gy, axis=0, keepdims=True), (8, 128))
    for c in tiles(C, 256):
        gi = r.gate_in[:, c] + dot_nt(gpj, r.w_proj[c, :])
        cs = r.conv_sum[:, c]
        sg = jax.nn.sigmoid(cs)
        r.gcs[0:T, c] = gi * (sg * (1.0 + cs * (1.0 - sg)))
    halo = start([rcopy(r.gcs.at[0:8], r.halo2, pair(), gdev(15))])
    for c in tiles(C, 128):
        gc = r.gcs[0:T, c]
        for k in range(4):
            r.rows[R + N + k : R + N + k + 1, c] = jnp.sum(gc * r.ext[5 + k : 5 + k + T, c], axis=0, keepdims=True)
        r.rows[R + N + 4 : R + N + 5, c] = jnp.sum(gc, axis=0, keepdims=True)
    r.rows[0:R, :] = jnp.zeros((R, C), F32)
    r.rows[R + N + 7 : T, :] = jnp.zeros((T - R - N - 7, C), F32)
    chan = (dot(r.gsr[...].T, r.step_in[...]) + r.rows[...].T).reshape(16, 2, 24, 128)
    ll = lax.broadcasted_iota(jnp.int32, (128, 128), 0)
    order = (lax.broadcasted_iota(jnp.int32, (128, 128), 1) == 4 * (2 * (ll & 15) + ((ll >> 4) & 1)) + (ll >> 5)).astype(BF16)
    pt = dot(dot_nt(order, gpj).astype(BF16), r.inner[...])
    for h in range(2):
        r.small[:, h, 24:48, :] = chan[:, h]
        for i in range(4):
            for j in range(6):
                r.small[:, h, i * 6 + j, :] = pt[32 * i + 16 * h : 32 * i + 16 * h + 16, 128 * j : 128 * j + 128]
    by_small = start([rcopy(r.small.at[:, 1 - core], r.small_recv, pair(), sibling)])
    for u in (*u_fd, *u_fg, *u_fu,):
        u.a2()
    finish(halo)
    r.gcs[T : T + 8, :] = jnp.where(p == GROUP - 1, 0.0, r.halo2[...])
    for c in tiles(C, 128):
        tot = vec[3:4, c] * r.gcs[0:T, c]
        for k in range(3):
            tot = tot + vec[k : k + 1, c] * r.gcs[3 - k : 3 - k + T, c]
        r.b_in[0:T, c] = tot.astype(BF16)
    by_in = both(r.b_in)
    finish(by_small)
    r.gr_small[...] = (r.small[:, core] + r.small_recv[...]).astype(BF16).reshape(4, 4, SMALL, 128)
    u_small.a0()
    gip = r.b_in[0:T, :]
    ggi = r.b_gate[0:T, :]
    sent = zscatter(r.rs2_src, r.rs1_dst)
    for j, c in enumerate(tiles(D, 512)):
        gnp = dot(gip, r.w_fd[0:C, c]) + dot(ggi, r.w_out[:, c])
        r.rs2_src[:, :, c] = fours(gnp)
        if j < 2:
            zsend(sent, r.rs2_src, r.rs1_dst, j)
        r.dn[0:1, c] = jnp.sum(r.tok[:, c].astype(F32) * (r.rinv[:, 0:1] * gnp), axis=0, keepdims=True)
    k4 = lax.broadcasted_iota(jnp.int32, (128, 128), 0)
    hot4 = (lax.broadcasted_iota(jnp.int32, (128, 128), 1) == (k4 & 3)).astype(BF16)
    r.gr_first[...] = jnp.zeros((4, 4, 8, 128), F32)
    for i, v in enumerate((rows_of(r.dn[0:1, :], 48, hot), rows_of(r.dn[1:2, :], 48, hot), rows_of(r.dg[0:1, :] * 0.25, 4, hot4))):
        for h in range(2):
            r.gr_first[:, :, 2 * i + h, :] = v[16 * h : 16 * h + 16, :].reshape(4, 4, 128)
    u_first.a0()
    zsend(sent, r.rs2_src, r.rs1_dst, 2)
    finish(by_in)
    for i in range(2):
        product_of(r.gr_in.at[i], r.l_nrm, r.b_in, 384 * i, 384)
        u_in[i].a0()
    for u in (*u_fd, *u_fg):
        u.b1()
    u_small.a2()
    u_first.add()
    r.nz2[z] = r.gr_first[y]
    first = zsum(r.nz2)
    gn1 = zsummed(r.rs2_src, r.rs1_dst, sent)
    v = r.tok[own, :].astype(F32)
    rs = lax.rsqrt(jnp.mean(v * v, axis=-1, keepdims=True) + EPS)
    vr = v * rs
    gn = gn1 * g1
    r.out_gt[z] = (r.gmid[...] + rs * (gn - vr * jnp.mean(vr * gn, axis=-1, keepdims=True))).astype(BF16)
    sent_tok = zgather(r.out_gt)
    u_out.a2()
    u_gate.a2()
    r.gr_first[y] = first()
    u_first.two.begin()
    for u in u_in:
        u.a2()
    for i in range(2):
        store_out(u_fd[i], 512 * i, 512)
        store_out(u_fg[i], F + 512 * i, 512)
        store_out(u_fu[i], 2 * F + 512 * i, 512)
    r.out_small[0:SMALL, :] = u_small.done()[0]
    store_out(u_out, 3 * F, C)
    store_out(u_gate, 3 * F + C, C)
    r.first[...] = u_first.done()[0]
    by_first = start([rcopy(r.first, r.first_recv, pair(), sibling)])
    for i in range(2):
        store_out(u_in[i], 3 * F + 2 * C + 384 * i, 384)
    finish(by_first)
    r.first[...] = r.first[...] + r.first_recv[...]
    for i in range(3):
        r.out_small[SMALL + i : SMALL + i + 1, :] = r.first[pl.ds(2 * i + core, 1), :]
    sent_out.wait()
    sent_tok.wait()
    assert len(taken) == SEMS


def V(*shape, dtype=BF16):
    return pltpu.VMEM(shape, dtype)


def V32(*shape):
    return pltpu.VMEM(shape, F32)


def S(*shape):
    return pltpu.SemaphoreType.DMA(shape)


BIG = 3 * F + 3 * C
HBM, VMEM = pl.ANY, pltpu.VMEM
INS = dict(
    in_tok=HBM, in_cot=HBM, in_w_in=HBM, in_w_gate=HBM, in_w_proj=HBM, in_w_step=HBM, in_w_out=HBM, in_w_fg=HBM, in_w_fu=HBM,
    in_w_fd=HBM, in_taps=HBM, in_cbias=HBM, in_sbias=HBM, in_skip=HBM, in_first=HBM, in_second=HBM, in_gains=HBM, in_rates=HBM,
)
OUTS = dict(out_y=((4, 32, D), BF16), out_gt=((4, 32, D), BF16), out_big=((48, BIG), F32), out_small=((56, 128), F32))
SCRATCH = dict(
    s_taps=V32(4, C), s_cbias=V32(C), s_sbias=V32(C), s_skip=V32(C), s_first=V32(D), s_second=V32(D), s_gains=V32(128), s_rates=V32(N, C),
    sem=S(SEMS),
    tok=V(T, D), cot=V(T, D), w_in=V(D, C), w_gate=V(D, C), w_proj=V(C, 128), w_step=V(T, C), w_out=V(C, D), w_fg=V(D, F), w_fu=V(D, F),
    w_fd=V(F, D),
    vec=V32(8, C), nr=V32(N, C), nr2=V32(N, C), rinv=V32(T, 128), normed=V(T, D), ext=V32(T + 8, C), halo=V32(8, C),
    gate_in=V32(T, C), conv_sum=V32(T, C), inner=V(T, C),
    pz=V(4, T, 128), proj=V32(T, 128), proj_r=V32(T, 128), pn=V32(T, 128), step_in=V(T, 128),
    raw=V32(T, C), step=V32(T, C), u=V32(T, C), Bb=V32(T, N, 128), Cb=V32(T, N, 128),
    nr2h=V32(2, N, W), pack=V(2, 2 * N, W), pack_sib=V(2 * N, W), chip_src=V(2 * N, W), chips=V(8, 2 * N, W), t01=V32(16, W),
    st_src=V32(N, W), st_sib=V32(N, W),
    pack_b=V(2, N, W), pack_b_sib=V(N, W), chip_b_src=V(N, W), chips_b=V(8, N, W),
    H=V32(T + 1, N, C), scan_out=V32(T, C),
    rs1_src=V(4, 32, D), rs1_dst=V(3, 32, D), rs2_src=V(4, 32, D), rs2_dst=V(3, 32, D),
    rs3_dst=V(3, 32, D),
    middle=V32(32, D), gmid=V32(32, D),

    gact=V32(4, 32, F), at_cot=V(16, 2, 48, T), at_nrm=V(16, 2, 48, T),
    l_cot=V(16, 48, 2 * T), l_nrm=V(16, 48, 2 * T), l_n2=V(16, 48, 2 * T), l_gmo=V(16, 48, 2 * T),
    b_out=V(2 * T, C), b_act=V(2 * T, F), b_gg=V(2 * T, F), b_gu=V(2 * T, F), b_gate=V(2 * T, C), b_in=V(2 * T, C),
    gr_fd=V(2, 4, 4, 48, 512), x_fd=V(2, 6, 2, 48, 512), y_fd=V(2, 6, 48, 512), gr_fg=V(2, 4, 4, 48, 512), x_fg=V(2, 6, 2, 48, 512), y_fg=V(2, 6, 48, 512),
    gr_fu=V(2, 4, 4, 48, 512), x_fu=V(2, 6, 2, 48, 512), y_fu=V(2, 3, 48, 512),
    gr_out=V(4, 4, 48, C), x_out=V(6, 2, 48, C), y_out=V(3, 48, C), gr_gate=V(4, 4, 48, C), x_gate=V(6, 2, 48, C), y_gate=V(3, 48, C),
    gr_in=V(2, 4, 4, 48, 384), x_in=V(2, 3, 4, 48, 384), y_in=V(2, 3, 48, 384),
    gso=V32(T, C), gstate=V32(N, C), PR=V32(T, N, 128), part_one=V(8 * T, C), part_two=V(8 * T, C), PE=V32(T, N, 128), rows=V32(T, C), er=V32(T, 128),
    gsr=V(T, C), gcs=V32(T + 8, C), halo2=V32(8, C), dn=V32(8, D), dg=V32(8, 128),
    nz2=V32(4, 4, 8, 128), first=V32(8, 128), first_recv=V32(8, 128), gr_first=V32(4, 4, 8, 128), x_first=V32(3, 4, 8, 128), y_first=V32(3, 8, 128), small=V32(16, 2, SMALL, 128), small_recv=V32(16, SMALL, 128),
    gr_small=V(4, 4, SMALL, 128), x_small=V(3, 4, SMALL, 128), y_small=V(3, SMALL, 128),
)


def local(
    tokens, cotangent, norm_first, in_inner, in_gate, conv_weight, conv_bias, projector, projector_gains, step_weight, step_bias,
    log_rates, skip_gain, out_weight, norm_second, gate_weight, up_weight, down_weight,
):
    y, gt, big, small = pl.pallas_call(
        kernel,
        out_shape=[pltpu.VMEM(shape, dtype) for shape, dtype in OUTS.values()],
        in_specs=[pl.BlockSpec(memory_space=m) for m in INS.values()],
        out_specs=[pl.BlockSpec(memory_space=VMEM) for _ in OUTS],
        scratch_shapes=list(SCRATCH.values()),
        compiler_params=pltpu.CompilerParams(collective_id=0, has_side_effects=True, vmem_limit_bytes=int(62.05 * 2**20)),
    )(
        tokens, cotangent, in_inner, in_gate, projector, step_weight, out_weight, gate_weight, up_weight, down_weight,
        conv_weight, conv_bias, step_bias, skip_gain, norm_first, norm_second, projector_gains, log_rates.T,
    )
    widths = (F, F, F, C, C, C)
    shapes = [(T, D)] * 2 + [(48, w) for w in widths] + [(4, C), (24, R), (N, 24), (4, 24)] + [(1, 24)] * 3 + [(1, 48)] * 2 + [(1, 4)]
    res = pl.pallas_call(
        hand_out,
        out_shape=[jax.ShapeDtypeStruct(sh, F32 if i > 1 else BF16) for i, sh in enumerate(shapes)],
        in_specs=[pl.BlockSpec(memory_space=VMEM)] * 4,
        out_specs=[pl.BlockSpec(memory_space=HBM if i < 8 else VMEM) for i in range(len(shapes))],
        scratch_shapes=[S(8)],
        compiler_params=pltpu.CompilerParams(vmem_limit_bytes=2 * 2**20),
    )(*(pltpu.with_memory_space_constraint(v, VMEM) for v in (y.reshape(T, D), gt.reshape(T, D), big, small)))
    y, gt, fd, fg, fu, out, gate, inn, proj, step_w, rates, taps, cbias, sbias, skip, first, second, gains = res
    return (
        y, gt, first[0], inn, gate, taps, cbias[0], proj.T, gains[0], step_w.T, sbias[0], rates.T, skip[0], out.T, second[0], fg, fu, fd.T,
    )


def hand_out(y, gt, big, small, *refs):
    outs, sem = refs[:-1], refs[-1]
    parts, at = [], 0
    for o in outs[2:8]:
        parts.append(big.at[:, at : at + o.shape[1]])
        at += o.shape[1]
    parts = [pltpu.make_async_copy(v, o, sem.at[i]) for i, (v, o) in enumerate(zip([*parts, y, gt], [*outs[2:8], *outs[:2]]))]
    start(parts)
    proj, step_w, rates, taps, cbias, sbias, skip, first, second, gains = outs[8:]
    for i in range(4):
        for j in range(6):
            proj[i : i + 1, 128 * j : 128 * j + 128] = small[i * 6 + j : i * 6 + j + 1, :]
    step_w[...] = small[24:48, 0:R]
    turned = jnp.concatenate([small[24:48, :], jnp.zeros((104, 128), F32)], axis=0).T
    rates[...] = turned[R : R + N, 0:24]
    taps[...] = turned[R + N : R + N + 4, 0:24]
    for i, o in enumerate((cbias, sbias, skip)):
        o[...] = turned[R + N + 4 + i : R + N + 5 + i, 0:24]
    first[...] = small[48:49, 0:48]
    second[...] = small[49:50, 0:48]
    gains[...] = small[50:51, 0:4]
    finish(parts)


def solution(mesh):
    row, col = P("seq", None), P(None, "head")
    flat, deep = P("head"), P("head", None)
    in_specs = (row, row, P(), col, col, col, flat, deep, P(), col, flat, deep, flat, deep, P(), col, col, deep)
    both, mix = ("head", "seq"), P("seq", "head")
    turned = P("head", "seq")
    out_specs = (
        row, row, P("seq"), mix, mix, P(None, both), P(both), turned, P("seq"), P(None, both), P(both), P(both, None), P(both),
        turned, P("seq"), mix, mix, turned,
    )
    return jax.shard_map(local, mesh=mesh, in_specs=in_specs, out_specs=out_specs, check_vma=False)
```

```python
import types

import jax
import jax.numpy as jnp
from jax import lax
from jax.experimental import pallas as pl
from jax.experimental.pallas import tpu as pltpu
from jax.sharding import PartitionSpec as P

F32 = jnp.float32
BF16 = jnp.bfloat16
T, D, C, F, N, R = 128, 1536, 768, 1024, 16, 96
GROUP = 16
EPS = 1e-5
LOG2E = 1.4426950408889634
HIGH = lax.Precision.HIGHEST
MESH = pl.DeviceIdType.MESH
SMALL = 48
SEMS = 112
W = 384


def dot(a, b, precision=None):
    return jnp.dot(a, b, precision=precision, preferred_element_type=F32)


def dot_nt(a, b, precision=None):
    return lax.dot_general(a, b, (((1,), (1,)), ((), ())), precision=precision, preferred_element_type=F32)


def tiles(total, width):
    return [slice(i, i + width) for i in range(0, total, width)]


def wide(v):
    return jnp.concatenate([v] * (W // 128), axis=1)


class Copy:
    def __init__(self, copy, sem, free):
        self.copy, self.sem, self.free = copy, sem, free

    def start(self):
        self.copy.start()

    def wait(self):
        self.copy.wait()
        self.free.append(self.sem)


def rcopy(src, dst, sems, device):
    send, recv, free = sems
    copy = pltpu.make_async_remote_copy(
        src_ref=src, dst_ref=dst, send_sem=send, recv_sem=recv, device_id=device, device_id_type=MESH
    )
    return Copy(copy, send, free)


def start(copies):
    for c in copies:
        c.start()
    return copies


def finish(copies):
    for c in copies:
        c.wait()


class Burst:
    def __init__(self, sems, src, dst, device):
        self.sems, self.all = sems, rcopy(src, dst, sems, device)

    def send(self, src, dst, device):
        rcopy(src, dst, self.sems, device).start()

    def wait(self):
        self.all.wait()


class Ring:
    def __init__(self, part, land, two, four, new, place, at):
        self.part, self.land, self.at, self.me = part, land, at, place
        self.right, self.left, self.far = lax.rem(place + 1, 4), lax.rem(place + 3, 4), lax.rem(place + 2, 4)
        self.first = Burst(new(), two, two, at(self.right))
        self.rest = Burst(new(), four, four, at(self.right))

    def begin(self):
        part, land, at, right, left, far = self.part, self.land, self.at, self.right, self.left, self.far
        self.first.send(part(far, 0), land(0, 0), at(right))
        self.first.send(part(far, 1), land(1, 1), at(left))
        self.rest.send(part(right, 1), land(2, 1), at(right))
        self.rest.send(part(left, 0), land(3, 0), at(left))

    def pass_on(self):
        self.first.wait()
        for h, d in enumerate((self.right, self.left)):
            own = self.part(d, h)
            own[...] = (own[...].astype(F32) + self.land(h, h)[...].astype(F32)).astype(own.dtype)
            self.rest.send(own, self.land(4 + h, h), self.at(d))

    def totals(self):
        self.rest.wait()
        for h, (a, b) in enumerate(((4, 3), (5, 2))):
            own = self.part(self.me, h)
            yield own, own[...].astype(F32) + (self.land(a, h)[...].astype(F32) + self.land(b, h)[...].astype(F32))


class Straight:
    def __init__(self, part, land, new, place, at):
        self.part, self.land, self.at, self.me = part, land, at, place
        self.burst = Burst(new(), land, land, at(lax.rem(place + 1, 4)))

    def begin(self):
        for k in (2, 1, 3):
            d = lax.rem(self.me + k, 4)
            self.burst.send(self.part(d), self.land.at[k - 1], self.at(d))

    def totals(self):
        self.burst.wait()
        own, land = self.part(self.me), self.land
        yield own, own[...].astype(F32) + ((land[0].astype(F32) + land[2].astype(F32)) + land[1].astype(F32))


class Unit:
    def __init__(self, grid, land_one, land_two, new, x, y, at, x_first, both_ways, split=0):
        along_x, along_y = (x, lambda d: at(d, y)), (y, lambda d: at(x, d))
        one, two = (along_x, along_y) if x_first else (along_y, along_x)

        def chunk(d, half=slice(0, 4)):
            return grid.at[half, d] if x_first else grid.at[d, half]

        def piece(d):
            return grid.at[d, x] if x_first else grid.at[y, d]

        if both_ways:
            self.one = Ring(
                lambda d, h: chunk(d, slice(2 * h, 2 * h + 2)), lambda i, h: land_one.at[i], land_one.at[0:2], land_one.at[2:6], new, *one
            )
        else:
            self.one = Straight(chunk, land_one, new, *one)
        if split:

            def side(ref, h):
                return ref.at[:, split:] if h else ref.at[:, 0:split]

            self.two = Ring(
                lambda d, h: side(piece(d), h), lambda i, h: side(land_two.at[i], h), land_two.at[0], land_two.at[0:2], new, *two
            )
        else:
            self.two = Straight(piece, land_two, new, *two)

    def a0(self):
        self.one.begin()

    def a1(self):
        self.one.pass_on()

    def add(self):
        for own, v in self.one.totals():
            own[...] = v.astype(own.dtype)

    def a2(self):
        self.add()
        self.two.begin()

    def b1(self):
        self.two.pass_on()

    def done(self):
        return [v for _, v in self.two.totals()]


def kernel(*refs):
    r = types.SimpleNamespace(**dict(zip([*INS, *OUTS, *SCRATCH], refs, strict=True)))
    s = lax.axis_index("seq")
    z = lax.axis_index("head")
    p = lax.rem(s, GROUP)
    base = s - p
    core = lax.rem(s, 2)
    x = lax.rem(s // 2, 4)
    y = s // 8

    def zdev(k):
        return (s, lax.rem(z + k, 4))

    def gdev(k):
        return (base + lax.rem(p + k, GROUP), z)

    def chip(cx, cy):
        return (cy * 8 + cx * 2 + core, z)

    sibling = (s + 1 - 2 * core, z)
    taken = []

    def new():
        taken.append(0)
        return r.sem.at[len(taken) - 1]

    free = []

    def sender():
        return free.pop() if free else new()

    def pair():
        return sender(), new(), free

    def local(src, dst):
        sem = sender()
        return Copy(pltpu.make_async_copy(src, dst, sem), sem, free)

    barrier = pltpu.get_barrier_semaphore()
    for k in range(1, 4):
        pl.semaphore_signal(barrier, 1, device_id=zdev(k), device_id_type=MESH)

    mates = sorted(((dy + min(dx, 4 - dx), dy, dx) for dy in range(2) for dx in range(4)), reverse=True)[:7]

    def mate(dy, dx):
        return base + lax.rem(y + dy, 2) * 8 + lax.rem(x + dx, 4) * 2 + core

    others = [(mate(dy, dx), z) for _, dy, dx in mates]
    for device in (*others, sibling, gdev(15 - 14 * core), (s + 8 * (3 - 2 * y), z)):
        pl.semaphore_signal(barrier, 1, device_id=device, device_id_type=MESH)

    def load(src, dst):
        c = local(src, dst)
        c.start()
        return c

    few = [load(v, o) for v, o in ((r.in_taps, r.s_taps), (r.in_cbias, r.s_cbias), (r.in_sbias, r.s_sbias), (r.in_skip, r.s_skip), (r.in_first, r.s_first), (r.in_second, r.s_second), (r.in_gains, r.s_gains), (r.in_rates, r.s_rates))]
    ld_tok = load(r.in_tok, r.tok)
    ld_in = load(r.in_w_in, r.w_in)

    finish(few)
    vec = r.vec
    vec[0:4, :] = r.s_taps[...]
    for i, v in enumerate((r.s_cbias, r.s_sbias, r.s_skip)):
        vec[4 + i : 5 + i, :] = v[...].reshape(1, C)
    g1 = r.s_first[...].reshape(1, D)
    g2 = r.s_second[...].reshape(1, D)
    nr = -jnp.exp(r.s_rates[...])
    r.nr[...] = nr
    nr2 = nr * LOG2E
    r.nr2[...] = nr2
    for j, c in enumerate(tiles(C, W)):
        r.nr2h[j] = nr2[:, c]

    ld_tok.wait()
    for rows in tiles(T, 32):
        v = r.tok[rows, :].astype(F32)
        rs = lax.rsqrt(jnp.mean(v * v, axis=-1, keepdims=True) + EPS)
        r.rinv[rows, :] = jnp.broadcast_to(rs, (32, 128))
        r.normed[rows, :] = (v * rs * g1).astype(BF16)
    ld_gate = load(r.in_w_gate, r.w_gate)
    ld_cot = load(r.in_cot, r.cot)
    ld_fd = load(r.in_w_fd, r.w_fd)
    ld_proj = load(r.in_w_proj, r.w_proj)
    r.w_step[...] = jnp.zeros((T, C), BF16)
    ld_step = load(r.in_w_step, r.w_step.at[0:R])
    ld_out = load(r.in_w_out, r.w_out)
    ld_fg = load(r.in_w_fg, r.w_fg)
    ld_fu = load(r.in_w_fu, r.w_fu)
    ld_in.wait()
    nrm = r.normed[...]
    for c in tiles(C, 256):
        r.ext[8 : 8 + T, c] = dot(nrm, r.w_in[:, c]).astype(BF16).astype(F32)
    pl.semaphore_wait(barrier, 3 + 7 + 3)
    halo = start([rcopy(r.ext.at[T : T + 8], r.halo, pair(), gdev(1))])
    ld_gate.wait()
    for c in tiles(C, 256):
        r.gate_in[:, c] = dot(nrm, r.w_gate[:, c])

    def turned(value, at, lhs):
        at[...] = value.T.reshape(16, 2, 48, T)
        lhs[:, :, 0:T] = at[:, core]
        return start([rcopy(at.at[:, 1 - core], lhs.at[:, :, T : 2 * T], pair(), sibling)])

    def both(b):
        return start([rcopy(b.at[0:T], b.at[T : 2 * T], pair(), sibling)])

    finish(halo)
    r.ext[0:8, :] = jnp.where(p == 0, 0.0, r.halo[...])
    for c in tiles(C, 128):
        tot = vec[4:5, c] + vec[0:1, c] * r.ext[5 : 5 + T, c]
        for k in range(1, 4):
            tot = tot + vec[k : k + 1, c] * r.ext[5 + k : 5 + k + T, c]
        r.conv_sum[:, c] = tot
        r.inner[:, c] = (tot * jax.nn.sigmoid(tot)).astype(BF16)

    def zgather(buf):
        burst = Burst(pair(), buf.at[0:3], buf.at[0:3], zdev(1))
        for k in (2, 1, 3):
            burst.send(buf.at[z], buf.at[z], zdev(k))
        return burst

    def zsum(buf):
        burst = zgather(buf)

        def result():
            burst.wait()
            return (buf[0].astype(F32) + buf[1].astype(F32)) + (buf[2].astype(F32) + buf[3].astype(F32))

        return result

    ld_proj.wait()
    r.pz[z] = dot(r.inner[...], r.w_proj[...]).astype(BF16)
    projected = zsum(r.pz)

    ld_cot.wait()
    ld_fd.wait()
    cot = r.cot[...]
    for c in tiles(F, 256):
        r.gact[:, :, c] = dot_nt(cot, r.w_fd[c, :]).reshape(4, 32, 256)

    tn_cot = turned(cot, r.at_cot, r.l_cot)
    tn_nrm = turned(nrm, r.at_nrm, r.l_nrm)

    proj = projected()
    r.proj[...] = proj
    lane = lax.broadcasted_iota(jnp.int32, (1, 128), 1)
    m1 = (lane < R).astype(F32)
    m3 = (lane >= R + N).astype(F32)
    m2 = 1.0 - m1 - m3

    def by_part(v):
        return (
            m1 * (jnp.sum(v * m1, -1, keepdims=True) / R)
            + m2 * (jnp.sum(v * m2, -1, keepdims=True) / N)
            + m3 * (jnp.sum(v * m3, -1, keepdims=True) / N)
        )

    rr = lax.rsqrt(by_part(proj * proj) + EPS)
    r.proj_r[...] = rr
    gains_in = r.s_gains[...].reshape(1, 128)
    pn = proj * rr * gains_in
    r.pn[...] = pn
    step_in = (pn * m1).astype(BF16)
    r.step_in[...] = step_in
    ld_step.wait()
    for c in tiles(C, 256):
        raw = dot(step_in, r.w_step[:, c]) + vec[5:6, c]
        r.raw[:, c] = raw
        st = jnp.maximum(raw, 0.0) + jnp.log1p(jnp.exp(-jnp.abs(raw)))
        r.step[:, c] = st
        r.u[:, c] = st * r.inner[:, c].astype(F32)
    rown = lax.broadcasted_iota(jnp.int32, (N, 128), 0)
    lanes = lax.broadcasted_iota(jnp.int32, (N, 128), 1)
    selb = (lanes == rown + R).astype(F32)
    selc = (lanes == rown + R + N).astype(F32)
    sel = selb + selc
    part_of = lax.broadcasted_iota(jnp.int32, (128, 256), 0) - jnp.where(lax.broadcasted_iota(jnp.int32, (128, 256), 1) < 128, R, R + N)
    to_lanes = ((part_of >= 0) & (part_of < N)).astype(BF16)

    for rows in tiles(T, 32):
        some = r.pn[rows, :]
        one = jnp.concatenate([jnp.broadcast_to(some[i : i + 1, :], (N, 128)) * sel for i in range(32)], axis=0)
        high = one.astype(BF16)
        low = (one - high.astype(F32)).astype(BF16)
        v = dot(high, to_lanes) + dot(low, to_lanes)
        r.Bb[rows] = v[:, 0:128].reshape(32, N, 128)
        r.Cb[rows] = v[:, 128:256].reshape(32, N, 128)

    top = lax.broadcasted_iota(jnp.int32, (N, W), 0) < 8

    def coded(ref, h, tot):
        high = tot.astype(BF16).astype(F32)
        ref[0:N, :] = h.astype(BF16)
        ref[N : 2 * N, :] = jnp.where(top, high, tot - high).astype(BF16)

    def state_of(ref):
        return ref[0:N, :].astype(F32)

    def steps_of(ref):
        v = ref[N : 2 * N, :].astype(F32)
        return v[0:1, :] + v[8:9, :]

    for half, c in enumerate(tiles(C, W)):
        a2 = r.nr2[:, c]

        def first(b, h):
            st = r.step[pl.ds(b * 16, 16), c]
            uu = r.u[pl.ds(b * 16, 16), c]
            for i in range(16):
                h = jnp.exp2(a2 * st[i : i + 1, :]) * h + uu[i : i + 1, :] * wide(r.Bb[b * 16 + i])
            return h

        h = lax.fori_loop(0, T // 16, first, jnp.zeros((N, W), F32))
        coded(r.pack.at[half], h, jnp.sum(r.step[:, c], axis=0, keepdims=True))

    nth = p // 2
    is_first = core == 0
    a2c = r.nr2h[core]

    def to_mates(src, land):
        burst = Burst(pair(), land.at[0:7], land.at[0:7], sibling)
        for device in others:
            burst.send(src, land.at[nth], device)
        land[nth] = src[...]
        return burst.wait

    def to_sibling(src, dst):
        return start([rcopy(src, dst, pair(), sibling)])

    finish(to_sibling(r.pack.at[1 - core], r.pack_sib))
    h_own, h_sib = state_of(r.pack.at[core]), state_of(r.pack_sib)
    t_own, t_sib = steps_of(r.pack.at[core]), steps_of(r.pack_sib)
    h0, h1 = jnp.where(is_first, h_own, h_sib), jnp.where(is_first, h_sib, h_own)
    t0, t1 = jnp.where(is_first, t_own, t_sib), jnp.where(is_first, t_sib, t_own)
    r.t01[0:1, :] = t0
    r.t01[8:9, :] = t1
    coded(r.chip_src, jnp.exp2(a2c * t1) * h0 + h1, t0 + t1)
    swapped = to_mates(r.chip_src, r.chips)
    ld_fu.wait()
    for c in tiles(F, 256):
        r.w_fd[c, :] = r.w_fu[:, c].T
    finish(tn_cot)
    finish(tn_nrm)
    swapped()
    state = jnp.zeros((N, W), F32)
    for j in range(7):
        at = r.chips.at[j]
        state = jnp.where(j < nth, jnp.exp2(a2c * steps_of(at)) * state + state_of(at), state)
    later = jnp.exp2(a2c * t0) * state + h0
    r.st_src[...] = jnp.where(is_first, later, state)
    entering = to_sibling(r.st_src, r.st_sib)
    state = jnp.where(is_first, state, later)
    finish(entering)
    for half, c in enumerate(tiles(C, W)):
        r.H[0, :, c] = jnp.where(core == half, state, r.st_sib[...])

    eights = (lax.broadcasted_iota(jnp.int32, (16, 128), 1) // 8 == lax.broadcasted_iota(jnp.int32, (16, 128), 0)).astype(BF16)

    def folded(v):
        return v[0:8, :] + v[8:16, :]

    def finished(part, out):
        for j in range(8):
            out[16 * j : 16 * j + 16, :] = dot(eights, part[128 * j : 128 * j + 128, :])

    for c in tiles(C, W):
        a2 = r.nr2[:, c]

        def second(b, h):
            st = r.step[pl.ds(b * 16, 16), c]
            uu = r.u[pl.ds(b * 16, 16), c]
            rows = []
            for i in range(16):
                h = jnp.exp2(a2 * st[i : i + 1, :]) * h + uu[i : i + 1, :] * wide(r.Bb[b * 16 + i])
                r.H[b * 16 + i + 1, :, c] = h
                rows.append(folded(h * wide(r.Cb[b * 16 + i])))
            r.part_one[pl.ds(pl.multiple_of(b * 128, 128), 128), c] = jnp.concatenate(rows, axis=0).astype(BF16)
            return h

        lax.fori_loop(0, T // 16, second, r.H[0, :, c])

    finished(r.part_one, r.scan_out)
    for c in tiles(C, 128):
        so = r.scan_out[:, c] + vec[6:7, c] * r.inner[:, c].astype(F32)
        r.scan_out[:, c] = so
        gi = r.gate_in[:, c]
        r.b_out[0:T, c] = (so * (gi * jax.nn.sigmoid(gi))).astype(BF16)
    by_out = both(r.b_out)

    def zscatter(src, dst):
        return Burst(pair(), src.at[0:3], dst, zdev(1))

    def zsend(burst, src, dst, j):
        c = slice(512 * j, 512 * j + 512)
        for k in (2, 1, 3):
            burst.send(src.at[lax.rem(z + k, 4), :, c], dst.at[k - 1, :, c], zdev(k))

    def zsummed(src, dst, burst):
        burst.wait()
        return (src[z].astype(F32) + dst[0].astype(F32)) + (dst[1].astype(F32) + dst[2].astype(F32))

    def fours(v):
        return v.astype(BF16).reshape(4, 32, v.shape[-1])

    ld_out.wait()
    own = pl.ds(pl.multiple_of(z * 32, 32), 32)
    halves = tiles(32, 16)
    mixed = r.b_out[0:T, :].reshape(4, 32, C)
    sent = []
    for hs in halves:
        some = mixed[:, hs].reshape(64, C)
        for c in tiles(D, 512):
            r.rs1_src[:, hs, c] = dot(some, r.w_out[:, c]).astype(BF16).reshape(4, 16, 512)
        burst = Burst(pair(), r.rs1_src.at[0:3, hs], r.rs1_dst.at[:, hs], zdev(1))
        for k in (2, 1, 3):
            burst.send(r.rs1_src.at[lax.rem(z + k, 4), hs], r.rs1_dst.at[k - 1, hs], zdev(k))
        sent.append(burst)
    gathered = []
    for hs, burst in zip(halves, sent):
        burst.wait()
        terms = [r.rs1_src[z, hs], *(r.rs1_dst[k, hs] for k in range(3))]
        rows = pl.ds(pl.multiple_of(z * 32 + hs.start, 16), 16)
        middle = r.tok[rows, :].astype(F32) + sum((v.astype(F32) for v in terms[1:]), terms[0].astype(F32))
        r.middle[hs, :] = middle
        r2 = lax.rsqrt(jnp.mean(middle * middle, axis=-1, keepdims=True) + EPS)
        r.out_y[z, hs] = (middle * r2 * g2).astype(BF16)
        burst = Burst(pair(), r.out_y.at[0:3, hs], r.out_y.at[0:3, hs], zdev(1))
        for k in (2, 1, 3):
            burst.send(r.out_y.at[z, hs], r.out_y.at[z, hs], zdev(k))
        gathered.append(burst)

    def unit(grid, land_one, land_two, x_first, both_ways=True, split=0):
        return Unit(grid, land_one, land_two, pair, x, y, chip, x_first, both_ways, split)

    def product_of(grid, lhs, b, lo, n):
        left = lhs[...].reshape(D // 2, 2 * T)
        for c in tiles(n, 256 if n % 256 == 0 else 128):
            cols = slice(lo + c.start, lo + c.stop)
            grid[:, :, :, c] = dot(left, b[:, cols]).astype(BF16).reshape(4, 4, 48, c.stop - c.start)

    def store_out(u, lo, n):
        at = lo
        for v in u.done():
            r.out_big[:, at : at + v.shape[1]] = v
            at += v.shape[1]

    u_fd = [unit(r.gr_fd.at[i], r.x_fd.at[i], r.y_fd.at[i], i == 0, split=256) for i in range(2)]
    u_fg = [unit(r.gr_fg.at[i], r.x_fg.at[i], r.y_fg.at[i], i == 0, split=256) for i in range(2)]
    u_fu = [unit(r.gr_fu.at[i], r.x_fu.at[i], r.y_fu.at[i], i == 0) for i in range(2)]

    def halves_of(units, grids, lhs, b):
        for i in range(2):
            product_of(grids.at[i], lhs, b, 512 * i, 512)
            units[i].a0()

    u_out = unit(r.gr_out, r.x_out, r.y_out, True)
    u_gate = unit(r.gr_gate, r.x_gate, r.y_gate, False)
    u_in = [unit(r.gr_in.at[i], r.x_in.at[i], r.y_in.at[i], i == 0, False) for i in range(2)]
    u_small = unit(r.gr_small, r.x_small, r.y_small, True, False)
    u_first = unit(r.gr_first, r.x_first, r.y_first, False, False)

    ld_fg.wait()
    for hs, burst in zip(halves, gathered):
        burst.wait()
        some = r.out_y[:, hs].reshape(64, D)
        for c in tiles(F, 256):
            g = dot(some, r.w_fg[:, c])
            u = dot(some, r.w_fu[:, c])
            ga = r.gact[:, hs, c].reshape(64, 256)
            sg = jax.nn.sigmoid(g)
            sl = g * sg
            for b, v in ((r.b_act, sl * u), (r.b_gg, ga * u * (sg * (1.0 + g * (1.0 - sg)))), (r.b_gu, ga * sl)):
                v = v.astype(BF16)
                for q in range(4):
                    b[32 * q + hs.start : 32 * q + hs.stop, c] = v[16 * q : 16 * q + 16, :]
    n2 = r.out_y[...].reshape(T, D)
    by_act = both(r.b_act)
    gg = r.b_gg[0:T, :]
    gu = r.b_gu[0:T, :]
    sent = zscatter(r.rs2_src, r.rs2_dst)
    for j, c in enumerate(tiles(D, 512)):
        r.rs2_src[:, :, c] = fours(dot_nt(gg, r.w_fg[c, :]) + dot(gu, r.w_fd[:, c]))
        zsend(sent, r.rs2_src, r.rs2_dst, j)
    ld_fd = load(r.in_w_fd, r.w_fd)
    by_gg = both(r.b_gg)
    by_gu = both(r.b_gu)
    tn_n2 = turned(n2, r.at_cot, r.l_n2)

    finish(by_act)
    halves_of(u_fd, r.gr_fd, r.l_cot, r.b_act)
    finish(tn_n2)
    finish(by_gg)
    halves_of(u_fg, r.gr_fg, r.l_n2, r.b_gg)
    finish(by_gu)
    halves_of(u_fu, r.gr_fu, r.l_n2, r.b_gu)

    gy = zsummed(r.rs2_src, r.rs2_dst, sent)
    v = r.middle[...]
    r2 = lax.rsqrt(jnp.mean(v * v, axis=-1, keepdims=True) + EPS)
    vr = v * r2
    gn = gy * g2
    gm = r.cot[own, :].astype(F32) + r2 * (gn - vr * jnp.mean(vr * gn, axis=-1, keepdims=True))
    r.gmid[...] = gm
    r.out_gt[z] = gm.astype(BF16)
    got = zgather(r.out_gt)
    r.dn[1:2, :] = jnp.sum(vr * gy, axis=0, keepdims=True)
    act = r.b_act[0:T, :]
    ld_fd.wait()
    sent3 = zscatter(r.rs1_src, r.rs3_dst)
    for j, c in enumerate(tiles(D, 512)):
        r.rs1_src[:, :, c] = fours(dot(act, r.w_fd[:, c]))
        zsend(sent3, r.rs1_src, r.rs3_dst, j)

    def owner(shape):
        i = lax.broadcasted_iota(jnp.int32, shape, 0)
        return 2 * (i & 15) + (i >> 4)

    def rows_of(v, width, hot):
        k = lax.broadcasted_iota(jnp.int32, (32, v.shape[1]), 1) - width * owner((32, v.shape[1]))
        one = jnp.where((k >= 0) & (k < width), v, 0.0)
        high = one.astype(BF16)
        return dot(high, hot) + dot((one - high.astype(F32)).astype(BF16), hot)

    kk = lax.broadcasted_iota(jnp.int32, (D, 128), 0)
    hot = lax.broadcasted_iota(jnp.int32, (D, 128), 1) == kk - 48 * ((kk * 683) >> 15)
    r.at_cot[...] = hot.astype(BF16).reshape(16, 2, 48, T)
    got.wait()
    for u in u_fd:
        u.a1()

    gmo = r.out_gt[...].reshape(T, D)
    for c in tiles(C, 256):
        gmx = dot_nt(gmo, r.w_out[c, :])
        gi = r.gate_in[:, c]
        sg = jax.nn.sigmoid(gi)
        r.gso[:, c] = gmx * (gi * sg)
        r.b_gate[0:T, c] = (gmx * r.scan_out[:, c] * (sg * (1.0 + gi * (1.0 - sg)))).astype(BF16)
    by_gate = both(r.b_gate)
    tn_gmo = turned(gmo, r.at_nrm, r.l_gmo)

    def rev_first(c):
        a2 = r.nr2[:, c]

        def body(k, cr):
            b = T // 16 - 1 - k
            st = r.step[pl.ds(b * 16, 16), c]
            gs = r.gso[pl.ds(b * 16, 16), c]
            for i in range(15, -1, -1):
                cr = jnp.exp2(a2 * st[i : i + 1, :]) * (gs[i : i + 1, :] * wide(r.Cb[b * 16 + i]) + cr)
            return cr

        cr = lax.fori_loop(0, T // 16, body, jnp.zeros((N, W), F32))
        r.pack_b[0 if c.start == 0 else 1] = cr.astype(BF16)

    for c in tiles(C, W):
        rev_first(c)
    finish(to_sibling(r.pack_b.at[1 - core], r.pack_b_sib))
    c_own, c_sib = r.pack_b[core].astype(F32), r.pack_b_sib[...].astype(F32)
    c0, c1 = jnp.where(is_first, c_own, c_sib), jnp.where(is_first, c_sib, c_own)
    t0, t1 = r.t01[0:1, :], r.t01[8:9, :]
    r.chip_b_src[...] = (c0 + jnp.exp2(a2c * t0) * c1).astype(BF16)
    swapped = to_mates(r.chip_b_src, r.chips_b)
    for u in u_fg:
        u.a1()
    hot = r.at_cot[...].reshape(D, 128)
    finish(by_gate)
    product_of(r.gr_gate, r.l_nrm, r.b_gate, 0, C)
    u_gate.a0()
    finish(tn_gmo)
    finish(by_out)
    product_of(r.gr_out, r.l_gmo, r.b_out, 0, C)
    u_out.a0()

    def read_rows(b, carry):
        gs = r.gso[pl.ds(b * 8, 8), :]
        for i in range(8):
            pr = gs[i : i + 1, :] * r.H[b * 8 + i + 1]
            r.PR[b * 8 + i] = sum((pr[:, k] for k in tiles(C, 128)[1:]), pr[:, 0:128])
        return carry

    lax.fori_loop(0, T // 8, read_rows, 0)
    for c in tiles(C, 256):
        r.w_out[c, :] = r.w_gate[:, c].T
    swapped()
    for u in u_fu:
        u.a1()
    state = jnp.zeros((N, W), F32)
    for j in range(7, 0, -1):
        state = jnp.where(j > nth, r.chips_b[j].astype(F32) + jnp.exp2(a2c * steps_of(r.chips.at[j])) * state, state)
    later = c1 + jnp.exp2(a2c * t1) * state
    r.st_src[...] = jnp.where(is_first, state, later)
    entering = to_sibling(r.st_src, r.st_sib)
    state = jnp.where(is_first, later, state)
    r.out_y[z] = (r.middle[...] + zsummed(r.rs1_src, r.rs3_dst, sent3)).astype(BF16)
    sent_out = zgather(r.out_y)
    finish(entering)
    for half, c in enumerate(tiles(C, W)):
        r.gstate[:, c] = jnp.where(core == half, state, r.st_sib[...])

    def rev_second(c):
        a2 = r.nr2[:, c]
        a = r.nr[:, c]

        def body(k, state):
            cr, gl = state
            b = T // 16 - 1 - k
            st = r.step[pl.ds(b * 16, 16), c]
            gs = r.gso[pl.ds(b * 16, 16), c]
            uu = r.u[pl.ds(b * 16, 16), c]
            s1, s2 = [None] * 16, [None] * 16
            for i in range(15, -1, -1):
                t = b * 16 + i
                si, gi, ui = st[i : i + 1, :], gs[i : i + 1, :], uu[i : i + 1, :]
                g = gi * wide(r.Cb[t]) + cr
                s1[i] = folded(g * wide(r.Bb[t]))
                pe = g * ui
                pe = (pe[:, 0:128] + pe[:, 128:256]) + pe[:, 256:384]
                if c.start:
                    pe = pe + r.PE[t]
                r.PE[t] = pe
                cr = jnp.exp2(a2 * si) * g
                q = cr * r.H[t, :, c]
                s2[i] = folded(q * a)
                gl = gl + q * si
            rows = pl.ds(pl.multiple_of(b * 128, 128), 128)
            r.part_one[rows, c] = jnp.concatenate(s1, axis=0).astype(BF16)
            r.part_two[rows, c] = jnp.concatenate(s2, axis=0).astype(BF16)
            return cr, gl

        _, gl = lax.fori_loop(0, T // 16, body, (r.gstate[:, c], jnp.zeros((N, W), F32)))
        r.rows[R : R + N, c] = gl * a

    for c in tiles(C, W):
        rev_second(c)
    finished(r.part_one, r.gate_in)
    finished(r.part_two, r.scan_out)

    ones = jnp.ones((128, 128), BF16)

    for tok in tiles(T, 32):
        pe = dot(r.PE[tok].reshape(32 * N, 128).astype(BF16), ones).reshape(32, N, 128)
        pr = dot(r.PR[tok].reshape(32 * N, 128).astype(BF16), ones).reshape(32, N, 128)
        r.er[tok, :] = jnp.sum(pe * selb[None] + pr * selc[None], axis=1)
    for c in tiles(C, 256):
        inner = r.inner[:, c].astype(F32)
        s1 = r.gate_in[:, c]
        raw_g = (r.scan_out[:, c] + s1 * inner) * jax.nn.sigmoid(r.raw[:, c])
        r.gsr[:, c] = raw_g.astype(BF16)
        r.rows[R + N + 5 : R + N + 6, c] = jnp.sum(raw_g, axis=0, keepdims=True)
        gso = r.gso[:, c]
        r.rows[R + N + 6 : R + N + 7, c] = jnp.sum(gso * inner, axis=0, keepdims=True)
        r.gate_in[:, c] = gso * vec[6:7, c] + s1 * r.step[:, c]
    r.pz[z] = (dot_nt(r.gsr[...], r.w_step[...]) + r.er[...]).astype(BF16)
    summed = zsum(r.pz)
    for c in tiles(C, 256):
        r.w_fd[c, :] = r.w_in[:, c].T
    u_out.a1()
    u_gate.a1()
    gy = summed()
    vr = r.proj[...] * r.proj_r[...]
    gn = gy * gains_in
    gpj = (r.proj_r[...] * (gn - vr * by_part(vr * gn))).astype(BF16)
    r.dg[...] = jnp.broadcast_to(jnp.sum(vr * gy, axis=0, keepdims=True), (8, 128))
    for c in tiles(C, 256):
        gi = r.gate_in[:, c] + dot_nt(gpj, r.w_proj[c, :])
        cs = r.conv_sum[:, c]
        sg = jax.nn.sigmoid(cs)
        r.gcs[0:T, c] = gi * (sg * (1.0 + cs * (1.0 - sg)))
    halo = start([rcopy(r.gcs.at[0:8], r.halo2, pair(), gdev(15))])
    for c in tiles(C, 128):
        gc = r.gcs[0:T, c]
        for k in range(4):
            r.rows[R + N + k : R + N + k + 1, c] = jnp.sum(gc * r.ext[5 + k : 5 + k + T, c], axis=0, keepdims=True)
        r.rows[R + N + 4 : R + N + 5, c] = jnp.sum(gc, axis=0, keepdims=True)
    r.rows[0:R, :] = jnp.zeros((R, C), F32)
    r.rows[R + N + 7 : T, :] = jnp.zeros((T - R - N - 7, C), F32)
    chan = (dot(r.gsr[...].T, r.step_in[...]) + r.rows[...].T).reshape(16, 2, 24, 128)
    ll = lax.broadcasted_iota(jnp.int32, (128, 128), 0)
    order = (lax.broadcasted_iota(jnp.int32, (128, 128), 1) == 4 * (2 * (ll & 15) + ((ll >> 4) & 1)) + (ll >> 5)).astype(BF16)
    pt = dot(dot_nt(order, gpj).astype(BF16), r.inner[...])
    for h in range(2):
        r.small[:, h, 24:48, :] = chan[:, h]
        for i in range(4):
            for j in range(6):
                r.small[:, h, i * 6 + j, :] = pt[32 * i + 16 * h : 32 * i + 16 * h + 16, 128 * j : 128 * j + 128]
    by_small = start([rcopy(r.small.at[:, 1 - core], r.small_recv, pair(), sibling)])
    for u in (*u_fd, *u_fg, *u_fu,):
        u.a2()
    finish(halo)
    r.gcs[T : T + 8, :] = jnp.where(p == GROUP - 1, 0.0, r.halo2[...])
    for c in tiles(C, 128):
        tot = vec[3:4, c] * r.gcs[0:T, c]
        for k in range(3):
            tot = tot + vec[k : k + 1, c] * r.gcs[3 - k : 3 - k + T, c]
        r.b_in[0:T, c] = tot.astype(BF16)
    by_in = both(r.b_in)
    finish(by_small)
    r.gr_small[...] = (r.small[:, core] + r.small_recv[...]).astype(BF16).reshape(4, 4, SMALL, 128)
    u_small.a0()
    gip = r.b_in[0:T, :]
    ggi = r.b_gate[0:T, :]
    sent = zscatter(r.rs2_src, r.rs1_dst)
    for j, c in enumerate(tiles(D, 512)):
        gnp = dot(gip, r.w_fd[0:C, c]) + dot(ggi, r.w_out[:, c])
        r.rs2_src[:, :, c] = fours(gnp)
        if j < 2:
            zsend(sent, r.rs2_src, r.rs1_dst, j)
        r.dn[0:1, c] = jnp.sum(r.tok[:, c].astype(F32) * (r.rinv[:, 0:1] * gnp), axis=0, keepdims=True)
    k4 = lax.broadcasted_iota(jnp.int32, (128, 128), 0)
    hot4 = (lax.broadcasted_iota(jnp.int32, (128, 128), 1) == (k4 & 3)).astype(BF16)
    r.gr_first[...] = jnp.zeros((4, 4, 8, 128), F32)
    for i, v in enumerate((rows_of(r.dn[0:1, :], 48, hot), rows_of(r.dn[1:2, :], 48, hot), rows_of(r.dg[0:1, :] * 0.25, 4, hot4))):
        for h in range(2):
            r.gr_first[:, :, 2 * i + h, :] = v[16 * h : 16 * h + 16, :].reshape(4, 4, 128)
    u_first.a0()
    zsend(sent, r.rs2_src, r.rs1_dst, 2)
    finish(by_in)
    for i in range(2):
        product_of(r.gr_in.at[i], r.l_nrm, r.b_in, 384 * i, 384)
        u_in[i].a0()
    for u in (*u_fd, *u_fg):
        u.b1()
    u_small.a2()
    u_first.add()
    r.nz2[z] = r.gr_first[y]
    first = zsum(r.nz2)
    gn1 = zsummed(r.rs2_src, r.rs1_dst, sent)
    v = r.tok[own, :].astype(F32)
    rs = lax.rsqrt(jnp.mean(v * v, axis=-1, keepdims=True) + EPS)
    vr = v * rs
    gn = gn1 * g1
    r.out_gt[z] = (r.gmid[...] + rs * (gn - vr * jnp.mean(vr * gn, axis=-1, keepdims=True))).astype(BF16)
    sent_tok = zgather(r.out_gt)
    u_out.a2()
    u_gate.a2()
    r.gr_first[y] = first()
    u_first.two.begin()
    for u in u_in:
        u.a2()
    for i in range(2):
        store_out(u_fd[i], 512 * i, 512)
        store_out(u_fg[i], F + 512 * i, 512)
        store_out(u_fu[i], 2 * F + 512 * i, 512)
    r.out_small[0:SMALL, :] = u_small.done()[0]
    store_out(u_out, 3 * F, C)
    store_out(u_gate, 3 * F + C, C)
    r.first[...] = u_first.done()[0]
    by_first = start([rcopy(r.first, r.first_recv, pair(), sibling)])
    for i in range(2):
        store_out(u_in[i], 3 * F + 2 * C + 384 * i, 384)
    finish(by_first)
    r.first[...] = r.first[...] + r.first_recv[...]
    for i in range(3):
        r.out_small[SMALL + i : SMALL + i + 1, :] = r.first[pl.ds(2 * i + core, 1), :]
    sent_out.wait()
    sent_tok.wait()
    assert len(taken) == SEMS


def V(*shape, dtype=BF16):
    return pltpu.VMEM(shape, dtype)


def V32(*shape):
    return pltpu.VMEM(shape, F32)


def S(*shape):
    return pltpu.SemaphoreType.DMA(shape)


BIG = 3 * F + 3 * C
HBM, VMEM = pl.ANY, pltpu.VMEM
INS = dict(
    in_tok=HBM, in_cot=HBM, in_w_in=HBM, in_w_gate=HBM, in_w_proj=HBM, in_w_step=HBM, in_w_out=HBM, in_w_fg=HBM, in_w_fu=HBM,
    in_w_fd=HBM, in_taps=HBM, in_cbias=HBM, in_sbias=HBM, in_skip=HBM, in_first=HBM, in_second=HBM, in_gains=HBM, in_rates=HBM,
)
OUTS = dict(out_y=((4, 32, D), BF16), out_gt=((4, 32, D), BF16), out_big=((48, BIG), F32), out_small=((56, 128), F32))
SCRATCH = dict(
    s_taps=V32(4, C), s_cbias=V32(C), s_sbias=V32(C), s_skip=V32(C), s_first=V32(D), s_second=V32(D), s_gains=V32(128), s_rates=V32(N, C),
    sem=S(SEMS),
    tok=V(T, D), cot=V(T, D), w_in=V(D, C), w_gate=V(D, C), w_proj=V(C, 128), w_step=V(T, C), w_out=V(C, D), w_fg=V(D, F), w_fu=V(D, F),
    w_fd=V(F, D),
    vec=V32(8, C), nr=V32(N, C), nr2=V32(N, C), rinv=V32(T, 128), normed=V(T, D), ext=V32(T + 8, C), halo=V32(8, C),
    gate_in=V32(T, C), conv_sum=V32(T, C), inner=V(T, C),
    pz=V(4, T, 128), proj=V32(T, 128), proj_r=V32(T, 128), pn=V32(T, 128), step_in=V(T, 128),
    raw=V32(T, C), step=V32(T, C), u=V32(T, C), Bb=V32(T, N, 128), Cb=V32(T, N, 128),
    nr2h=V32(2, N, W), pack=V(2, 2 * N, W), pack_sib=V(2 * N, W), chip_src=V(2 * N, W), chips=V(8, 2 * N, W), t01=V32(16, W),
    st_src=V32(N, W), st_sib=V32(N, W),
    pack_b=V(2, N, W), pack_b_sib=V(N, W), chip_b_src=V(N, W), chips_b=V(8, N, W),
    H=V32(T + 1, N, C), scan_out=V32(T, C),
    rs1_src=V(4, 32, D), rs1_dst=V(3, 32, D), rs2_src=V(4, 32, D), rs2_dst=V(3, 32, D),
    rs3_dst=V(3, 32, D),
    middle=V32(32, D), gmid=V32(32, D),

    gact=V32(4, 32, F), at_cot=V(16, 2, 48, T), at_nrm=V(16, 2, 48, T),
    l_cot=V(16, 48, 2 * T), l_nrm=V(16, 48, 2 * T), l_n2=V(16, 48, 2 * T), l_gmo=V(16, 48, 2 * T),
    b_out=V(2 * T, C), b_act=V(2 * T, F), b_gg=V(2 * T, F), b_gu=V(2 * T, F), b_gate=V(2 * T, C), b_in=V(2 * T, C),
    gr_fd=V(2, 4, 4, 48, 512), x_fd=V(2, 6, 2, 48, 512), y_fd=V(2, 6, 48, 512), gr_fg=V(2, 4, 4, 48, 512), x_fg=V(2, 6, 2, 48, 512), y_fg=V(2, 6, 48, 512),
    gr_fu=V(2, 4, 4, 48, 512), x_fu=V(2, 6, 2, 48, 512), y_fu=V(2, 3, 48, 512),
    gr_out=V(4, 4, 48, C), x_out=V(6, 2, 48, C), y_out=V(3, 48, C), gr_gate=V(4, 4, 48, C), x_gate=V(6, 2, 48, C), y_gate=V(3, 48, C),
    gr_in=V(2, 4, 4, 48, 384), x_in=V(2, 3, 4, 48, 384), y_in=V(2, 3, 48, 384),
    gso=V32(T, C), gstate=V32(N, C), PR=V32(T, N, 128), part_one=V(8 * T, C), part_two=V(8 * T, C), PE=V32(T, N, 128), rows=V32(T, C), er=V32(T, 128),
    gsr=V(T, C), gcs=V32(T + 8, C), halo2=V32(8, C), dn=V32(8, D), dg=V32(8, 128),
    nz2=V32(4, 4, 8, 128), first=V32(8, 128), first_recv=V32(8, 128), gr_first=V32(4, 4, 8, 128), x_first=V32(3, 4, 8, 128), y_first=V32(3, 8, 128), small=V32(16, 2, SMALL, 128), small_recv=V32(16, SMALL, 128),
    gr_small=V(4, 4, SMALL, 128), x_small=V(3, 4, SMALL, 128), y_small=V(3, SMALL, 128),
)


def local(
    tokens, cotangent, norm_first, in_inner, in_gate, conv_weight, conv_bias, projector, projector_gains, step_weight, step_bias,
    log_rates, skip_gain, out_weight, norm_second, gate_weight, up_weight, down_weight,
):
    y, gt, big, small = pl.pallas_call(
        kernel,
        out_shape=[pltpu.VMEM(shape, dtype) for shape, dtype in OUTS.values()],
        in_specs=[pl.BlockSpec(memory_space=m) for m in INS.values()],
        out_specs=[pl.BlockSpec(memory_space=VMEM) for _ in OUTS],
        scratch_shapes=list(SCRATCH.values()),
        compiler_params=pltpu.CompilerParams(collective_id=0, has_side_effects=True, vmem_limit_bytes=int(62.1 * 2**20)),
    )(
        tokens, cotangent, in_inner, in_gate, projector, step_weight, out_weight, gate_weight, up_weight, down_weight,
        conv_weight, conv_bias, step_bias, skip_gain, norm_first, norm_second, projector_gains, log_rates.T,
    )
    widths = (F, F, F, C, C, C)
    shapes = [(T, D)] * 2 + [(48, w) for w in widths] + [(4, C), (24, R), (N, 24), (4, 24)] + [(1, 24)] * 3 + [(1, 48)] * 2 + [(1, 4)]
    res = pl.pallas_call(
        hand_out,
        out_shape=[jax.ShapeDtypeStruct(sh, F32 if i > 1 else BF16) for i, sh in enumerate(shapes)],
        in_specs=[pl.BlockSpec(memory_space=VMEM)] * 4,
        out_specs=[pl.BlockSpec(memory_space=HBM if i < 8 else VMEM) for i in range(len(shapes))],
        scratch_shapes=[S(8)],
        compiler_params=pltpu.CompilerParams(vmem_limit_bytes=2 * 2**20),
    )(*(pltpu.with_memory_space_constraint(v, VMEM) for v in (y.reshape(T, D), gt.reshape(T, D), big, small)))
    y, gt, fd, fg, fu, out, gate, inn, proj, step_w, rates, taps, cbias, sbias, skip, first, second, gains = res
    return (
        y, gt, first[0], inn, gate, taps, cbias[0], proj.T, gains[0], step_w.T, sbias[0], rates.T, skip[0], out.T, second[0], fg, fu, fd.T,
    )


def hand_out(y, gt, big, small, *refs):
    outs, sem = refs[:-1], refs[-1]
    parts, at = [], 0
    for o in outs[2:8]:
        parts.append(big.at[:, at : at + o.shape[1]])
        at += o.shape[1]
    parts = [pltpu.make_async_copy(v, o, sem.at[i]) for i, (v, o) in enumerate(zip([*parts, y, gt], [*outs[2:8], *outs[:2]]))]
    start(parts)
    proj, step_w, rates, taps, cbias, sbias, skip, first, second, gains = outs[8:]
    for i in range(4):
        for j in range(6):
            proj[i : i + 1, 128 * j : 128 * j + 128] = small[i * 6 + j : i * 6 + j + 1, :]
    step_w[...] = small[24:48, 0:R]
    turned = jnp.concatenate([small[24:48, :], jnp.zeros((104, 128), F32)], axis=0).T
    rates[...] = turned[R : R + N, 0:24]
    taps[...] = turned[R + N : R + N + 4, 0:24]
    for i, o in enumerate((cbias, sbias, skip)):
        o[...] = turned[R + N + 4 + i : R + N + 5 + i, 0:24]
    first[...] = small[48:49, 0:48]
    second[...] = small[49:50, 0:48]
    gains[...] = small[50:51, 0:4]
    finish(parts)


def solution(mesh):
    row, col = P("seq", None), P(None, "head")
    flat, deep = P("head"), P("head", None)
    in_specs = (row, row, P(), col, col, col, flat, deep, P(), col, flat, deep, flat, deep, P(), col, col, deep)
    both, mix = ("head", "seq"), P("seq", "head")
    turned = P("head", "seq")
    out_specs = (
        row, row, P("seq"), mix, mix, P(None, both), P(both), turned, P("seq"), P(None, both), P(both), P(both, None), P(both),
        turned, P("seq"), mix, mix, turned,
    )
    return jax.shard_map(local, mesh=mesh, in_specs=in_specs, out_specs=out_specs, check_vma=False)
```
